32 devices in a mesh: dp: 16 (over z, y, x), blk: 2 (over core).
Axes of the slice: x: 2, y: 2, z: 4, core: 2. Of those that a mesh axis runs over, the one named last changes fastest.
Arguments:
- gene_ids: int32 [16, 1024], P('dp', 'blk'), may hold values from 0 to 2303, as said below
- values: float32 [16, 1024], P('dp', 'blk'), may hold values from -6 to 6
- knowledge: bfloat16 [16, 1024, 768], P('dp', 'blk'), may hold values from -6 to 6
- lengths: int32 [16], P('dp'), may hold values from 513 to 1024, as said below
- groups: int32 [16], P('dp'), may hold values from 0 to 63
- gene_table: bfloat16 [2304, 768], replicated, may hold values from -6 to 6
- group_table: bfloat16 [64, 768], replicated, may hold values from -4 to 4
- w_know: bfloat16 [768, 768], replicated, may hold values from -0.21875 to 0.21875
- w_value: float32 [768], replicated, may hold values from -5 to 5
- norm1_gain: float32 [768], replicated, may hold values from 0.5 to 1.5
- norm1_bias: float32 [768], replicated, may hold values from -2 to 2
- w_qkv: bfloat16 [768, 2304], replicated, may hold values from -0.21875 to 0.21875
- bias_q: float32 [768], replicated, may hold values from -2 to 2
- bias_v: float32 [768], replicated, may hold values from -2 to 2
- w_out: bfloat16 [768, 768], replicated, may hold values from -1.75 to 1.75
- bias_out: float32 [768], replicated, may hold values from -2 to 2
- norm2_gain: float32 [768], replicated, may hold values from 0.5 to 1.5
- norm2_bias: float32 [768], replicated, may hold values from -2 to 2
- w_up: bfloat16 [768, 3072], replicated, may hold values from -0.21875 to 0.21875
- bias_up: float32 [3072], replicated, may hold values from -2 to 2
- w_down: bfloat16 [3072, 768], replicated, may hold values from -0.109375 to 0.109375
- bias_down: float32 [768], replicated, may hold values from -2 to 2
- cotangent: bfloat16 [16, 1024, 768], P('dp', 'blk'), may hold values from -6 to 6
Outputs:
- block_output: bfloat16 [16, 1024, 768], P('dp', 'blk')
- gene_table_grad: float32 [2304, 768], P(('dp', 'blk'))
- group_table_grad: float32 [64, 768], P(None, 'dp')
- w_know_grad: float32 [768, 768], P('dp')
- w_value_grad: float32 [768], P('dp')
- norm1_gain_grad: float32 [768], P('dp')
- norm1_bias_grad: float32 [768], P('dp')
- w_qkv_grad: float32 [768, 2304], P('dp')
- bias_q_grad: float32 [768], P('dp')
- bias_v_grad: float32 [768], P('dp')
- w_out_grad: float32 [768, 768], P('dp')
- bias_out_grad: float32 [768], P('dp')
- norm2_gain_grad: float32 [768], P('dp')
- norm2_bias_grad: float32 [768], P('dp')
- w_up_grad: float32 [768, 3072], P('dp')
- bias_up_grad: float32 [3072], P('dp')
- w_down_grad: float32 [3072, 768], P('dp')
- bias_down_grad: float32 [768], P('dp')
The draws below stay inside these ranges and needn't reach their ends.
Inputs may be any that keep to these rules, and one draw needn't show every extreme that they name: lengths[c] is the number of live genes of cell c, which come first; some cell is full. `gene_ids`: take each run of 512 positions of a cell (one device's) and vocabulary blocks of 72 consecutive genes (block = gene // 72): at most 32 positions of a run name genes of one block, and in every run some block is named by exactly 32 positions.
All inputs are finite; a program needn't handle non-finite values.
Results may differ from the reference program's by a relative error of at most 0.015.
Values may be sent and summed in bfloat16 or wider, within the bound.
No kernel may reach another device: no remote copies, remote signals or barrier semaphores. Data moves between devices by JAX's collectives and lax.ppermute only.
A program may use at most 256 MiB of HBM per device.

```python
import math
import jax
import jax.numpy as jnp
import numpy as np
from jax import lax

D = 768
HEADS = 12
HEAD_DIM = 64
FF = 3072
TOK_DEV = 512
VOC_DEV = 72
GROUPS = 64
VOCAB = 2304
CELL = 1024
CELLS = 16
CAP = 32


def draw_lengths(key, part):
    key = jax.random.fold_in(key, 11)
    first_key, second_key = jax.random.split(key)
    lengths_drawn = jax.random.randint(first_key, (CELLS,), TOK_DEV + 1, CELL + 1)
    chosen_cell = jax.random.randint(second_key, (), 0, CELLS)
    return lengths_drawn.at[chosen_cell].set(CELL).astype(jnp.int32)


def device_run(key):
    owners = VOCAB // VOC_DEV
    slot_count = owners * CAP
    keys = jax.random.split(key, 5)
    score = jax.random.permutation(keys[0], slot_count).astype(jnp.int32)
    target = jax.random.randint(keys[1], (), 0, owners)
    slot_index = jnp.arange(slot_count, dtype=jnp.int32)
    score = jnp.where(slot_index // CAP == target, slot_index % CAP - CAP, score)
    taken = jnp.argsort(score, stable=True)[:TOK_DEV].astype(jnp.int32)
    owner = taken // CAP
    offset = jnp.minimum(jax.random.randint(keys[2], (TOK_DEV,), 0, VOC_DEV), jax.random.randint(keys[3], (TOK_DEV,), 0, VOC_DEV))
    ids = (owner * VOC_DEV + offset).astype(jnp.int32)
    return ids[jax.random.permutation(keys[4], TOK_DEV)]


def draw_gene_ids(key, part):
    key = jax.random.fold_in(key, 23)
    run_keys = jax.random.split(key, CELLS * (CELL // TOK_DEV))
    runs = jax.vmap(device_run)(run_keys)
    return runs.reshape(CELLS, CELL).astype(jnp.int32)


def with_ends(values, stream_key, least, high):
    longest = values.shape.index(max(values.shape))
    spots = []
    for shift in (0, 1):
        where = [jax.random.randint(jax.random.fold_in(stream_key, axis), (), 0, length) for axis, length in enumerate(values.shape)]
        where[longest] = (where[longest] + shift) % values.shape[longest]
        spots.append(tuple(where))
    return values.at[spots[0]].set(least).at[spots[1]].set(high)


def block_levels(own_key, shape, cuts, smallest, high):
    def one(position, blocks):
        draws = jax.random.uniform(jax.random.fold_in(jax.random.fold_in(own_key, 6), position), (blocks,), jnp.float32, smallest / len(cuts), high / len(cuts))
        return jnp.repeat(jnp.exp(draws), shape[position] // blocks).reshape((-1,) + (1,) * (len(shape) - position - 1))

    loudness = one(*cuts[0])
    for cut in cuts[1:]:
        loudness = loudness * one(*cut)
    return loudness


def rank_bounds(number_of, lean):
    weights = [(1 << 20) // math.isqrt(rank ** lean) + 1 for rank in range(1, number_of + 1)]
    scale = 1 + sum(weights) // (1 << 30)
    return np.cumsum(np.array([max(1, weight // scale) for weight in weights]))


def ranked(key, extent, number_of, skew):
    table = rank_bounds(number_of, skew)
    lot = jax.random.randint(jax.random.fold_in(key, 1), extent, 0, int(table[number_of - 1]))
    standing = jnp.searchsorted(jnp.asarray(table, jnp.int32), lot, side="right")
    return jax.random.permutation(jax.random.fold_in(key, 2), number_of)[standing].astype(jnp.int32)


def noise(key, extent, deviation, limit, cuts=(), kind=jnp.bfloat16):
    drawn = deviation * jax.random.normal(key, extent, jnp.float32)
    if cuts:
        drawn = drawn * block_levels(key, extent, cuts, -0.22, 0.18)
    return jnp.clip(drawn, -limit, limit).astype(kind)


def setup_inputs(seed: int = 0) -> dict:
    arg_keys = jax.random.split(jax.random.key(seed), 24)
    gene_ids = draw_gene_ids(jax.random.fold_in(arg_keys[23], 71), 0)
    values = noise(arg_keys[1], (CELLS, CELL), 1.0, 6.0, ((0, 16), (1, 2)), jnp.float32)
    knowledge = noise(arg_keys[2], (CELLS, CELL, D), 1.0, 6.0, ((0, 16), (1, 2)))
    lengths = draw_lengths(jax.random.fold_in(arg_keys[23], 71), 0)
    groups = with_ends(ranked(arg_keys[4], (CELLS,), GROUPS, 2), jax.random.fold_in(arg_keys[4], 3), 0, GROUPS - 1).astype(jnp.int32)
    gene_table = noise(arg_keys[5], (VOCAB, D), 1.0, 6.0)
    group_table = noise(arg_keys[6], (GROUPS, D), 0.5, 4.0)
    w_know = noise(arg_keys[7], (D, D), D ** -0.5, 0.21875)
    w_value = noise(arg_keys[8], (D,), 1.0, 5.0, (), jnp.float32)
    norm1_gain = jnp.clip(1.0 + 0.1 * jax.random.normal(arg_keys[9], (D,), jnp.float32), 0.5, 1.5)
    norm1_bias = noise(arg_keys[10], (D,), 0.3, 2.0, (), jnp.float32)
    w_qkv = noise(arg_keys[11], (D, 3 * D), D ** -0.5, 0.21875)
    bias_q = noise(arg_keys[12], (D,), 0.3, 2.0, (), jnp.float32)
    bias_v = noise(arg_keys[13], (D,), 0.3, 2.0, (), jnp.float32)
    w_out = noise(arg_keys[14], (D, D), (D // 64) ** -0.5, 1.75)
    bias_out = noise(arg_keys[15], (D,), 0.3, 2.0, (), jnp.float32)
    norm2_gain = jnp.clip(1.0 + 0.1 * jax.random.normal(arg_keys[16], (D,), jnp.float32), 0.5, 1.5)
    norm2_bias = noise(arg_keys[17], (D,), 0.3, 2.0, (), jnp.float32)
    w_up = noise(arg_keys[18], (D, FF), D ** -0.5, 0.21875)
    bias_up = noise(arg_keys[19], (FF,), 0.3, 2.0, (), jnp.float32)
    w_down = noise(arg_keys[20], (FF, D), FF ** -0.5, 0.109375)
    bias_down = noise(arg_keys[21], (D,), 0.3, 2.0, (), jnp.float32)
    cotangent = noise(arg_keys[22], (CELLS, CELL, D), 1.0, 6.0, ((0, 16), (1, 2)))
    return {"gene_ids": gene_ids, "values": values, "knowledge": knowledge, "lengths": lengths, "groups": groups, "gene_table": gene_table, "group_table": group_table, "w_know": w_know, "w_value": w_value, "norm1_gain": norm1_gain, "norm1_bias": norm1_bias, "w_qkv": w_qkv, "bias_q": bias_q, "bias_v": bias_v, "w_out": w_out, "bias_out": bias_out, "norm2_gain": norm2_gain, "norm2_bias": norm2_bias, "w_up": w_up, "bias_up": bias_up, "w_down": w_down, "bias_down": bias_down, "cotangent": cotangent}


EPSILON = 1e-05

@jax.custom_vjp
def low(v):
    return lax.optimization_barrier(v.astype(jnp.bfloat16)).astype(jnp.float32)

@jax.custom_vjp
def low_back(v):
    return v

def low_keep(v):
    return (low(v), None)

def low_pass(kept, grad):
    return (grad,)

def back_keep(v):
    return (v, None)

def back_low(kept, grad):
    return (low(grad),)
low.defvjp(low_keep, low_pass)
low_back.defvjp(back_keep, back_low)

def layer_norm(values_in, gain_vec, offset):
    center = values_in - lax.optimization_barrier(jnp.mean(values_in, -1, keepdims=True))
    spread = lax.optimization_barrier(jnp.mean(center * center, -1, keepdims=True))
    return center * lax.rsqrt(spread + EPSILON) * gain_vec + offset

def matmul_high(left, right):
    return jnp.dot(left, right, precision=lax.Precision.HIGHEST)

def cell_forward(params, table_rows, expression, prior, length, group_id):
    group_table, w_know, w_value, norm1_gain, norm1_bias, w_qkv, bias_q, bias_v, w_out, bias_out, norm2_gain, norm2_bias, w_up, bias_up, w_down, bias_down = params
    model_width = w_out.shape[0]
    cell_len = table_rows.shape[0]
    prior_proj = low_back(matmul_high(prior, w_know))
    embedded = table_rows + group_table[group_id][None, :] + expression[:, None] * w_value[None, :] + prior_proj
    normed = low(layer_norm(embedded, norm1_gain, norm1_bias))
    projected = matmul_high(normed, w_qkv)
    queries = low(low_back(projected[:, :model_width] + bias_q))
    key_rows = low(low_back(projected[:, model_width:2 * model_width]))
    value_rows = low(low_back(projected[:, 2 * model_width:] + bias_v))
    score_scale = HEAD_DIM ** (-0.5)
    key_heads = key_rows.reshape(cell_len, HEADS, HEAD_DIM)
    value_heads = value_rows.reshape(cell_len, HEADS, HEAD_DIM)
    key_live = jnp.arange(cell_len) < length
    block_rows = 512 if cell_len % 512 == 0 else cell_len

    def attend(query_block):
        scores = jnp.einsum('qhd,khd->hqk', query_block, key_heads, precision=lax.Precision.HIGHEST) * score_scale
        scores = low_back(scores)
        scores = jnp.where(key_live[None, None, :], scores, -jnp.inf)
        attn_probs = low(jax.nn.softmax(scores, axis=-1))
        return jnp.einsum('hqk,khd->qhd', attn_probs, value_heads, precision=lax.Precision.HIGHEST)
    attended = lax.map(jax.checkpoint(attend), queries.reshape(cell_len // block_rows, block_rows, HEADS, HEAD_DIM))
    attended = low(low_back(attended.reshape(cell_len, model_width)))
    residual = embedded + low_back(matmul_high(attended, w_out) + bias_out)
    normed_two = low(layer_norm(residual, norm2_gain, norm2_bias))
    hidden = low_back(matmul_high(normed_two, w_up) + bias_up)
    activated = low(jax.nn.gelu(hidden, approximate=False))
    final_rows = residual + low_back(matmul_high(activated, w_down) + bias_down)
    live_rows = (jnp.arange(cell_len) < length).astype(jnp.float32)
    return live_rows[:, None] * final_rows

def to_wide(array):
    return array.astype(jnp.float32)

def reference(gene_ids, values, knowledge, lengths, groups, gene_table, group_table, w_know, w_value, norm1_gain, norm1_bias, w_qkv, bias_q, bias_v, w_out, bias_out, norm2_gain, norm2_bias, w_up, bias_up, w_down, bias_down, cotangent):
    params = (to_wide(group_table), to_wide(w_know), w_value, norm1_gain, norm1_bias, to_wide(w_qkv), bias_q, bias_v, to_wide(w_out), bias_out, norm2_gain, norm2_bias, to_wide(w_up), bias_up, to_wide(w_down), bias_down)
    table = to_wide(gene_table)

    def one_cell(carry, inputs):
        param_grads, table_grad = carry
        cell_ids, expression, prior, length, group_id, cot_rows = inputs
        table_rows = table[cell_ids]

        def run(param_set, rows_in):
            return cell_forward(param_set, rows_in, expression, to_wide(prior), length, group_id)
        output, pullback = jax.vjp(run, params, table_rows)
        grad_params, grad_rows = pullback(to_wide(cot_rows))
        param_grads = jax.tree.map(jnp.add, param_grads, grad_params)
        table_grad = table_grad + jax.ops.segment_sum(grad_rows, cell_ids, num_segments=table.shape[0])
        return ((param_grads, table_grad), output.astype(jnp.bfloat16))
    start_state = (jax.tree.map(jnp.zeros_like, params), jnp.zeros_like(table))
    (param_grads, table_grad), outputs = lax.scan(one_cell, start_state, (gene_ids, values, knowledge, lengths, groups, cotangent))
    g_group, g_know, g_value, g_gain1, g_bias1, g_qkv, g_bias_q, g_bias_v, g_out, g_bias_out, g_gain2, g_bias2, g_up, g_bias_up, g_down, g_bias_down = param_grads
    return (outputs, table_grad, g_group, g_know, g_value, g_gain1, g_bias1, g_qkv, g_bias_q, g_bias_v, g_out, g_bias_out, g_gain2, g_bias2, g_up, g_bias_up, g_down, g_bias_down)
```

```python
import jax
import jax.numpy as jnp
from jax import lax
from jax.sharding import PartitionSpec as P

HEADS = 12
HEAD_DIM = 64
VOC_DEV = 72


EPSILON = 1e-05


def layer_norm(values_in, gain_vec, offset):
    center = values_in - jnp.mean(values_in, -1, keepdims=True)
    spread = jnp.mean(center * center, -1, keepdims=True)
    return center * lax.rsqrt(spread + EPSILON) * gain_vec + offset


def contract_rows(left, right):
    return lax.dot_general(
        left, right, (((0,), (0,)), ((), ())), preferred_element_type=jnp.float32
    )


def contract_cols(left, right):
    return lax.dot_general(
        left, right, (((1,), (1,)), ((), ())), preferred_element_type=jnp.float32
    )


def row_sums(array):
    return jnp.sum(array.astype(jnp.float32), 0)


def onehot_rows(grad_rows, slot_ids, count):
    targets = jnp.arange(count, dtype=jnp.int32)
    picker = (slot_ids[:, None] == targets[None, :]).astype(jnp.bfloat16)
    return contract_rows(picker, grad_rows)


def swap_cores(array):
    return lax.ppermute(array, "blk", [(0, 1), (1, 0)])


def bits_apart(array, mask):
    count = lax.axis_size("dp")
    return lax.ppermute(array, "dp", [(i, i ^ mask) for i in range(count)])


def pick(array, position, index):
    return lax.dynamic_index_in_dim(array, index, position, keepdims=False)


def total(terms):
    wide = terms[0].astype(jnp.float32)
    for term in terms[1:]:
        wide = wide + term.astype(jnp.float32)
    return wide


def scatter_sum(terms, turn):
    count = lax.axis_size("dp")
    bits = count.bit_length() - 1
    me = lax.axis_index("dp")
    wire = jnp.bfloat16 if terms[0].dtype == jnp.bfloat16 else jnp.float32
    terms = [term.reshape((2,) * bits + term.shape[1:]) for term in terms]
    left = list(range(bits - 1, -1, -1))
    order = list(range(bits - 2))
    if turn:
        order = order[1::-1] + order[2:]
    for bit in order:
        mine = (me >> bit) & 1
        position = left.index(bit)
        sent = total([pick(term, position, 1 - mine) for term in terms]).astype(wire)
        got = bits_apart(sent, 1 << bit)
        terms = [pick(term, position, mine) for term in terms] + [got]
        left.remove(bit)
    low, high = left[1], left[0]
    mine_low, mine_high = (me >> low) & 1, (me >> high) & 1
    arrived = []
    for step in (1, 2, 3):
        to_low, to_high = mine_low ^ (step & 1), mine_high ^ (step >> 1)
        sent = total([pick(pick(term, 0, to_high), 0, to_low) for term in terms]).astype(wire)
        arrived.append(bits_apart(sent, ((step & 1) << low) | ((step >> 1) << high)))
    return total([pick(pick(term, 0, mine_high), 0, mine_low) for term in terms] + arrived)


def half_columns(array, index):
    half = array.shape[-1] // 2
    return lax.dynamic_slice_in_dim(array, index * half, half, array.ndim - 1)


def both_halves(own, other, block_index):
    first = jnp.where(block_index == 0, own, other)
    second = jnp.where(block_index == 0, other, own)
    return jnp.concatenate([first, second], axis=-1)


def weight_share(grad, turn):
    block_index = lax.axis_index("blk")
    count = lax.axis_size("dp")
    low = grad.astype(jnp.bfloat16).reshape(count, grad.shape[0] // count, grad.shape[1])
    arrived = swap_cores(half_columns(low, 1 - block_index))
    own = scatter_sum([half_columns(low, block_index), arrived], turn)
    return both_halves(own, swap_cores(own), block_index)


def body(
    gene_ids,
    values,
    knowledge,
    lengths,
    groups,
    gene_table,
    group_table,
    w_know,
    w_value,
    norm1_gain,
    norm1_bias,
    w_qkv,
    bias_q,
    bias_v,
    w_out,
    bias_out,
    norm2_gain,
    norm2_bias,
    w_up,
    bias_up,
    w_down,
    bias_down,
    cotangent,
):
    model_width = w_out.shape[0]
    local_rows = gene_ids.shape[1]
    blocks = lax.axis_size("blk")
    block_index = lax.axis_index("blk")
    cell_len = local_rows * blocks
    token_ids = gene_ids[0]
    expression = values[0]
    prior = knowledge[0]
    length = lengths[0]
    positions = block_index * local_rows + jnp.arange(local_rows)
    live_rows = (positions < length).astype(jnp.float32)[:, None]
    group_hot = (jnp.arange(group_table.shape[0]) == groups[0]).astype(jnp.float32)
    group_row = group_table[groups[0]].astype(jnp.float32)
    embedded = (
        gene_table[token_ids].astype(jnp.float32)
        + group_row[None, :]
        + expression[:, None] * w_value[None, :]
        + jnp.dot(prior, w_know, preferred_element_type=jnp.float32)
    )
    normed, norm1_back = jax.vjp(layer_norm, embedded, norm1_gain, norm1_bias)
    normed_low = normed.astype(jnp.bfloat16)
    projected = jnp.dot(normed_low, w_qkv, preferred_element_type=jnp.float32)
    queries = (projected[:, :model_width] + bias_q).astype(jnp.bfloat16)
    key_rows = projected[:, model_width : 2 * model_width].astype(jnp.bfloat16)
    value_rows = (projected[:, 2 * model_width :] + bias_v).astype(jnp.bfloat16)
    key_all = jnp.concatenate([key_rows, swap_cores(key_rows)], axis=0)
    value_all = jnp.concatenate([value_rows, swap_cores(value_rows)], axis=0)
    key_heads = key_all.reshape(cell_len, HEADS, HEAD_DIM)
    value_heads = value_all.reshape(cell_len, HEADS, HEAD_DIM)
    key_live = jnp.concatenate(
        [positions, (1 - block_index) * local_rows + jnp.arange(local_rows)]
    ) < length
    score_scale = HEAD_DIM ** (-0.5)
    block_rows = 512
    count_blocks = local_rows // block_rows
    query_blocks = queries.reshape(count_blocks, block_rows, HEADS, HEAD_DIM)

    def block_scores(query_block):
        scores = (
            jnp.einsum("qhd,khd->hqk", query_block, key_heads, preferred_element_type=jnp.float32)
            * score_scale
        )
        return jnp.where(key_live[None, None, :], scores, -jnp.inf)

    def attend(query_block):
        scores = block_scores(query_block)
        row_max = jnp.max(scores, -1, keepdims=True)
        shifted = jnp.exp(scores - row_max)
        row_total = jnp.sum(shifted, -1, keepdims=True)
        attn_probs = (shifted / row_total).astype(jnp.bfloat16)
        out_block = jnp.einsum(
            "hqk,khd->qhd", attn_probs, value_heads, preferred_element_type=jnp.float32
        )
        return (out_block, row_max + jnp.log(row_total))

    attended, log_totals = lax.map(attend, query_blocks)
    attended = attended.reshape(local_rows, model_width).astype(jnp.bfloat16)
    residual = embedded + (jnp.dot(attended, w_out, preferred_element_type=jnp.float32) + bias_out)
    normed_two, norm2_back = jax.vjp(layer_norm, residual, norm2_gain, norm2_bias)
    normed_two_low = normed_two.astype(jnp.bfloat16)
    hidden = jnp.dot(normed_two_low, w_up, preferred_element_type=jnp.float32) + bias_up
    activated, gelu_back = jax.vjp(
        lambda inner_in: jax.nn.gelu(inner_in, approximate=False), hidden
    )
    activated_low = activated.astype(jnp.bfloat16)
    final_rows = residual + (
        jnp.dot(activated_low, w_down, preferred_element_type=jnp.float32) + bias_down
    )
    block_output = (live_rows * final_rows).astype(jnp.bfloat16)
    grad_final = cotangent[0].astype(jnp.float32) * live_rows
    grad_ffn = grad_final.astype(jnp.bfloat16)
    w_down_grad = contract_rows(activated_low, grad_ffn)
    bias_down_grad = row_sums(grad_ffn)
    grad_act = contract_cols(grad_ffn, w_down)
    grad_hidden = gelu_back(grad_act)[0].astype(jnp.bfloat16)
    w_up_grad = contract_rows(normed_two_low, grad_hidden)
    bias_up_grad = row_sums(grad_hidden)
    grad_normed_two = contract_cols(grad_hidden, w_up)
    grad_resid_norm, norm2_gain_grad, norm2_bias_grad = norm2_back(grad_normed_two)
    grad_residual = grad_final + grad_resid_norm
    grad_branch = grad_residual.astype(jnp.bfloat16)
    w_out_grad = contract_rows(attended, grad_branch)
    bias_out_grad = row_sums(grad_branch)
    grad_attended = contract_cols(grad_branch, w_out).astype(jnp.bfloat16)
    grad_blocks = grad_attended.reshape(count_blocks, block_rows, HEADS, HEAD_DIM)

    def attend_back(carry, inputs):
        key_grad, value_grad = carry
        query_block, grad_block, log_total = inputs
        scores = block_scores(query_block)
        probs_wide = jnp.exp(scores - log_total)
        probs_low = probs_wide.astype(jnp.bfloat16)
        value_grad = value_grad + jnp.einsum(
            "hqk,qhd->khd", probs_low, grad_block, preferred_element_type=jnp.float32
        )
        grad_probs = jnp.einsum(
            "qhd,khd->hqk", grad_block, value_heads, preferred_element_type=jnp.float32
        )
        row_inner = jnp.sum(probs_wide * grad_probs, -1, keepdims=True)
        grad_scores = (probs_wide * (grad_probs - row_inner)).astype(jnp.bfloat16)
        query_grad = (
            jnp.einsum("hqk,khd->qhd", grad_scores, key_heads, preferred_element_type=jnp.float32)
            * score_scale
        )
        key_grad = (
            key_grad
            + jnp.einsum(
                "hqk,qhd->khd", grad_scores, query_block, preferred_element_type=jnp.float32
            )
            * score_scale
        )
        return ((key_grad, value_grad), query_grad)

    empty_heads = jnp.zeros((cell_len, HEADS, HEAD_DIM), jnp.float32)
    (key_part, value_part), query_grads = lax.scan(
        attend_back, (empty_heads, empty_heads), (query_blocks, grad_blocks, log_totals)
    )
    def gather_halves(part):
        low = part.reshape(cell_len, model_width).astype(jnp.bfloat16)
        return low[:local_rows].astype(jnp.float32) + swap_cores(low[local_rows:]).astype(
            jnp.float32
        )

    key_grad, value_grad = gather_halves(key_part), gather_halves(value_part)
    query_low = query_grads.reshape(local_rows, model_width).astype(jnp.bfloat16)
    value_low = value_grad.astype(jnp.bfloat16)
    grad_qkv = jnp.concatenate([query_low, key_grad.astype(jnp.bfloat16), value_low], axis=1)
    w_qkv_grad = contract_rows(normed_low, grad_qkv)
    bias_q_grad = row_sums(query_low)
    bias_v_grad = row_sums(value_low)
    grad_normed = contract_cols(grad_qkv, w_qkv)
    grad_embed_norm, norm1_gain_grad, norm1_bias_grad = norm1_back(grad_normed)
    grad_embedded = grad_residual + grad_embed_norm
    w_know_grad = contract_rows(prior, grad_embedded.astype(jnp.bfloat16))
    w_value_grad = jnp.sum(expression[:, None] * grad_embedded, 0)
    count = lax.axis_size("dp")
    column_total = jnp.sum(grad_embedded, 0)
    group_grad = group_hot[None, :, None] * column_total.reshape(count, 1, -1)
    vectors = (
        w_value_grad,
        norm1_gain_grad,
        norm1_bias_grad,
        bias_q_grad,
        bias_v_grad,
        bias_out_grad,
        norm2_gain_grad,
        norm2_bias_grad,
        bias_up_grad,
        bias_down_grad,
        group_grad,
    )
    packed = jnp.concatenate([vector.reshape(count, -1) for vector in vectors], axis=1)
    widths = [vector.size // count for vector in vectors]
    packed = jnp.pad(packed, ((0, 0), (0, -packed.shape[1] % 256)))
    packed_half = scatter_sum(
        [half_columns(packed, block_index), swap_cores(half_columns(packed, 1 - block_index))],
        0,
    )
    row = both_halves(packed_half, swap_cores(packed_half), block_index)
    parts, start = [], 0
    for width in widths:
        parts.append(row[start : start + width])
        start += width
    (
        w_value_share,
        norm1_gain_share,
        norm1_bias_share,
        bias_q_share,
        bias_v_share,
        bias_out_share,
        norm2_gain_share,
        norm2_bias_share,
        bias_up_share,
        bias_down_share,
        group_share,
    ) = parts
    group_share = group_share.reshape(group_table.shape[0], -1)
    gene_part = onehot_rows(
        grad_embedded.astype(jnp.bfloat16), token_ids, count * blocks * VOC_DEV
    ).astype(jnp.bfloat16)
    gene_part = gene_part.reshape(count, blocks, VOC_DEV, model_width)
    gene_own = pick(gene_part, 1, block_index)
    gene_got = swap_cores(pick(gene_part, 1, 1 - block_index))
    half = model_width // 2
    gene_grad = jnp.concatenate(
        [
            scatter_sum([gene_own[..., :half], gene_got[..., :half]], 0),
            scatter_sum([gene_own[..., half:], gene_got[..., half:]], 1),
        ],
        axis=-1,
    )
    return (
        block_output.reshape(1, local_rows, model_width),
        gene_grad,
        group_share,
        weight_share(w_know_grad, 0),
        w_value_share,
        norm1_gain_share,
        norm1_bias_share,
        jnp.concatenate(
            [
                weight_share(w_qkv_grad[:, :model_width], 0),
                weight_share(w_qkv_grad[:, model_width:], 1),
            ],
            axis=-1,
        ),
        bias_q_share,
        bias_v_share,
        weight_share(w_out_grad, 0),
        bias_out_share,
        norm2_gain_share,
        norm2_bias_share,
        weight_share(w_up_grad, 0),
        bias_up_share,
        weight_share(w_down_grad, 1),
        bias_down_share,
    )


def solution(mesh):
    in_specs = (
        P("dp", "blk"),
        P("dp", "blk"),
        P("dp", "blk", None),
        P("dp"),
        P("dp"),
        P(),
        P(),
        P(),
        P(),
        P(),
        P(),
        P(),
        P(),
        P(),
        P(),
        P(),
        P(),
        P(),
        P(),
        P(),
        P(),
        P(),
        P("dp", "blk", None),
    )
    out_specs = (
        P("dp", "blk", None),
        P(("dp", "blk"), None),
        P(None, "dp"),
        P("dp", None),
        P("dp"),
        P("dp"),
        P("dp"),
        P("dp", None),
        P("dp"),
        P("dp"),
        P("dp", None),
        P("dp"),
        P("dp"),
        P("dp"),
        P("dp", None),
        P("dp"),
        P("dp", None),
        P("dp"),
    )
    return jax.shard_map(body, mesh=mesh, in_specs=in_specs, out_specs=out_specs, check_vma=False)
```

```python
import jax
import jax.numpy as jnp
from jax import lax
from jax.experimental import pallas as pl
from jax.experimental.pallas import tpu as pltpu
from jax.sharding import PartitionSpec as P

HEAD_DIM = 64
VOC_DEV = 72
EPSILON = 1e-05
LOW = jnp.bfloat16
WIDE = jnp.float32
GRANT = 52 << 20


def dot(left, right, left_dim=1, right_dim=0):
    return lax.dot_general(
        left, right, (((left_dim,), (right_dim,)), ((), ())), preferred_element_type=WIDE
    )


def column_sums(array):
    return jnp.sum(array, 0, keepdims=True)


def row_means(array):
    return jnp.mean(array, -1, keepdims=True)


def normalize(array):
    center = array - row_means(array)
    scale = lax.rsqrt(row_means(center * center) + EPSILON)
    return center * scale, scale


def norm_back(grad, unit, scale, gain):
    inner = grad * gain
    return scale * (inner - row_means(inner) - unit * row_means(inner * unit))


def half_of(index, half):
    return pl.ds(pl.multiple_of(index * half, 128), half)


def whole(shape):
    return pl.BlockSpec(shape, lambda *_: (0,) * len(shape))


def params():
    return pltpu.CompilerParams(vmem_limit_bytes=GRANT)


def shaped(shape, dtype):
    return jax.ShapeDtypeStruct(shape, dtype)


def embed_kernel(
    ids_ref,
    expression_ref,
    prior_ref,
    table_ref,
    group_ref,
    w_know_ref,
    w_value_ref,
    gain_ref,
    offset_ref,
    w_key_ref,
    w_val_ref,
    bias_val_ref,
    embedded_ref,
    normed_ref,
    kv_ref,
):
    rows, width = prior_ref.shape
    embedded = dot(prior_ref[...], w_know_ref[...])
    if table_ref.shape[0] == rows:
        gathered = table_ref[...].astype(WIDE)
    else:
        ids = jnp.broadcast_to(ids_ref[...], (8, rows)).T[:, :1]
        slots = lax.broadcasted_iota(jnp.int32, (rows, table_ref.shape[0]), 1)
        picker = jnp.where(slots == ids, 1.0, 0.0).astype(LOW)
        gathered = dot(picker, table_ref[...])
    expression = jnp.broadcast_to(expression_ref[...], (8, rows)).T[:, :1]
    embedded = gathered + group_ref[...] + expression * w_value_ref[...] + embedded
    embedded_ref[...] = embedded
    unit, _ = normalize(embedded)
    normed = (unit * gain_ref[...] + offset_ref[...]).astype(LOW)
    normed_ref[...] = normed
    kv_ref[:, :width] = dot(normed, w_key_ref[...]).astype(LOW)
    kv_ref[:, width:] = (dot(normed, w_val_ref[...]) + bias_val_ref[...]).astype(LOW)


def embed(
    ids, expression, prior, table, group_row, w_know, w_value, gain, offset, w_qkv, bias_v
):
    rows, width = prior.shape
    columns = lambda index: pl.BlockSpec((width, width), lambda _: (0, index))
    return pl.pallas_call(
        embed_kernel,
        grid=(1,),
        in_specs=[
            whole((1, rows)),
            whole((1, rows)),
            whole((rows, width)),
            whole(table.shape),
            whole((1, width)),
            whole((width, width)),
            whole((1, width)),
            whole((1, width)),
            whole((1, width)),
            columns(1),
            columns(2),
            whole((1, width)),
        ],
        out_specs=[whole((rows, width)), whole((rows, width)), whole((rows, 2 * width))],
        out_shape=[
            shaped((rows, width), WIDE),
            shaped((rows, width), LOW),
            shaped((rows, 2 * width), LOW),
        ],
        compiler_params=params(),
        name="embed",
    )(ids, expression, prior, table, group_row, w_know, w_value, gain, offset, w_qkv, w_qkv, bias_v)


def query_kernel(normed_ref, w_query_ref, bias_ref, out_ref):
    out_ref[...] = (dot(normed_ref[...], w_query_ref[...]) + bias_ref[...]).astype(LOW)


def project_queries(normed, w_qkv, bias_q):
    rows, width = normed.shape
    return pl.pallas_call(
        query_kernel,
        grid=(1,),
        in_specs=[whole((rows, width)), whole((width, width)), whole((1, width))],
        out_specs=whole((rows, width)),
        out_shape=shaped((rows, width), LOW),
        compiler_params=params(),
        cost_estimate=pl.CostEstimate(
            flops=2 * rows * width * width, bytes_accessed=4 * rows * width, transcendentals=0
        ),
        name="queries",
    )(normed, w_qkv, bias_q)


def attend_kernel(live_ref, q_ref, ko_ref, vo_ref, kr_ref, vr_ref, out_ref, p_ref, c_ref):
    rows = q_ref.shape[0]
    lane = lax.broadcasted_iota(jnp.int32, (rows, 128), 1)
    place = lax.broadcasted_iota(jnp.int32, (rows, 128), 0)
    queries = q_ref[...] * LOW(HEAD_DIM**-0.5)
    halves = []
    for index, k_ref in enumerate((ko_ref, kr_ref)):
        dead = jnp.where(place < live_ref[index], 0.0, -1e30).astype(LOW)
        halves.append((k_ref[...], dead))
    values = [vo_ref[...].T, vr_ref[...].T]
    outs = []
    for head in range(2):
        inside = (lane < HEAD_DIM) if head == 0 else (lane >= HEAD_DIM)
        spare = HEAD_DIM * (1 - head)
        asked = jnp.where(inside, queries, jnp.where(lane == spare, 1.0, 0.0).astype(LOW))
        scores = [dot(jnp.where(lane == spare, dead, keys), asked, 1, 1) for keys, dead in halves]
        top = jnp.maximum(*[jnp.max(part, 0, keepdims=True) for part in scores])
        mass, mixed = 0.0, 0.0
        for index in range(2):
            probs = jnp.exp(scores[index] - top)
            mass = mass + column_sums(probs)
            low = probs.astype(LOW)
            p_ref[head, index * rows : (index + 1) * rows, :] = low
            mixed = mixed + dot(values[index][head * HEAD_DIM : (head + 1) * HEAD_DIM], low)
        inverse = 1.0 / mass
        c_ref[0, head : head + 1, :] = inverse
        outs.append(mixed * inverse)
    out_ref[...] = jnp.concatenate(outs, 0).T.astype(LOW)


def attend(live, queries, kv_own, kv_other):
    rows, width = queries.shape
    pairs = width // 128
    block = lambda shift: pl.BlockSpec((rows, 128), lambda j, _: (0, shift + j))
    return pl.pallas_call(
        attend_kernel,
        grid_spec=pltpu.PrefetchScalarGridSpec(
            num_scalar_prefetch=1,
            grid=(pairs,),
            in_specs=[block(0), block(0), block(pairs), block(0), block(pairs)],
            out_specs=[
                block(0),
                pl.BlockSpec((2, 2 * rows, rows), lambda j, _: (j, 0, 0)),
                pl.BlockSpec((1, 2, rows), lambda j, _: (j, 0, 0)),
            ],
        ),
        out_shape=[
            shaped((rows, width), LOW),
            shaped((2 * pairs, 2 * rows, rows), LOW),
            shaped((pairs, 2, rows), WIDE),
        ],
        compiler_params=params(),
        cost_estimate=pl.CostEstimate(
            flops=16 * rows * rows * width,
            bytes_accessed=8 * rows * rows * pairs,
            transcendentals=4 * rows * rows * pairs,
        ),
        name="attend",
    )(live, queries, kv_own, kv_own, kv_other, kv_other)


def attend_back_kernel(
    q_ref,
    ko_ref,
    vo_ref,
    kr_ref,
    vr_ref,
    a_ref,
    g_ref,
    p_ref,
    c_ref,
    after_ref,
    dq_ref,
    dkvo_ref,
    dkvr_ref,
):
    rows = q_ref.shape[0]
    lane = lax.broadcasted_iota(jnp.int32, (rows, 128), 1)
    mixed = a_ref[...].astype(WIDE).T
    grad = g_ref[...].astype(WIDE).T
    grad = jnp.concatenate(
        [grad[:HEAD_DIM] * c_ref[0, :1, :], grad[HEAD_DIM:] * c_ref[0, 1:, :]], 0
    )
    inner = grad * mixed
    inner = [column_sums(inner[:HEAD_DIM]), column_sums(inner[HEAD_DIM:])]
    first = lax.broadcasted_iota(jnp.int32, (128, rows), 0) < HEAD_DIM
    low = grad.astype(LOW)
    masked = [
        jnp.where(first, low, jnp.zeros_like(low)),
        jnp.where(first, jnp.zeros_like(low), low),
    ]
    grad_rows = grad.T.astype(LOW)
    queries = q_ref[...]
    parts = [0.0, 0.0]
    for index, (k_ref, v_ref, out_ref) in enumerate(
        ((ko_ref, vo_ref, dkvo_ref), (kr_ref, vr_ref, dkvr_ref))
    ):
        keys = k_ref[...].T
        values = v_ref[...]
        key_grads, val_grads = [], []
        for head in range(2):
            probs = p_ref[head, index * rows : (index + 1) * rows, :]
            wide = dot(values, masked[head]) - inner[head]
            score = (probs.astype(WIDE) * wide).astype(LOW)
            val_grads.append(dot(probs, grad_rows))
            key_grads.append(dot(score, queries))
            parts[head] = parts[head] + dot(keys[head * HEAD_DIM : (head + 1) * HEAD_DIM], score)
        chosen = lane < HEAD_DIM
        out_ref[0] = (jnp.where(chosen, *key_grads) * HEAD_DIM**-0.5).astype(LOW)
        out_ref[1] = jnp.where(chosen, *val_grads).astype(LOW)
    dq_ref[...] = (jnp.concatenate(parts, 0).T * HEAD_DIM**-0.5).astype(LOW)


def attend_back(queries, kv_own, kv_other, attended, grad, probs, inverse, start, count, after):
    rows, width = queries.shape
    pairs = width // 128
    block = lambda shift: pl.BlockSpec((rows, 128), lambda j: (0, shift + j))
    near, far = block(start), block(pairs + start)
    both = pl.BlockSpec((2, rows, 128), lambda j: (0, 0, j))
    return pl.pallas_call(
        attend_back_kernel,
        grid=(count,),
        in_specs=[
            near,
            near,
            far,
            near,
            far,
            near,
            near,
            pl.BlockSpec((2, 2 * rows, rows), lambda j: (start + j, 0, 0)),
            pl.BlockSpec((1, 2, rows), lambda j: (start + j, 0, 0)),
            pl.BlockSpec(memory_space=pl.ANY),
        ],
        out_specs=[block(0), both, both],
        out_shape=[
            shaped((rows, 128 * count), LOW),
            shaped((2, rows, 128 * count), LOW),
            shaped((2, rows, 128 * count), LOW),
        ],
        compiler_params=params(),
        cost_estimate=pl.CostEstimate(
            flops=32 * rows * rows * 128 * count * 2,
            bytes_accessed=8 * rows * rows * count,
            transcendentals=0,
        ),
        name="attend_back",
    )(queries, kv_own, kv_own, kv_other, kv_other, attended, grad, probs, inverse, after)


def ffn_kernel(
    place_ref,
    attended_ref,
    embedded_ref,
    cotangent_ref,
    w_out_ref,
    bias_out_ref,
    gain_ref,
    offset_ref,
    w_up_ref,
    bias_up_ref,
    w_down_ref,
    bias_down_ref,
    output_ref,
    g_residual_ref,
    g_attended_ref,
    up_send_ref,
    up_keep_ref,
    down_send_ref,
    down_keep_ref,
    vectors_ref,
    bias_up_grad_ref,
    residual_ref,
    normed_ref,
    turned_ref,
    total_ref,
    g_normed_ref,
    g_out_ref,
):
    step, steps = pl.program_id(0), pl.num_programs(0)
    rows, width = attended_ref.shape
    tile = w_up_ref.shape[1]
    mine = place_ref[0]
    own, other = half_of(mine, width // 2), half_of(1 - mine, width // 2)
    alive = lax.broadcasted_iota(jnp.int32, (rows, 1), 0) < place_ref[1]

    @pl.when(step == 0)
    def _():
        residual = embedded_ref[...] + (dot(attended_ref[...], w_out_ref[...]) + bias_out_ref[...])
        residual_ref[...] = residual
        unit, _ = normalize(residual)
        normed = unit * gain_ref[...] + offset_ref[...]
        normed_ref[...] = normed.astype(LOW)
        turned_ref[...] = normed.T.astype(LOW)
        g_out_ref[...] = jnp.where(alive, cotangent_ref[...].astype(WIDE), 0.0).astype(LOW)
        total_ref[...] = jnp.zeros_like(total_ref)
        g_normed_ref[...] = jnp.zeros_like(g_normed_ref)

    g_out = g_out_ref[...]
    hidden = dot(normed_ref[...], w_up_ref[...]) + bias_up_ref[...]
    g_act = dot(g_out, w_down_ref[...], 1, 1)
    share = 0.5 * (1.0 + lax.erf(hidden * 0.5**0.5))
    density = jnp.exp(-0.5 * hidden * hidden) * 0.3989422804014327
    activated = (hidden * share).astype(LOW)
    g_wide = g_act * (share + hidden * density)
    g_hidden = g_wide.astype(LOW)
    total_ref[...] += dot(activated, w_down_ref[...])
    g_normed_ref[...] += dot(g_hidden, w_up_ref[...], 1, 1)
    down_send_ref[...] = dot(activated, g_out_ref[:, other], 0, 0).astype(LOW)
    down_keep_ref[...] = dot(activated, g_out_ref[:, own], 0, 0).astype(LOW)
    up = dot(turned_ref[...], g_hidden).astype(LOW)
    bias_up_grad_ref[...] = column_sums(g_hidden.astype(WIDE))
    columns = pl.ds(pl.multiple_of(lax.rem(step, steps // 2) * tile, 128), tile)

    @pl.when(step < steps // 2)
    def _():
        up_send_ref[:, columns] = up

    @pl.when(step >= steps // 2)
    def _():
        up_keep_ref[:, columns] = up

    @pl.when(step == steps - 1)
    def _():
        residual = residual_ref[...]
        final = residual + (total_ref[...] + bias_down_ref[...])
        output_ref[...] = jnp.where(alive, final, 0.0).astype(LOW)
        unit, scale = normalize(residual)
        g_final = g_out_ref[...].astype(WIDE)
        g_normed = g_normed_ref[...]
        g_residual = g_final + norm_back(g_normed, unit, scale, gain_ref[...])
        g_residual_ref[...] = g_residual
        g_branch = g_residual.astype(LOW)
        g_attended_ref[...] = dot(g_branch, w_out_ref[...], 1, 1).astype(LOW)
        vectors_ref[...] = jnp.concatenate(
            [
                column_sums(g_branch.astype(WIDE)),
                column_sums(g_normed * unit),
                column_sums(g_normed),
                column_sums(g_final),
            ],
            0,
        )
        normed_ref[...] = g_branch
        attended = attended_ref[...].astype(WIDE).T.astype(LOW)
        half = width // 2
        last = up_send_ref.shape[1] - half
        up_send_ref[:, last:] = dot(attended, normed_ref[:, other]).astype(LOW)
        up_keep_ref[:, last:] = dot(attended, normed_ref[:, own]).astype(LOW)


def feed_forward(
    place,
    attended,
    embedded,
    cotangent,
    w_out,
    bias_out,
    gain,
    offset,
    w_up,
    bias_up,
    w_down,
    bias_down,
):
    rows, width = attended.shape
    units = w_up.shape[1]
    tile = 768
    steps = units // tile
    turn = lambda j, place: lax.rem(j + (1 - place[0]) * (steps // 2), steps)
    down_tile = pl.BlockSpec((tile, width // 2), lambda j, place: (turn(j, place), 0))
    merged = units // 2 + width // 2
    return pl.pallas_call(
        ffn_kernel,
        grid_spec=pltpu.PrefetchScalarGridSpec(
            num_scalar_prefetch=1,
            grid=(steps,),
            in_specs=[
                whole((rows, width)),
                whole((rows, width)),
                whole((rows, width)),
                whole((width, width)),
                whole((1, width)),
                whole((1, width)),
                whole((1, width)),
                pl.BlockSpec((width, tile), lambda j, place: (0, turn(j, place))),
                pl.BlockSpec((1, tile), lambda j, place: (0, turn(j, place))),
                pl.BlockSpec((tile, width), lambda j, place: (turn(j, place), 0)),
                whole((1, width)),
            ],
            out_specs=[
                whole((rows, width)),
                whole((rows, width)),
                whole((rows, width)),
                whole((width, merged)),
                whole((width, merged)),
                down_tile,
                down_tile,
                whole((4, width)),
                pl.BlockSpec((1, tile), lambda j, place: (0, turn(j, place))),
            ],
            scratch_shapes=[
                pltpu.VMEM((rows, width), WIDE),
                pltpu.VMEM((rows, width), LOW),
                pltpu.VMEM((width, rows), LOW),
                pltpu.VMEM((rows, width), WIDE),
                pltpu.VMEM((rows, width), WIDE),
                pltpu.VMEM((rows, width), LOW),
            ],
        ),
        out_shape=[
            shaped((rows, width), LOW),
            shaped((rows, width), WIDE),
            shaped((rows, width), LOW),
            shaped((width, merged), LOW),
            shaped((width, merged), LOW),
            shaped((units, width // 2), LOW),
            shaped((units, width // 2), LOW),
            shaped((4, width), WIDE),
            shaped((1, units), WIDE),
        ],
        compiler_params=params(),
        cost_estimate=pl.CostEstimate(
            flops=12 * rows * width * units + 6 * rows * width * width,
            bytes_accessed=8 * width * units,
            transcendentals=2 * rows * units,
        ),
        name="feed_forward",
    )(
        place,
        attended,
        embedded,
        cotangent,
        w_out,
        bias_out,
        gain,
        offset,
        w_up,
        bias_up,
        w_down,
        bias_down,
    )


def project_back(place_ref, normed_turned, dq_ref, own_ref, got_ref, weights, joined_ref, send_ref, keep_ref, bias_ref):
    group = dq_ref.shape[1]
    half = 3 * group // 2
    mine = place_ref[0]
    joined_ref[:, :group] = dq_ref[...]
    for index in range(2):
        total = own_ref[index].astype(WIDE) + got_ref[index].astype(WIDE)
        joined_ref[:, (1 + index) * group : (2 + index) * group] = total.astype(LOW)
    send_ref[:, :half] = dot(normed_turned, joined_ref[:, half_of(1 - mine, half)]).astype(LOW)
    keep_ref[:, :half] = dot(normed_turned, joined_ref[:, half_of(mine, half)]).astype(LOW)
    bias_ref[0:1] = column_sums(joined_ref[:, :group].astype(WIDE))
    bias_ref[1:2] = column_sums(joined_ref[:, 2 * group :].astype(WIDE))
    back = 0.0
    for index, weight_ref in enumerate(weights):
        part = joined_ref[:, index * group : (index + 1) * group]
        back = back + dot(part, weight_ref[...], 1, 1)
    return back


def first_back_kernel(
    place_ref,
    normed_ref,
    dq_ref,
    own_ref,
    got_ref,
    wq_ref,
    wk_ref,
    wv_ref,
    send_ref,
    keep_ref,
    bias_ref,
    part_ref,
    turned_ref,
    joined_ref,
):
    @pl.when(pl.program_id(0) == 0)
    def _():
        turned_ref[...] = normed_ref[...].astype(WIDE).T.astype(LOW)
        part_ref[...] = jnp.zeros_like(part_ref)

    part_ref[...] += project_back(
        place_ref,
        turned_ref[...],
        dq_ref,
        own_ref,
        got_ref,
        (wq_ref, wk_ref, wv_ref),
        joined_ref,
        send_ref,
        keep_ref,
        bias_ref,
    )


def last_back_kernel(
    place_ref,
    normed_ref,
    dq_ref,
    own_ref,
    got_ref,
    wq_ref,
    wk_ref,
    wv_ref,
    part_ref,
    embedded_ref,
    g_residual_ref,
    gain_ref,
    prior_ref,
    expression_ref,
    bias_first_ref,
    vectors_ref,
    bias_up_ref,
    send_ref,
    keep_ref,
    g_low_ref,
    rows_ref,
    turned_ref,
    joined_ref,
    bias_ref,
):
    rows, width = normed_ref.shape
    half = width // 2
    mine = place_ref[0]
    turned_ref[...] = normed_ref[...].astype(WIDE).T.astype(LOW)
    back = part_ref[...] + project_back(
        place_ref,
        turned_ref[...],
        dq_ref,
        own_ref,
        got_ref,
        (wq_ref, wk_ref, wv_ref),
        joined_ref,
        send_ref,
        keep_ref,
        bias_ref,
    )
    unit, scale = normalize(embedded_ref[...])
    g_embedded = g_residual_ref[...] + norm_back(back, unit, scale, gain_ref[...])
    g_low_ref[...] = g_embedded.astype(LOW)
    prior = prior_ref[...].astype(WIDE).T.astype(LOW)
    send_ref[:, half:] = dot(prior, g_low_ref[:, half_of(1 - mine, half)]).astype(LOW)
    keep_ref[:, half:] = dot(prior, g_low_ref[:, half_of(mine, half)]).astype(LOW)
    expression = jnp.broadcast_to(expression_ref[...], (8, rows)).T[:, :1]
    total = column_sums(g_embedded)
    groups = rows_ref.shape[0] - 16
    hot = lax.broadcasted_iota(jnp.int32, (groups, width), 0) == place_ref[1]
    rows_ref[:groups] = jnp.where(hot, total, 0.0)
    rows_ref[groups:] = jnp.concatenate(
        [
            column_sums(expression * g_embedded),
            column_sums(back * unit),
            column_sums(back),
            jnp.concatenate([bias_first_ref[0, 0:1], bias_first_ref[1, 0:1], bias_ref[0:1]], 1),
            jnp.concatenate([bias_first_ref[0, 1:2], bias_first_ref[1, 1:2], bias_ref[1:2]], 1),
            vectors_ref[...],
            bias_up_ref[...],
            jnp.zeros((3, width), WIDE),
        ],
        0,
    )


def back_specs(rows, width, group, first):
    third = width // group
    weight = lambda part: pl.BlockSpec((width, group), lambda j, _: (0, part * third + first + j))
    both = pl.BlockSpec((2, rows, group), lambda j, _: (0, 0, j))
    return [
        whole((rows, width)),
        pl.BlockSpec((rows, group), lambda j, _: (0, j)),
        both,
        both,
        weight(0),
        weight(1),
        weight(2),
    ]


def first_back(place, normed, dq, own, got, w_qkv, group):
    rows, width = normed.shape
    count = dq.shape[1] // group
    half = 3 * group // 2
    tile = pl.BlockSpec((width, half), lambda j, _: (0, j))
    return pl.pallas_call(
        first_back_kernel,
        grid_spec=pltpu.PrefetchScalarGridSpec(
            num_scalar_prefetch=1,
            grid=(count,),
            in_specs=back_specs(rows, width, group, 0),
            out_specs=[
                tile,
                tile,
                pl.BlockSpec((None, 2, group), lambda j, _: (j, 0, 0)),
                whole((rows, width)),
            ],
            scratch_shapes=[
                pltpu.VMEM((width, rows), LOW),
                pltpu.VMEM((rows, 3 * group), LOW),
            ],
        ),
        out_shape=[
            shaped((width, count * half), LOW),
            shaped((width, count * half), LOW),
            shaped((count, 2, group), WIDE),
            shaped((rows, width), WIDE),
        ],
        compiler_params=params(),
        cost_estimate=pl.CostEstimate(
            flops=12 * rows * width * group * count,
            bytes_accessed=16 * width * width,
            transcendentals=0,
        ),
        name="first_back",
    )(place, normed, dq, own, got, w_qkv, w_qkv, w_qkv)


def last_back(
    place,
    normed,
    dq,
    own,
    got,
    w_qkv,
    group,
    part,
    embedded,
    g_residual,
    gain,
    prior,
    expression,
    bias_first,
    vectors,
    bias_up,
    groups,
):
    rows, width = normed.shape
    half = width // 2
    first = width // group - 1
    return pl.pallas_call(
        last_back_kernel,
        grid_spec=pltpu.PrefetchScalarGridSpec(
            num_scalar_prefetch=1,
            grid=(1,),
            in_specs=back_specs(rows, width, group, first)
            + [
                whole((rows, width)),
                whole((rows, width)),
                whole((rows, width)),
                whole((1, width)),
                whole((rows, width)),
                whole((1, rows)),
                whole(bias_first.shape),
                whole((4, width)),
                whole((4, width)),
            ],
            out_specs=[
                whole((width, width)),
                whole((width, width)),
                whole((rows, width)),
                whole((groups + 16, width)),
            ],
            scratch_shapes=[
                pltpu.VMEM((width, rows), LOW),
                pltpu.VMEM((rows, 3 * group), LOW),
                pltpu.VMEM((2, group), WIDE),
            ],
        ),
        out_shape=[
            shaped((width, width), LOW),
            shaped((width, width), LOW),
            shaped((rows, width), LOW),
            shaped((groups + 16, width), WIDE),
        ],
        compiler_params=params(),
        name="last_back",
    )(
        place,
        normed,
        dq,
        own,
        got,
        w_qkv,
        w_qkv,
        w_qkv,
        part,
        embedded,
        g_residual,
        gain,
        prior,
        expression,
        bias_first,
        vectors,
        bias_up,
    )


def gene_kernel(slots_ref, ids_ref, grad_ref, out_ref):
    slots = slots_ref[...]
    rows = grad_ref.shape[0]
    picker = jnp.where(slots == jnp.broadcast_to(ids_ref[...], (slots.shape[0], rows)), 1.0, 0.0)
    out_ref[...] = dot(picker.astype(LOW), grad_ref[...]).astype(LOW)


def gene_rows(slots, ids, grad):
    count = slots.shape[0]
    rows, width = grad.shape
    tile = min(count, 1152)
    return pl.pallas_call(
        gene_kernel,
        grid=(count // tile,),
        in_specs=[
            pl.BlockSpec((tile, 1), lambda j: (j, 0)),
            whole((1, rows)),
            whole((rows, width)),
        ],
        out_specs=pl.BlockSpec((tile, width), lambda j: (j, 0)),
        out_shape=shaped((count, width), LOW),
        compiler_params=params(),
        cost_estimate=pl.CostEstimate(
            flops=2 * rows * width * count, bytes_accessed=2 * width * count, transcendentals=0
        ),
        name="gene_rows",
    )(slots, ids, grad)


def swap_cores(array):
    return lax.ppermute(array, "blk", [(0, 1), (1, 0)])


def bits_apart(array, mask):
    count = lax.axis_size("dp")
    return lax.ppermute(array, "dp", [(i, i ^ mask) for i in range(count)])


def pick(array, position, index):
    return lax.dynamic_index_in_dim(array, index, position, keepdims=False)


def total(terms):
    wide = terms[0].astype(WIDE)
    for term in terms[1:]:
        wide = wide + term.astype(WIDE)
    return wide


class Share:
    def __init__(self, terms, turn, wire=LOW):
        count = lax.axis_size("dp")
        bits = count.bit_length() - 1
        self.me = lax.axis_index("dp")
        self.wire = wire
        self.terms = [term.reshape((2,) * bits + term.shape[1:]) for term in terms]
        self.left = list(range(bits - 1, -1, -1))
        order = list(range(bits - 2))
        self.order = order[1::-1] + order[2:] if turn else order

    def halve(self):
        bit = self.order.pop(0)
        mine = (self.me >> bit) & 1
        position = self.left.index(bit)
        sent = total([pick(term, position, 1 - mine) for term in self.terms]).astype(self.wire)
        got = bits_apart(sent, 1 << bit)
        self.terms = [pick(term, position, mine) for term in self.terms] + [got]
        self.left.remove(bit)
        return sent

    def finish(self):
        while self.order:
            self.halve()
        low, high = self.left[1], self.left[0]
        mine_low, mine_high = (self.me >> low) & 1, (self.me >> high) & 1
        arrived = []
        for step in (1, 2, 3):
            to_low, to_high = mine_low ^ (step & 1), mine_high ^ (step >> 1)
            sent = total([pick(pick(term, 0, to_high), 0, to_low) for term in self.terms])
            mask = ((step & 1) << low) | ((step >> 1) << high)
            arrived.append(bits_apart(sent.astype(self.wire), mask))
        own = [pick(pick(term, 0, mine_high), 0, mine_low) for term in self.terms]
        return total(own + arrived)


def both_halves(own, block_index):
    other = swap_cores(own)
    return (
        jnp.where(block_index == 0, own, other),
        jnp.where(block_index == 0, other, own),
    )


def body(
    gene_ids,
    values,
    knowledge,
    lengths,
    groups,
    gene_table,
    group_table,
    w_know,
    w_value,
    norm1_gain,
    norm1_bias,
    w_qkv,
    bias_q,
    bias_v,
    w_out,
    bias_out,
    norm2_gain,
    norm2_bias,
    w_up,
    bias_up,
    w_down,
    bias_down,
    cotangent,
):
    width = w_out.shape[0]
    units = w_up.shape[1]
    rows = gene_ids.shape[1]
    count = lax.axis_size("dp")
    mine = lax.axis_index("blk")
    length, group = lengths[0], groups[0]
    prior = knowledge[0]
    row = lambda vector: vector.reshape(1, -1)
    live_own = length - mine * rows
    live_other = length - (1 - mine) * rows
    group_row = group_table[group].astype(WIDE)[None]
    if gene_table.shape[0] > 8 * rows:
        table = gene_table[gene_ids[0]]
    else:
        table = gene_table
    embedded, normed, kv_own = embed(
        gene_ids,
        values,
        prior,
        table,
        group_row,
        w_know,
        row(w_value),
        row(norm1_gain),
        row(norm1_bias),
        w_qkv,
        row(bias_v),
    )
    kv_other = swap_cores(kv_own)
    queries = project_queries(normed, w_qkv, row(bias_q))
    attended, probs, inverse = attend(
        jnp.stack([live_own, live_other]).astype(jnp.int32), queries, kv_own, kv_other
    )
    (
        block_output,
        g_residual,
        g_attended,
        up_send,
        up_keep,
        down_send,
        down_keep,
        vectors,
        bias_up_grad,
    ) = feed_forward(
        jnp.stack([mine, live_own]).astype(jnp.int32),
        attended,
        embedded,
        cotangent[0],
        w_out,
        row(bias_out),
        row(norm2_gain),
        row(norm2_bias),
        w_up,
        row(bias_up),
        w_down,
        row(bias_down),
    )

    owners = lambda array: array.reshape(count, -1, array.shape[-1])
    down = Share([owners(down_keep), owners(swap_cores(down_send))], 0)
    up = Share([owners(up_keep), owners(swap_cores(up_send))], 1)
    dq1, own1, other1 = attend_back(
        queries, kv_own, kv_other, attended, g_attended, probs, inverse, 0, 4, g_attended
    )
    got1 = swap_cores(other1)
    down.halve()
    after = up.halve()
    dq2, own2, other2 = attend_back(
        queries, kv_own, kv_other, attended, g_attended, probs, inverse, 4, 2, after
    )
    got2 = swap_cores(other2)
    place = jnp.stack([mine, group]).astype(jnp.int32)
    qkv_send, qkv_keep, bias_first, part = first_back(
        place, normed, dq1, own1, got1, w_qkv, 256
    )
    tail_send, tail_keep, g_low, sums = last_back(
        place,
        normed,
        dq2,
        own2,
        got2,
        w_qkv,
        256,
        part,
        embedded,
        g_residual,
        row(norm1_gain),
        prior,
        values,
        bias_first,
        vectors,
        bias_up_grad.reshape(count, 4, -1).swapaxes(0, 1).reshape(4, width),
        group_table.shape[0],
    )
    slot = jnp.arange(count * VOC_DEV, dtype=jnp.int32)[:, None]
    slot = slot + slot // VOC_DEV * VOC_DEV
    gene_send = gene_rows(slot + (1 - mine) * VOC_DEV, gene_ids, g_low)
    gene_got = swap_cores(gene_send)
    gene_keep = gene_rows(slot + mine * VOC_DEV, gene_ids, g_low)
    qkv = Share([owners(qkv_keep), owners(swap_cores(qkv_send))], 0)
    tail = Share([owners(tail_keep), owners(swap_cores(tail_send))], 1)
    half = width // 2
    gene_terms = [owners(gene_keep), owners(gene_got)]
    gene_left = Share([term[..., :half] for term in gene_terms], 0)
    gene_right = Share([term[..., half:] for term in gene_terms], 1)

    sums = sums.reshape(-1, count, width // count).swapaxes(0, 1).reshape(count, 2, -1)
    small = Share([pick(sums, 1, mine), swap_cores(pick(sums, 1, 1 - mine))], 0, WIDE)

    down_halves = both_halves(down.finish(), mine)
    up_halves = both_halves(up.finish(), mine)
    qkv_halves = both_halves(qkv.finish(), mine)
    gene_grad = jnp.concatenate([gene_left.finish(), gene_right.finish()], 1)
    tail_halves = both_halves(tail.finish(), mine)
    small = jnp.concatenate(both_halves(small.finish(), mine)).reshape(-1, width // count)
    join = lambda pieces: jnp.concatenate(pieces, 1)
    q_parts, k_parts, v_parts = [], [], []
    cut = 384
    for index in range(3):
        if index < 2:
            low, high = [side[:, index * cut : (index + 1) * cut] for side in qkv_halves]
        else:
            low, high = [side[:, :cut] for side in tail_halves]
        q_parts.append(low[:, :256])
        k_parts += [low[:, 256:], high[:, :128]]
        v_parts.append(high[:, 128:])
    extra = small[group_table.shape[0] :]
    return (
        block_output[None],
        gene_grad,
        small[: group_table.shape[0]],
        join([side[:, cut:] for side in tail_halves]),
        extra[0],
        extra[1],
        extra[2],
        join(q_parts + k_parts + v_parts),
        extra[3],
        extra[4],
        join([side[:, units // 2 :] for side in up_halves]),
        extra[5],
        extra[6],
        extra[7],
        join([side[:, : units // 2] for side in up_halves]),
        extra[9:13].reshape(-1),
        join(down_halves),
        extra[8],
    )


def solution(mesh):
    in_specs = (
        P("dp", "blk"),
        P("dp", "blk"),
        P("dp", "blk", None),
        P("dp"),
        P("dp"),
        P(),
        P(),
        P(),
        P(),
        P(),
        P(),
        P(),
        P(),
        P(),
        P(),
        P(),
        P(),
        P(),
        P(),
        P(),
        P(),
        P(),
        P("dp", "blk", None),
    )
    out_specs = (
        P("dp", "blk", None),
        P(("dp", "blk"), None),
        P(None, "dp"),
        P("dp", None),
        P("dp"),
        P("dp"),
        P("dp"),
        P("dp", None),
        P("dp"),
        P("dp"),
        P("dp", None),
        P("dp"),
        P("dp"),
        P("dp"),
        P("dp", None),
        P("dp"),
        P("dp", None),
        P("dp"),
    )
    return jax.shard_map(body, mesh=mesh, in_specs=in_specs, out_specs=out_specs, check_vma=False)
```

```python
import functools

import jax
import jax.numpy as jnp
from jax import lax
from jax.experimental import pallas as pl
from jax.experimental.pallas import tpu as pltpu
from jax.sharding import PartitionSpec as P

HEAD_DIM = 64
VOC_DEV = 72
EPSILON = 1e-05
LOW = jnp.bfloat16
WIDE = jnp.float32
GRANT = 52 << 20


LONG = pl.CostEstimate(flops=10**12, bytes_accessed=1, transcendentals=0)


def dot(left, right, left_dim=1, right_dim=0):
    return lax.dot_general(
        left, right, (((left_dim,), (right_dim,)), ((), ())), preferred_element_type=WIDE
    )


def column_sums(array):
    return jnp.sum(array, 0, keepdims=True)


def row_means(array):
    return jnp.mean(array, -1, keepdims=True)


def normalize(array):
    center = array - row_means(array)
    scale = lax.rsqrt(row_means(center * center) + EPSILON)
    return center * scale, scale


def norm_back(grad, unit, scale, gain):
    inner = grad * gain
    return scale * (inner - row_means(inner) - unit * row_means(inner * unit))


def half_of(index, half):
    return pl.ds(pl.multiple_of(index * half, 128), half)


def whole(shape):
    return pl.BlockSpec(shape, lambda *_: (0,) * len(shape))


def params(grant=GRANT):
    return pltpu.CompilerParams(vmem_limit_bytes=grant)


def shaped(shape, dtype):
    return jax.ShapeDtypeStruct(shape, dtype)


def embed_kernel(
    place_ref,
    ids_ref,
    expression_ref,
    prior_ref,
    table_ref,
    group_ref,
    w_know_ref,
    w_value_ref,
    gain_ref,
    offset_ref,
    w_key_ref,
    w_val_ref,
    bias_val_ref,
    embedded_ref,
    normed_ref,
    kv_ref,
):
    rows, width = prior_ref.shape
    embedded = dot(prior_ref[...], w_know_ref[...])
    if table_ref.shape[0] == rows:
        gathered = table_ref[...].astype(WIDE)
    else:
        ids = jnp.broadcast_to(ids_ref[...], (8, rows)).T[:, :1]
        slots = lax.broadcasted_iota(jnp.int32, (rows, table_ref.shape[0]), 1)
        picker = jnp.where(slots == ids, 1.0, 0.0).astype(LOW)
        gathered = dot(picker, table_ref[...])
    expression = jnp.broadcast_to(expression_ref[...], (8, rows)).T[:, :1]
    groups = lax.broadcasted_iota(jnp.int32, (8, group_ref.shape[0]), 1)
    group_row = dot(jnp.where(groups == place_ref[3], 1.0, 0.0).astype(LOW), group_ref[...])[:1]
    embedded = gathered + group_row + expression * w_value_ref[...][None] + embedded
    embedded_ref[...] = embedded
    unit, _ = normalize(embedded)
    normed = (unit * gain_ref[...][None] + offset_ref[...][None]).astype(LOW)
    normed_ref[...] = normed
    kv_ref[:, :width] = dot(normed, w_key_ref[...]).astype(LOW)
    kv_ref[:, width:] = (dot(normed, w_val_ref[...]) + bias_val_ref[...][None]).astype(LOW)


def embed(
    place, ids, expression, prior, table, group_table, w_know, w_value, gain, offset, w_qkv, bias_v
):
    rows, width = prior.shape
    columns = lambda index: pl.BlockSpec((width, width), lambda *_: (0, index))
    return pl.pallas_call(
        embed_kernel,
        grid_spec=pltpu.PrefetchScalarGridSpec(
            num_scalar_prefetch=1,
            grid=(1,),
            in_specs=[
                whole((1, rows)),
                whole((1, rows)),
                whole((rows, width)),
                whole(table.shape),
                whole(group_table.shape),
                whole((width, width)),
                whole((width,)),
                whole((width,)),
                whole((width,)),
                columns(1),
                columns(2),
                whole((width,)),
            ],
            out_specs=[whole((rows, width)), whole((rows, width)), whole((rows, 2 * width))],
        ),
        out_shape=[
            shaped((rows, width), WIDE),
            shaped((rows, width), LOW),
            shaped((rows, 2 * width), LOW),
        ],
        compiler_params=params(60 << 20),
        name="embed",
    )(
        place,
        ids,
        expression,
        prior,
        table,
        group_table,
        w_know,
        w_value,
        gain,
        offset,
        w_qkv,
        w_qkv,
        bias_v,
    )


def query_kernel(normed_ref, w_query_ref, bias_ref, out_ref):
    out_ref[...] = (dot(normed_ref[...], w_query_ref[...]) + bias_ref[...][None]).astype(LOW)


def project_queries(normed, w_qkv, bias_q):
    rows, width = normed.shape
    return pl.pallas_call(
        query_kernel,
        grid=(1,),
        in_specs=[whole((rows, width)), whole((width, width)), whole((width,))],
        out_specs=whole((rows, width)),
        out_shape=shaped((rows, width), LOW),
        compiler_params=params(),
        cost_estimate=pl.CostEstimate(
            flops=2 * rows * width * width, bytes_accessed=4 * rows * width, transcendentals=0
        ),
        name="queries",
    )(normed, w_qkv, bias_q)


def attend_kernel(place_ref, q_ref, ko_ref, vo_ref, kr_ref, vr_ref, out_ref, p_ref, c_ref):
    rows = q_ref.shape[0]
    lane = lax.broadcasted_iota(jnp.int32, (rows, 128), 1)
    place = lax.broadcasted_iota(jnp.int32, (rows, 128), 0)
    queries = q_ref[...] * LOW(HEAD_DIM**-0.5)
    halves = []
    for index, k_ref in enumerate((ko_ref, kr_ref)):
        dead = jnp.where(place < place_ref[1 + index], 0.0, -1e30).astype(LOW)
        halves.append((k_ref[...], dead))
    values = [vo_ref[...].T, vr_ref[...].T]
    outs = []
    for head in range(2):
        inside = (lane < HEAD_DIM) if head == 0 else (lane >= HEAD_DIM)
        spare = HEAD_DIM * (1 - head)
        asked = jnp.where(inside, queries, jnp.where(lane == spare, 1.0, 0.0).astype(LOW))
        scores = [dot(jnp.where(lane == spare, dead, keys), asked, 1, 1) for keys, dead in halves]
        top = jnp.maximum(*[jnp.max(part, 0, keepdims=True) for part in scores])
        mass, mixed = 0.0, 0.0
        for index in range(2):
            probs = jnp.exp(scores[index] - top)
            mass = mass + column_sums(probs)
            low = probs.astype(LOW)
            p_ref[head, index * rows : (index + 1) * rows, :] = low
            mixed = mixed + dot(values[index][head * HEAD_DIM : (head + 1) * HEAD_DIM], low)
        inverse = 1.0 / mass
        c_ref[0, head : head + 1, :] = inverse
        outs.append(mixed * inverse)
    out_ref[...] = jnp.concatenate(outs, 0).T.astype(LOW)


def attend(place, queries, kv_own, kv_other):
    rows, width = queries.shape
    pairs = width // 128
    block = lambda shift: pl.BlockSpec((rows, 128), lambda j, _: (0, shift + j))
    return pl.pallas_call(
        attend_kernel,
        grid_spec=pltpu.PrefetchScalarGridSpec(
            num_scalar_prefetch=1,
            grid=(pairs,),
            in_specs=[block(0), block(0), block(pairs), block(0), block(pairs)],
            out_specs=[
                block(0),
                pl.BlockSpec((2, 2 * rows, rows), lambda j, _: (j, 0, 0)),
                pl.BlockSpec((1, 2, rows), lambda j, _: (j, 0, 0)),
            ],
        ),
        out_shape=[
            shaped((rows, width), LOW),
            shaped((2 * pairs, 2 * rows, rows), LOW),
            shaped((pairs, 2, rows), WIDE),
        ],
        compiler_params=params(),
        cost_estimate=pl.CostEstimate(
            flops=16 * rows * rows * width,
            bytes_accessed=8 * rows * rows * pairs,
            transcendentals=4 * rows * rows * pairs,
        ),
        name="attend",
    )(place, queries, kv_own, kv_own, kv_other, kv_other)


def attend_back_kernel(
    q_ref,
    ko_ref,
    vo_ref,
    kr_ref,
    vr_ref,
    a_ref,
    g_ref,
    p_ref,
    c_ref,
    *rest,
):
    dq_ref, dkvo_ref, dkvr_ref = rest[-3:]
    rows = q_ref.shape[0]
    lane = lax.broadcasted_iota(jnp.int32, (rows, 128), 1)
    mixed = a_ref[...].astype(WIDE).T
    grad = g_ref[...].astype(WIDE).T
    grad = jnp.concatenate(
        [grad[:HEAD_DIM] * c_ref[0, :1, :], grad[HEAD_DIM:] * c_ref[0, 1:, :]], 0
    )
    inner = grad * mixed
    inner = [column_sums(inner[:HEAD_DIM]), column_sums(inner[HEAD_DIM:])]
    first = lax.broadcasted_iota(jnp.int32, (128, rows), 0) < HEAD_DIM
    low = grad.astype(LOW)
    masked = [
        jnp.where(first, low, jnp.zeros_like(low)),
        jnp.where(first, jnp.zeros_like(low), low),
    ]
    grad_rows = grad.T.astype(LOW)
    queries = q_ref[...]
    parts = [0.0, 0.0]
    for index, (k_ref, v_ref, out_ref) in enumerate(
        ((ko_ref, vo_ref, dkvo_ref), (kr_ref, vr_ref, dkvr_ref))
    ):
        keys = k_ref[...].T
        values = v_ref[...]
        key_grads, val_grads = [], []
        for head in range(2):
            probs = p_ref[head, index * rows : (index + 1) * rows, :]
            wide = dot(values, masked[head]) - inner[head]
            score = (probs.astype(WIDE) * wide).astype(LOW)
            val_grads.append(dot(probs, grad_rows))
            key_grads.append(dot(score, queries))
            parts[head] = parts[head] + dot(keys[head * HEAD_DIM : (head + 1) * HEAD_DIM], score)
        chosen = lane < HEAD_DIM
        out_ref[0] = (jnp.where(chosen, *key_grads) * HEAD_DIM**-0.5).astype(LOW)
        out_ref[1] = jnp.where(chosen, *val_grads).astype(LOW)
    dq_ref[...] = (jnp.concatenate(parts, 0).T * HEAD_DIM**-0.5).astype(LOW)


def attend_back(queries, kv_own, kv_other, attended, grad, probs, inverse, start, count, after):
    rows, width = queries.shape
    pairs = width // 128
    block = lambda shift: pl.BlockSpec((rows, 128), lambda j: (0, shift + j))
    near, far = block(start), block(pairs + start)
    both = pl.BlockSpec((2, rows, 128), lambda j: (0, 0, j))
    return pl.pallas_call(
        attend_back_kernel,
        grid=(count,),
        in_specs=[
            near,
            near,
            far,
            near,
            far,
            near,
            near,
            pl.BlockSpec((2, 2 * rows, rows), lambda j: (start + j, 0, 0)),
            pl.BlockSpec((1, 2, rows), lambda j: (start + j, 0, 0)),
        ]
        + [pl.BlockSpec(memory_space=pl.ANY)] * len(after),
        out_specs=[block(0), both, both],
        out_shape=[
            shaped((rows, 128 * count), LOW),
            shaped((2, rows, 128 * count), LOW),
            shaped((2, rows, 128 * count), LOW),
        ],
        compiler_params=params(),
        cost_estimate=LONG,
        name="attend_back",
    )(queries, kv_own, kv_own, kv_other, kv_other, attended, grad, probs, inverse, *after)


def ffn_kernel(
    place_ref,
    attended_ref,
    embedded_ref,
    cotangent_ref,
    w_out_ref,
    bias_out_ref,
    gain_ref,
    offset_ref,
    w_up_ref,
    bias_up_ref,
    w_down_ref,
    bias_down_ref,
    output_ref,
    g_residual_ref,
    g_attended_ref,
    up_send_ref,
    up_keep_ref,
    down_send_ref,
    down_keep_ref,
    out_send_ref,
    out_keep_ref,
    vectors_ref,
    bias_up_grad_ref,
    residual_ref,
    normed_ref,
    turned_ref,
    total_ref,
    g_normed_ref,
    g_out_ref,
):
    step, steps = pl.program_id(0), pl.num_programs(0)
    rows, width = attended_ref.shape
    tile = w_up_ref.shape[1]
    mine = place_ref[0]
    own, other = half_of(mine, width // 2), half_of(1 - mine, width // 2)
    alive = lax.broadcasted_iota(jnp.int32, (rows, 1), 0) < place_ref[1]

    @pl.when(step == 0)
    def _():
        residual = embedded_ref[...] + (dot(attended_ref[...], w_out_ref[...]) + bias_out_ref[...][None])
        residual_ref[...] = residual
        unit, _ = normalize(residual)
        normed = unit * gain_ref[...][None] + offset_ref[...][None]
        normed_ref[...] = normed.astype(LOW)
        turned_ref[...] = normed.T.astype(LOW)
        g_out_ref[...] = jnp.where(alive, cotangent_ref[...].astype(WIDE), 0.0).astype(LOW)
        total_ref[...] = jnp.zeros_like(total_ref)
        g_normed_ref[...] = jnp.zeros_like(g_normed_ref)

    g_out = g_out_ref[...]
    hidden = dot(normed_ref[...], w_up_ref[...]) + bias_up_ref[...]
    g_act = dot(g_out, w_down_ref[...], 1, 1)
    share = 0.5 * (1.0 + lax.erf(hidden * 0.5**0.5))
    density = jnp.exp(-0.5 * hidden * hidden) * 0.3989422804014327
    activated = (hidden * share).astype(LOW)
    g_wide = g_act * (share + hidden * density)
    g_hidden = g_wide.astype(LOW)
    total_ref[...] += dot(activated, w_down_ref[...])
    g_normed_ref[...] += dot(g_hidden, w_up_ref[...], 1, 1)
    down_send_ref[...] = dot(activated, g_out_ref[:, other], 0, 0).astype(LOW)
    down_keep_ref[...] = dot(activated, g_out_ref[:, own], 0, 0).astype(LOW)
    up = dot(turned_ref[...], g_hidden).astype(LOW)
    bias_up_grad_ref[...] = column_sums(g_hidden.astype(WIDE))
    columns = pl.ds(pl.multiple_of(lax.rem(step, steps // 2) * tile, 128), tile)

    @pl.when(step < steps // 2)
    def _():
        up_send_ref[:, columns] = up

    @pl.when(step >= steps // 2)
    def _():
        up_keep_ref[:, columns] = up

    @pl.when(step == steps - 1)
    def _():
        residual = residual_ref[...]
        final = residual + (total_ref[...] + bias_down_ref[...][None])
        output_ref[...] = jnp.where(alive, final, 0.0).astype(LOW)
        unit, scale = normalize(residual)
        g_final = g_out_ref[...].astype(WIDE)
        g_normed = g_normed_ref[...]
        g_residual = g_final + norm_back(g_normed, unit, scale, gain_ref[...][None])
        g_residual_ref[...] = g_residual
        g_branch = g_residual.astype(LOW)
        g_attended_ref[...] = dot(g_branch, w_out_ref[...], 1, 1).astype(LOW)
        vectors_ref[...] = jnp.concatenate(
            [
                column_sums(g_branch.astype(WIDE)),
                column_sums(g_normed * unit),
                column_sums(g_normed),
                column_sums(g_final),
            ],
            0,
        )
        normed_ref[...] = g_branch
        attended = attended_ref[...].astype(WIDE).T.astype(LOW)
        out_send_ref[...] = dot(attended, normed_ref[:, other]).astype(LOW)
        out_keep_ref[...] = dot(attended, normed_ref[:, own]).astype(LOW)


def feed_forward(
    place,
    attended,
    embedded,
    cotangent,
    w_out,
    bias_out,
    gain,
    offset,
    w_up,
    bias_up,
    w_down,
    bias_down,
):
    rows, width = attended.shape
    units = w_up.shape[1]
    tile = 768
    steps = units // tile
    turn = lambda j, place: lax.rem(j + (1 - place[0]) * (steps // 2), steps)
    down_tile = pl.BlockSpec((tile, width // 2), lambda j, place: (turn(j, place), 0))
    return pl.pallas_call(
        ffn_kernel,
        grid_spec=pltpu.PrefetchScalarGridSpec(
            num_scalar_prefetch=1,
            grid=(steps,),
            in_specs=[
                whole((rows, width)),
                whole((rows, width)),
                whole((rows, width)),
                whole((width, width)),
                whole((width,)),
                whole((width,)),
                whole((width,)),
                pl.BlockSpec((width, tile), lambda j, place: (0, turn(j, place))),
                pl.BlockSpec((1, tile), lambda j, place: (0, turn(j, place))),
                pl.BlockSpec((tile, width), lambda j, place: (turn(j, place), 0)),
                whole((width,)),
            ],
            out_specs=[
                whole((rows, width)),
                whole((rows, width)),
                whole((rows, width)),
                whole((width, units // 2)),
                whole((width, units // 2)),
                down_tile,
                down_tile,
                whole((width, width // 2)),
                whole((width, width // 2)),
                whole((4, width)),
                pl.BlockSpec((1, tile), lambda j, place: (0, turn(j, place))),
            ],
            scratch_shapes=[
                pltpu.VMEM((rows, width), WIDE),
                pltpu.VMEM((rows, width), LOW),
                pltpu.VMEM((width, rows), LOW),
                pltpu.VMEM((rows, width), WIDE),
                pltpu.VMEM((rows, width), WIDE),
                pltpu.VMEM((rows, width), LOW),
            ],
        ),
        out_shape=[
            shaped((rows, width), LOW),
            shaped((rows, width), WIDE),
            shaped((rows, width), LOW),
            shaped((width, units // 2), LOW),
            shaped((width, units // 2), LOW),
            shaped((units, width // 2), LOW),
            shaped((units, width // 2), LOW),
            shaped((width, width // 2), LOW),
            shaped((width, width // 2), LOW),
            shaped((4, width), WIDE),
            shaped((1, units), WIDE),
        ],
        compiler_params=params(),
        cost_estimate=pl.CostEstimate(
            flops=12 * rows * width * units + 6 * rows * width * width,
            bytes_accessed=8 * width * units,
            transcendentals=2 * rows * units,
        ),
        name="feed_forward",
    )(
        place,
        attended,
        embedded,
        cotangent,
        w_out,
        bias_out,
        gain,
        offset,
        w_up,
        bias_up,
        w_down,
        bias_down,
    )


def project_back(place_ref, normed_turned, dq_ref, own_ref, got_ref, weights, joined_ref, send_ref, keep_ref, bias_ref):
    group = dq_ref.shape[1]
    half = 3 * group // 2
    mine = place_ref[0]
    joined_ref[:, :group] = dq_ref[...]
    for index in range(2):
        total = own_ref[index].astype(WIDE) + got_ref[index].astype(WIDE)
        joined_ref[:, (1 + index) * group : (2 + index) * group] = total.astype(LOW)
    send_ref[:, :half] = dot(normed_turned, joined_ref[:, half_of(1 - mine, half)]).astype(LOW)
    keep_ref[:, :half] = dot(normed_turned, joined_ref[:, half_of(mine, half)]).astype(LOW)
    bias_ref[0:1] = column_sums(joined_ref[:, :group].astype(WIDE))
    bias_ref[1:2] = column_sums(joined_ref[:, 2 * group :].astype(WIDE))
    back = 0.0
    for index, weight_ref in enumerate(weights):
        part = joined_ref[:, index * group : (index + 1) * group]
        back = back + dot(part, weight_ref[...], 1, 1)
    return back


def first_back_kernel(
    place_ref,
    normed_ref,
    dq_ref,
    own_ref,
    got_ref,
    wq_ref,
    wk_ref,
    wv_ref,
    after_ref,
    send_ref,
    keep_ref,
    bias_ref,
    part_ref,
    turned_ref,
    joined_ref,
):
    @pl.when(pl.program_id(0) == 0)
    def _():
        turned_ref[...] = normed_ref[...].astype(WIDE).T.astype(LOW)
        part_ref[...] = jnp.zeros_like(part_ref)

    part_ref[...] += project_back(
        place_ref,
        turned_ref[...],
        dq_ref,
        own_ref,
        got_ref,
        (wq_ref, wk_ref, wv_ref),
        joined_ref,
        send_ref,
        keep_ref,
        bias_ref,
    )


def last_back_kernel(
    groups,
    place_ref,
    normed_ref,
    dq_ref,
    own_ref,
    got_ref,
    wq_ref,
    wk_ref,
    wv_ref,
    part_ref,
    embedded_ref,
    g_residual_ref,
    gain_ref,
    prior_ref,
    expression_ref,
    bias_first_ref,
    vectors_ref,
    bias_up_ref,
    send_ref,
    keep_ref,
    g_low_ref,
    small_send_ref,
    small_keep_ref,
    turned_ref,
    joined_ref,
    bias_ref,
    rows_ref,
    owned_ref,
):
    rows, width = normed_ref.shape
    half = width // 2
    mine = place_ref[0]
    turned_ref[...] = normed_ref[...].astype(WIDE).T.astype(LOW)
    back = part_ref[...] + project_back(
        place_ref,
        turned_ref[...],
        dq_ref,
        own_ref,
        got_ref,
        (wq_ref, wk_ref, wv_ref),
        joined_ref,
        send_ref,
        keep_ref,
        bias_ref,
    )
    unit, scale = normalize(embedded_ref[...])
    g_embedded = g_residual_ref[...] + norm_back(back, unit, scale, gain_ref[...][None])
    g_low_ref[...] = g_embedded.astype(LOW)
    prior = prior_ref[...].astype(WIDE).T.astype(LOW)
    send_ref[:, half:] = dot(prior, g_low_ref[:, half_of(1 - mine, half)]).astype(LOW)
    keep_ref[:, half:] = dot(prior, g_low_ref[:, half_of(mine, half)]).astype(LOW)
    expression = jnp.broadcast_to(expression_ref[...], (8, rows)).T[:, :1]
    total = column_sums(g_embedded)
    hot = lax.broadcasted_iota(jnp.int32, (groups, width), 0) == place_ref[3]
    rows_ref[:groups] = jnp.where(hot, total, 0.0)
    rows_ref[groups : groups + 16] = jnp.concatenate(
        [
            column_sums(expression * g_embedded),
            column_sums(back * unit),
            column_sums(back),
            jnp.concatenate([bias_first_ref[0, 0:1], bias_first_ref[1, 0:1], bias_ref[0:1]], 1),
            jnp.concatenate([bias_first_ref[0, 1:2], bias_first_ref[1, 1:2], bias_ref[1:2]], 1),
            vectors_ref[...],
            jnp.zeros((7, width), WIDE),
        ],
        0,
    )
    count = owned_ref.shape[0]
    share = width // count
    owned_ref[...] = jnp.zeros_like(owned_ref)
    for owner in range(count):
        columns = slice(owner * share, (owner + 1) * share)
        for start in range(0, groups + 16, 32):
            size = min(32, groups + 16 - start)
            lanes = slice(start * 4, start * 4 + share)
            owned_ref[owner, :size, lanes] = rows_ref[start : start + size, columns]
        at, lanes = groups % 32 + 9, slice(groups // 32 * 128, groups // 32 * 128 + share)
        for part in range(4):
            first = (owner * 4 + part) * share
            owned_ref[owner, at + part : at + part + 1, lanes] = bias_up_ref[
                :, first : first + share
            ]
    small_send_ref[...] = owned_ref[:, pl.ds(pl.multiple_of((1 - mine) * 16, 16), 16), :].astype(LOW)
    small_keep_ref[...] = owned_ref[:, pl.ds(pl.multiple_of(mine * 16, 16), 16), :].astype(LOW)


def back_specs(rows, width, group, first):
    third = width // group
    weight = lambda part: pl.BlockSpec((width, group), lambda j, _: (0, part * third + first + j))
    both = pl.BlockSpec((2, rows, group), lambda j, _: (0, 0, j))
    return [
        whole((rows, width)),
        pl.BlockSpec((rows, group), lambda j, _: (0, j)),
        both,
        both,
        weight(0),
        weight(1),
        weight(2),
    ]


def first_back(place, normed, dq, own, got, w_qkv, group, after):
    rows, width = normed.shape
    count = dq.shape[1] // group
    half = 3 * group // 2
    tile = pl.BlockSpec((width, half), lambda j, _: (0, j))
    return pl.pallas_call(
        first_back_kernel,
        grid_spec=pltpu.PrefetchScalarGridSpec(
            num_scalar_prefetch=1,
            grid=(count,),
            in_specs=back_specs(rows, width, group, 0) + [pl.BlockSpec(memory_space=pl.ANY)],
            out_specs=[
                tile,
                tile,
                pl.BlockSpec((None, 2, group), lambda j, _: (j, 0, 0)),
                whole((rows, width)),
            ],
            scratch_shapes=[
                pltpu.VMEM((width, rows), LOW),
                pltpu.VMEM((rows, 3 * group), LOW),
            ],
        ),
        out_shape=[
            shaped((width, count * half), LOW),
            shaped((width, count * half), LOW),
            shaped((count, 2, group), WIDE),
            shaped((rows, width), WIDE),
        ],
        compiler_params=params(),
        cost_estimate=LONG,
        name="first_back",
    )(place, normed, dq, own, got, w_qkv, w_qkv, w_qkv, after)


def last_back(
    place,
    normed,
    dq,
    own,
    got,
    w_qkv,
    group,
    part,
    embedded,
    g_residual,
    gain,
    prior,
    expression,
    bias_first,
    vectors,
    bias_up,
    groups,
    count,
):
    rows, width = normed.shape
    half = width // 2
    first = width // group - 1
    return pl.pallas_call(
        functools.partial(last_back_kernel, groups),
        grid_spec=pltpu.PrefetchScalarGridSpec(
            num_scalar_prefetch=1,
            grid=(1,),
            in_specs=back_specs(rows, width, group, first)
            + [
                whole((rows, width)),
                whole((rows, width)),
                whole((rows, width)),
                whole((width,)),
                whole((rows, width)),
                whole((1, rows)),
                whole(bias_first.shape),
                whole((4, width)),
                whole(bias_up.shape),
            ],
            out_specs=[
                whole((width, width)),
                whole((width, width)),
                whole((rows, width)),
                whole((count, 16, 384)),
                whole((count, 16, 384)),
            ],
            scratch_shapes=[
                pltpu.VMEM((width, rows), LOW),
                pltpu.VMEM((rows, 3 * group), LOW),
                pltpu.VMEM((2, group), WIDE),
                pltpu.VMEM((groups + 16, width), WIDE),
                pltpu.VMEM((count, 32, 384), WIDE),
            ],
        ),
        out_shape=[
            shaped((width, width), LOW),
            shaped((width, width), LOW),
            shaped((rows, width), LOW),
            shaped((count, 16, 384), LOW),
            shaped((count, 16, 384), LOW),
        ],
        compiler_params=params(),
        cost_estimate=LONG,
        name="last_back",
    )(
        place,
        normed,
        dq,
        own,
        got,
        w_qkv,
        w_qkv,
        w_qkv,
        part,
        embedded,
        g_residual,
        gain,
        prior,
        expression,
        bias_first,
        vectors,
        bias_up,
    )


def gene_kernel(slots_ref, ids_ref, grad_ref, after_ref, out_ref):
    slots = slots_ref[...]
    rows = grad_ref.shape[0]
    picker = jnp.where(slots == jnp.broadcast_to(ids_ref[...], (slots.shape[0], rows)), 1.0, 0.0)
    out_ref[...] = dot(picker.astype(LOW), grad_ref[...]).astype(LOW)


def gene_rows(slots, ids, grad, after):
    count = slots.shape[0]
    rows, width = grad.shape
    tile = min(count, 1152)
    return pl.pallas_call(
        gene_kernel,
        grid=(count // tile,),
        in_specs=[
            pl.BlockSpec((tile, 1), lambda j: (j, 0)),
            whole((1, rows)),
            whole((rows, width)),
            pl.BlockSpec(memory_space=pl.ANY),
        ],
        out_specs=pl.BlockSpec((tile, width), lambda j: (j, 0)),
        out_shape=shaped((count, width), LOW),
        compiler_params=params(),
        cost_estimate=LONG,
        name="gene_rows",
    )(slots, ids, grad, after)


def swap_cores(array):
    return lax.ppermute(array, "blk", [(0, 1), (1, 0)])


def bits_apart(array, mask):
    count = lax.axis_size("dp")
    return lax.ppermute(array, "dp", [(i, i ^ mask) for i in range(count)])


def pick(array, position, index):
    return lax.dynamic_index_in_dim(array, index, position, keepdims=False)


LANES = 384


def up16(rows):
    return -(-rows // 16) * 16


class Share:
    QUAD = "quad"

    def __init__(self, segments, route):
        self.bits = lax.axis_size("dp").bit_length() - 1
        self.route = list(route)
        self.rows = [arrays[0].shape[1] for arrays, _ in segments]
        self.settle()
        dims = tuple(range(self.bits - 1, -1, -1))
        self.sources = [
            (array.reshape((2,) * self.bits + array.shape[1:]), dims, block, [(index, 0)])
            for index, (arrays, block) in enumerate(segments)
            for array in arrays
        ]
        self.fixed = ()

    def join(self, other):
        shift = len(self.rows)
        self.rows = self.rows + other.rows
        self.sources += [
            (array, dims, block, [(index + shift, start) for index, start in parts])
            for array, dims, block, parts in other.sources
        ]
        self.settle()
        return self

    def settle(self):
        self.places, place = [], 0
        for rows in self.rows:
            self.places.append(place)
            place += up16(rows)
        self.height = self.places[-1] + self.rows[-1]

    def targets(self):
        step = self.route[0] if self.route else None
        if step is None:
            return [{}]
        if step == self.QUAD:
            low, high = self.bits - 2, self.bits - 1
            return [{low: way & 1, high: way >> 1} for way in (1, 2, 3)]
        return [{step: 1}]

    def left(self, target):
        return [bit for bit in range(self.bits - 1, -1, -1) if bit not in self.fixed + tuple(target)]

    def receive(self, targets, sent):
        if self.route:
            self.route.pop(0)
        for target, array in zip(targets, sent):
            mask = sum(flip << bit for bit, flip in target.items())
            dims = tuple(self.left(target))
            parts = list(enumerate(self.places))
            self.sources.append((bits_apart(array, mask), dims, 0, parts))
        self.fixed += tuple(targets[0])


def combine(place, shares, after, last=None):
    operands, specs, plan, out_specs, out_shape = [], [], [], [], []
    steps = []
    for share in shares:
        targets = share.targets()
        steps.append(targets)
        for target in targets:
            left = share.left(target) if last is None else []
            used = []
            for array, dims, block, parts in share.sources:
                shape, where = [], []
                for bit in dims:
                    free = bit in left
                    shape.append(2 if free else None)
                    where.append(None if free else (bit, target.get(bit, 0)))

                def index(_, place, where=tuple(where), block=block):
                    lead = tuple(
                        0 if at is None else (1 - place[4 + at[0]] if at[1] else place[4 + at[0]])
                        for at in where
                    )
                    return lead + (0, block)

                specs.append(pl.BlockSpec(tuple(shape) + (array.shape[-2], LANES), index))
                used.append((len(operands), parts))
                operands.append(array)
            plan.append((share.rows, share.places, used))
            if last is None:
                shape = (2,) * len(left) + (share.height, LANES)
                out_specs.append(whole(shape))
                out_shape.append(shaped(shape, LOW))
    if last is not None:
        for shape, _ in last:
            out_specs.append(whole(shape))
            out_shape.append(shaped(shape, WIDE))
    count = len(operands)

    def kernel(*refs):
        sources, outs = refs[1 : 1 + count], refs[1 + count + len(after) :]

        def summed(item, segment):
            rows, _, used = plan[item]
            total = None
            for operand, parts in used:
                for index, start in parts:
                    if index == segment:
                        part = sources[operand][..., start : start + rows[segment], :].astype(WIDE)
                        total = part if total is None else total + part
            return total

        if last is None:
            for item, out in enumerate(outs):
                for segment, start in enumerate(plan[item][1]):
                    out[..., start : start + plan[item][0][segment], :] = summed(
                        item, segment
                    ).astype(LOW)
        else:
            for (_, pieces), out in zip(last, outs):
                for item, segment, row, column in pieces:
                    value = summed(item, segment)
                    out[row : row + value.shape[0], column : column + LANES] = value

    outs = pl.pallas_call(
        kernel,
        grid_spec=pltpu.PrefetchScalarGridSpec(
            num_scalar_prefetch=1,
            grid=(1,),
            in_specs=specs + [pl.BlockSpec(memory_space=pl.ANY)] * len(after),
            out_specs=out_specs,
        ),
        out_shape=out_shape,
        compiler_params=params(),
        cost_estimate=LONG,
        name="combine",
    )(place, *operands, *after)
    if last is not None:
        return outs
    taken = 0
    for share, targets in zip(shares, steps):
        share.receive(targets, outs[taken : taken + len(targets)])
        taken += len(targets)
    return outs


def assemble(place, own, other, shapes, pieces, small_row=None):
    def kernel(place_ref, own_ref, other_ref, *outs):
        first = place_ref[0] == 0

        def of_core(core, rows, columns):
            return jnp.where(first == (core == 0), own_ref[rows, columns], other_ref[rows, columns])

        for core, row, rows, column, columns, target, out_column in pieces:
            value = of_core(core, slice(row, row + rows), slice(column, column + columns))
            outs[target][:, out_column : out_column + columns] = value
        if small_row is None:
            return
        group_ref, vector_refs, long_ref = outs[2], outs[3:-1], outs[-1]
        groups, share = group_ref.shape
        rows = slice(small_row, small_row + 16)
        for start in range(0, groups, 16):
            lanes = slice(start // 32 * 128, start // 32 * 128 + share)
            group_ref[start : start + 16] = of_core(start // 16 % 2, rows, lanes)
        rest = of_core(0, rows, slice(groups // 32 * 128, groups // 32 * 128 + 128))
        for index, ref in enumerate(vector_refs):
            ref[...] = rest[index, :share]
        long_ref[...] = jnp.concatenate(
            [rest[9 + part : 10 + part, :share] for part in range(4)], 1
        )[0]

    return pl.pallas_call(
        kernel,
        grid_spec=pltpu.PrefetchScalarGridSpec(
            num_scalar_prefetch=1,
            grid=(1,),
            in_specs=[whole(own.shape), whole(own.shape)],
            out_specs=[whole(shape) for shape in shapes],
        ),
        out_shape=[shaped(shape, WIDE) for shape in shapes],
        compiler_params=params(),
        cost_estimate=LONG,
        name="assemble",
    )(place, own, other)


def body(
    gene_ids,
    values,
    knowledge,
    lengths,
    groups,
    gene_table,
    group_table,
    w_know,
    w_value,
    norm1_gain,
    norm1_bias,
    w_qkv,
    bias_q,
    bias_v,
    w_out,
    bias_out,
    norm2_gain,
    norm2_bias,
    w_up,
    bias_up,
    w_down,
    bias_down,
    cotangent,
):
    width = w_out.shape[0]
    units = w_up.shape[1]
    rows = gene_ids.shape[1]
    count = lax.axis_size("dp")
    mine = lax.axis_index("blk")
    length, group = lengths[0], groups[0]
    prior = knowledge[0]
    row = lambda vector: vector.reshape(1, -1)
    me = lax.axis_index("dp")
    bits = count.bit_length() - 1
    place = jnp.stack(
        [mine, length - mine * rows, length - (1 - mine) * rows, group]
        + [(me >> bit) & 1 for bit in range(bits)]
    ).astype(jnp.int32)
    if gene_table.shape[0] > 8 * rows:
        table = gene_table[gene_ids[0]]
    else:
        table = gene_table
    embedded, normed, kv_own = embed(
        place,
        gene_ids,
        values,
        prior,
        table,
        group_table,
        w_know,
        w_value,
        norm1_gain,
        norm1_bias,
        w_qkv,
        bias_v,
    )
    kv_other = swap_cores(kv_own)
    queries = project_queries(normed, w_qkv, bias_q)
    attended, probs, inverse = attend(place, queries, kv_own, kv_other)
    (
        block_output,
        g_residual,
        g_attended,
        up_send,
        up_keep,
        down_send,
        down_keep,
        out_send,
        out_keep,
        vectors,
        bias_up_grad,
    ) = feed_forward(
        place,
        attended,
        embedded,
        cotangent[0],
        w_out,
        bias_out,
        norm2_gain,
        norm2_bias,
        w_up,
        row(bias_up),
        w_down,
        bias_down,
    )

    owners = lambda array: array.reshape(count, -1, array.shape[-1])
    low_bits = list(range(bits - 2))
    turned = low_bits[1::-1] + low_bits[2:]
    quad = [Share.QUAD]
    up_terms = [owners(up_keep), owners(swap_cores(up_send))]
    blocks = units // 2 // LANES
    out_terms = [owners(out_keep), owners(swap_cores(out_send))]
    down_terms = [owners(down_keep), owners(swap_cores(down_send))]
    early = [
        Share([(down_terms, 0), (out_terms, 0)], low_bits + quad),
        Share([(up_terms, block) for block in range(blocks)], turned + quad),
    ]
    dq1, own1, other1 = attend_back(
        queries, kv_own, kv_other, attended, g_attended, probs, inverse, 0, 4, []
    )
    got1 = swap_cores(other1)
    sent = combine(place, early, [dq1])
    dq2, own2, other2 = attend_back(
        queries, kv_own, kv_other, attended, g_attended, probs, inverse, 4, 2, sent
    )
    got2 = swap_cores(other2)
    qkv_send, qkv_keep, bias_first, part = first_back(
        place, normed, dq1, own1, got1, w_qkv, 256, dq2
    )
    tail_send, tail_keep, g_low, small_send, small_keep = last_back(
        place,
        normed,
        dq2,
        own2,
        got2,
        w_qkv,
        256,
        part,
        embedded,
        g_residual,
        norm1_gain,
        prior,
        values,
        bias_first,
        vectors,
        bias_up_grad,
        group_table.shape[0],
        count,
    )
    slot = jnp.arange(count * VOC_DEV, dtype=jnp.int32)[:, None]
    slot = slot + slot // VOC_DEV * VOC_DEV
    qkv = [owners(qkv_keep), owners(swap_cores(qkv_send))]
    gene_send = gene_rows(slot + (1 - mine) * VOC_DEV, gene_ids, g_low, qkv[1])
    gene_got = swap_cores(gene_send)
    gene_keep = gene_rows(slot + mine * VOC_DEV, gene_ids, g_low, gene_send)
    share = width // count
    small = [small_keep, swap_cores(small_send)]
    tail = [owners(tail_keep), owners(swap_cores(tail_send))]
    gene = [owners(gene_keep), owners(gene_got)]
    late = [
        Share([(qkv, 0), (qkv, 1), (gene, 0)], low_bits + quad),
        Share([(tail, 0), (tail, 1), (small, 0), (gene, 1)], turned + quad),
    ]
    token = [gene_keep]
    for _ in low_bits[1:]:
        token = combine(place, early, token)
    early = [early[0].join(early[1])]
    token = combine(place, late, token)
    token = combine(place, early, token)
    for _ in low_bits[1:]:
        token = combine(place, late, token)
    late = [late[0].join(late[1])]
    step = up16(share)
    high = units // count
    layout = [(0, 0, 0, 0), (0, 1, high + blocks * step, 0)]
    layout += [(0, 2 + block, high + block * step, 0) for block in range(blocks)]
    (own,) = combine(place, early, token, [((high + (blocks + 1) * step, LANES), layout)])
    other = swap_cores(own)
    combine(place, late, [own])
    pieces = []
    for core in range(2):
        pieces.append((core, 0, high, 0, LANES, 0, core * LANES))
        for block in range(blocks):
            place_in = (core * blocks + block) * LANES
            pieces.append((core, high + block * step, share, 0, LANES, 1, place_in))
        pieces.append((core, high + blocks * step, share, 0, LANES, 2, core * LANES))
    w_down_share, w_up_share, w_out_share = assemble(
        place, own, other, [(high, width), (share, units), (share, width)], pieces
    )
    layout = [(0, 0, 0, 0), (0, 1, step, 0)]
    layout += [(0, 3 + index, (2 + index) * step, 0) for index in range(3)]
    own, gene_grad = combine(
        place,
        late,
        [w_down_share],
        [
            ((4 * step + 16, LANES), layout),
            ((VOC_DEV, width), [(0, 2, 0, 0), (0, 6, 0, LANES)]),
        ],
    )
    other = swap_cores(own)
    pieces = []
    for block in range(3):
        at = block * step
        pieces.append((0, at, share, 0, 256, 0, block * 256))
        pieces.append((0, at, share, 256, 128, 0, width + block * 256))
        pieces.append((1, at, share, 0, 128, 0, width + block * 256 + 128))
        pieces.append((1, at, share, 128, 256, 0, 2 * width + block * 256))
    for core in range(2):
        pieces.append((core, 3 * step, share, 0, LANES, 1, core * LANES))
    w_qkv_share, w_know_share, group_share, *extra, bias_up_share = assemble(
        place,
        own,
        other,
        [(share, 3 * width), (share, width), (group_table.shape[0], share)]
        + [(share,)] * 9
        + [(units // count,)],
        pieces,
        4 * step,
    )
    return (
        block_output[None],
        gene_grad,
        group_share,
        w_know_share,
        extra[0],
        extra[1],
        extra[2],
        w_qkv_share,
        extra[3],
        extra[4],
        w_out_share,
        extra[5],
        extra[6],
        extra[7],
        w_up_share,
        bias_up_share,
        w_down_share,
        extra[8],
    )


def solution(mesh):
    in_specs = (
        P("dp", "blk"),
        P("dp", "blk"),
        P("dp", "blk", None),
        P("dp"),
        P("dp"),
        P(),
        P(),
        P(),
        P(),
        P(),
        P(),
        P(),
        P(),
        P(),
        P(),
        P(),
        P(),
        P(),
        P(),
        P(),
        P(),
        P(),
        P("dp", "blk", None),
    )
    out_specs = (
        P("dp", "blk", None),
        P(("dp", "blk"), None),
        P(None, "dp"),
        P("dp", None),
        P("dp"),
        P("dp"),
        P("dp"),
        P("dp", None),
        P("dp"),
        P("dp"),
        P("dp", None),
        P("dp"),
        P("dp"),
        P("dp"),
        P("dp", None),
        P("dp"),
        P("dp", None),
        P("dp"),
    )
    return jax.shard_map(body, mesh=mesh, in_specs=in_specs, out_specs=out_specs, check_vma=False)
```

```python
import functools

import jax
import jax.numpy as jnp
from jax import lax
from jax.experimental import pallas as pl
from jax.experimental.pallas import tpu as pltpu
from jax.sharding import PartitionSpec as P

HEAD_DIM = 64
VOC_DEV = 72
EPSILON = 1e-05
LANES = 384
LOW = jnp.bfloat16
WIDE = jnp.float32
GRANT = 44 << 20


LONG = pl.CostEstimate(flops=10**12, bytes_accessed=1, transcendentals=0)


def dot(left, right, left_dim=1, right_dim=0):
    return lax.dot_general(
        left, right, (((left_dim,), (right_dim,)), ((), ())), preferred_element_type=WIDE
    )


def column_sums(array):
    return jnp.sum(array, 0, keepdims=True)


def row_means(array):
    return jnp.mean(array, -1, keepdims=True)


def normalize(array):
    center = array - row_means(array)
    scale = lax.rsqrt(row_means(center * center) + EPSILON)
    return center * scale, scale


def norm_back(grad, unit, scale, gain):
    inner = grad * gain
    return scale * (inner - row_means(inner) - unit * row_means(inner * unit))


def half_of(index, half):
    return pl.ds(pl.multiple_of(index * half, 128), half)


def whole(shape):
    return pl.BlockSpec(shape, lambda *_: (0,) * len(shape))


def up16(rows):
    return -(-rows // 16) * 16


def unread(arrays):
    return [pl.BlockSpec(memory_space=pl.ANY)] * len(arrays)


def params(grant=GRANT):
    return pltpu.CompilerParams(vmem_limit_bytes=grant)


def shaped(shape, dtype):
    return jax.ShapeDtypeStruct(shape, dtype)


def embed_kernel(
    place_ref,
    ids_ref,
    expression_ref,
    prior_ref,
    table_ref,
    group_ref,
    w_know_ref,
    w_value_ref,
    gain_ref,
    offset_ref,
    w_key_ref,
    w_val_ref,
    bias_val_ref,
    embedded_ref,
    normed_ref,
    kv_ref,
):
    rows, width = prior_ref.shape
    embedded = dot(prior_ref[...], w_know_ref[...])
    if table_ref.shape[0] == rows:
        gathered = table_ref[...].astype(WIDE)
    else:
        ids = jnp.broadcast_to(ids_ref[...], (8, rows)).T[:, :1]
        slots = lax.broadcasted_iota(jnp.int32, (rows, table_ref.shape[0]), 1)
        picker = jnp.where(slots == ids, 1.0, 0.0).astype(LOW)
        gathered = dot(picker, table_ref[...])
    expression = jnp.broadcast_to(expression_ref[...], (8, rows)).T[:, :1]
    groups = lax.broadcasted_iota(jnp.int32, (8, group_ref.shape[0]), 1)
    group_row = dot(jnp.where(groups == place_ref[3], 1.0, 0.0).astype(LOW), group_ref[...])[:1]
    embedded = gathered + group_row + expression * w_value_ref[...][None] + embedded
    embedded_ref[...] = embedded
    unit, _ = normalize(embedded)
    normed = (unit * gain_ref[...][None] + offset_ref[...][None]).astype(LOW)
    normed_ref[...] = normed
    kv_ref[:, :width] = dot(normed, w_key_ref[...]).astype(LOW)
    kv_ref[:, width:] = (dot(normed, w_val_ref[...]) + bias_val_ref[...][None]).astype(LOW)


def embed(
    place, ids, expression, prior, table, group_table, w_know, w_value, gain, offset, w_qkv, bias_v
):
    rows, width = prior.shape
    columns = lambda index: pl.BlockSpec((width, width), lambda *_: (0, index))
    return pl.pallas_call(
        embed_kernel,
        grid_spec=pltpu.PrefetchScalarGridSpec(
            num_scalar_prefetch=1,
            grid=(1,),
            in_specs=[
                whole((1, rows)),
                whole((1, rows)),
                whole((rows, width)),
                whole(table.shape),
                whole(group_table.shape),
                whole((width, width)),
                whole((width,)),
                whole((width,)),
                whole((width,)),
                columns(1),
                columns(2),
                whole((width,)),
            ],
            out_specs=[whole((rows, width)), whole((rows, width)), whole((rows, 2 * width))],
        ),
        out_shape=[
            shaped((rows, width), WIDE),
            shaped((rows, width), LOW),
            shaped((rows, 2 * width), LOW),
        ],
        compiler_params=params(60 << 20),
        name="embed",
    )(
        place,
        ids,
        expression,
        prior,
        table,
        group_table,
        w_know,
        w_value,
        gain,
        offset,
        w_qkv,
        w_qkv,
        bias_v,
    )


def query_kernel(normed_ref, w_query_ref, bias_ref, out_ref):
    out_ref[...] = (dot(normed_ref[...], w_query_ref[...]) + bias_ref[...][None]).astype(LOW)


def project_queries(normed, w_qkv, bias_q):
    rows, width = normed.shape
    return pl.pallas_call(
        query_kernel,
        grid=(1,),
        in_specs=[whole((rows, width)), whole((width, width)), whole((width,))],
        out_specs=whole((rows, width)),
        out_shape=shaped((rows, width), LOW),
        compiler_params=params(),
        cost_estimate=pl.CostEstimate(
            flops=2 * rows * width * width, bytes_accessed=4 * rows * width, transcendentals=0
        ),
        name="queries",
    )(normed, w_qkv, bias_q)


def attend_kernel(place_ref, q_ref, ko_ref, vo_ref, kr_ref, vr_ref, out_ref, p_ref, c_ref):
    rows = q_ref.shape[0]
    lane = lax.broadcasted_iota(jnp.int32, (rows, 128), 1)
    place = lax.broadcasted_iota(jnp.int32, (rows, 128), 0)
    queries = q_ref[...] * LOW(HEAD_DIM**-0.5)
    halves = []
    for index, k_ref in enumerate((ko_ref, kr_ref)):
        dead = jnp.where(place < place_ref[1 + index], 0.0, -1e30).astype(LOW)
        halves.append((k_ref[...], dead))
    values = [vo_ref[...].T, vr_ref[...].T]
    ones = jnp.ones((16, rows), LOW)
    scored, outs = [], []
    for head in range(2):
        inside = (lane < HEAD_DIM) if head == 0 else (lane >= HEAD_DIM)
        spare = HEAD_DIM * (1 - head)
        asked = jnp.where(inside, queries, jnp.where(lane == spare, 1.0, 0.0).astype(LOW))
        scored.append(
            [dot(jnp.where(lane == spare, dead, keys), asked, 1, 1) for keys, dead in halves]
        )
    for head in range(2):
        scores = scored[head]
        top = jnp.maximum(*[jnp.max(part, 0, keepdims=True) for part in scores])
        mixed = 0.0
        for index in range(2):
            low = jnp.exp(scores[index] - top).astype(LOW)
            p_ref[head, index * rows : (index + 1) * rows, :] = low
            own = values[index][head * HEAD_DIM : (head + 1) * HEAD_DIM]
            mixed = mixed + dot(jnp.concatenate([own, ones], 0), low)
        inverse = 1.0 / mixed[HEAD_DIM : HEAD_DIM + 1]
        c_ref[0, head : head + 1, :] = inverse
        outs.append(mixed[:HEAD_DIM] * inverse)
    out_ref[...] = jnp.concatenate(outs, 0).T.astype(LOW)


def attend(place, queries, kv_own, kv_other):
    rows, width = queries.shape
    pairs = width // 128
    block = lambda shift: pl.BlockSpec((rows, 128), lambda j, _: (0, shift + j))
    return pl.pallas_call(
        attend_kernel,
        grid_spec=pltpu.PrefetchScalarGridSpec(
            num_scalar_prefetch=1,
            grid=(pairs,),
            in_specs=[block(0), block(0), block(pairs), block(0), block(pairs)],
            out_specs=[
                block(0),
                pl.BlockSpec((2, 2 * rows, rows), lambda j, _: (j, 0, 0)),
                pl.BlockSpec((1, 2, rows), lambda j, _: (j, 0, 0)),
            ],
        ),
        out_shape=[
            shaped((rows, width), LOW),
            shaped((2 * pairs, 2 * rows, rows), LOW),
            shaped((pairs, 2, rows), WIDE),
        ],
        compiler_params=params(),
        cost_estimate=pl.CostEstimate(
            flops=16 * rows * rows * width,
            bytes_accessed=8 * rows * rows * pairs,
            transcendentals=4 * rows * rows * pairs,
        ),
        name="attend",
    )(place, queries, kv_own, kv_own, kv_other, kv_other)


def attend_back_kernel(
    q_ref,
    ko_ref,
    vo_ref,
    kr_ref,
    vr_ref,
    a_ref,
    g_ref,
    p_ref,
    c_ref,
    *rest,
):
    dq_ref, dkvo_ref, dkvr_ref = rest[-3:]
    rows = q_ref.shape[0]
    lane = lax.broadcasted_iota(jnp.int32, (rows, 128), 1)
    mixed = a_ref[...].astype(WIDE).T
    grad = g_ref[...].astype(WIDE).T
    grad = jnp.concatenate(
        [grad[:HEAD_DIM] * c_ref[0, :1, :], grad[HEAD_DIM:] * c_ref[0, 1:, :]], 0
    )
    inner = grad * mixed
    inner = [column_sums(inner[:HEAD_DIM]), column_sums(inner[HEAD_DIM:])]
    first = lax.broadcasted_iota(jnp.int32, (128, rows), 0) < HEAD_DIM
    low = grad.astype(LOW)
    masked = [
        jnp.where(first, low, jnp.zeros_like(low)),
        jnp.where(first, jnp.zeros_like(low), low),
    ]
    grad_rows = grad.T.astype(LOW)
    queries = q_ref[...]
    parts = [0.0, 0.0]
    for index, (k_ref, v_ref, out_ref) in enumerate(
        ((ko_ref, vo_ref, dkvo_ref), (kr_ref, vr_ref, dkvr_ref))
    ):
        keys = k_ref[...].T
        values = v_ref[...]
        key_grads, val_grads = [], []
        for head in range(2):
            probs = p_ref[head, index * rows : (index + 1) * rows, :]
            wide = dot(values, masked[head]) - inner[head]
            score = (probs.astype(WIDE) * wide).astype(LOW)
            val_grads.append(dot(probs, grad_rows))
            key_grads.append(dot(score, queries))
            parts[head] = parts[head] + dot(keys[head * HEAD_DIM : (head + 1) * HEAD_DIM], score)
        chosen = lane < HEAD_DIM
        out_ref[0] = (jnp.where(chosen, *key_grads) * HEAD_DIM**-0.5).astype(LOW)
        out_ref[1] = jnp.where(chosen, *val_grads).astype(LOW)
    dq_ref[...] = (jnp.concatenate(parts, 0).T * HEAD_DIM**-0.5).astype(LOW)


def attend_back(queries, kv_own, kv_other, attended, grad, probs, inverse, start, count, after):
    rows, width = queries.shape
    pairs = width // 128
    block = lambda shift: pl.BlockSpec((rows, 128), lambda j: (0, shift + j))
    near, far = block(start), block(pairs + start)
    both = pl.BlockSpec((2, rows, 128), lambda j: (0, 0, j))
    return pl.pallas_call(
        attend_back_kernel,
        grid=(count,),
        in_specs=[
            near,
            near,
            far,
            near,
            far,
            near,
            near,
            pl.BlockSpec((2, 2 * rows, rows), lambda j: (start + j, 0, 0)),
            pl.BlockSpec((1, 2, rows), lambda j: (start + j, 0, 0)),
        ]
        + unread(after),
        out_specs=[block(0), both, both],
        out_shape=[
            shaped((rows, 128 * count), LOW),
            shaped((2, rows, 128 * count), LOW),
            shaped((2, rows, 128 * count), LOW),
        ],
        compiler_params=params(),
        cost_estimate=LONG,
        name="attend_back",
    )(queries, kv_own, kv_own, kv_other, kv_other, attended, grad, probs, inverse, *after)


def ffn_kernel(
    place_ref,
    attended_ref,
    embedded_ref,
    cotangent_ref,
    w_out_ref,
    bias_out_ref,
    gain_ref,
    offset_ref,
    w_up_ref,
    bias_up_ref,
    w_down_ref,
    bias_down_ref,
    output_ref,
    residual_ref,
    g_normed_ref,
    up_send_ref,
    up_keep_ref,
    down_send_ref,
    down_keep_ref,
    bias_up_grad_ref,
    normed_ref,
    turned_ref,
    total_ref,
    g_out_ref,
    g_halves_ref,
):
    step, steps = pl.program_id(0), pl.num_programs(0)
    rows, width = attended_ref.shape
    half = width // 2
    mine = place_ref[0]
    alive = lax.broadcasted_iota(jnp.int32, (rows, 1), 0) < place_ref[1]

    @pl.when(step == 0)
    def _():
        residual = embedded_ref[...] + (
            dot(attended_ref[...], w_out_ref[...]) + bias_out_ref[...][None]
        )
        residual_ref[...] = residual
        unit, _ = normalize(residual)
        normed = unit * gain_ref[...][None] + offset_ref[...][None]
        normed_ref[...] = normed.astype(LOW)
        turned_ref[...] = normed.T.astype(LOW)
        g_out_ref[...] = jnp.where(alive, cotangent_ref[...].astype(WIDE), 0.0).astype(LOW)
        g_halves_ref[:, :half] = g_out_ref[:, half_of(1 - mine, half)]
        g_halves_ref[:, half:] = g_out_ref[:, half_of(mine, half)]
        total_ref[...] = jnp.zeros_like(total_ref)
        g_normed_ref[...] = jnp.zeros_like(g_normed_ref)

    hidden = dot(normed_ref[...], w_up_ref[...]) + bias_up_ref[...]
    g_act = dot(g_out_ref[...], w_down_ref[...], 1, 1)
    share = 0.5 * (1.0 + lax.erf(hidden * 0.5**0.5))
    density = jnp.exp(-0.5 * hidden * hidden) * 0.3989422804014327
    activated = (hidden * share).astype(LOW)
    g_hidden = (g_act * (share + hidden * density)).astype(LOW)
    total_ref[...] += dot(activated, w_down_ref[...])
    g_normed_ref[...] += dot(g_hidden, w_up_ref[...], 1, 1)
    down = dot(activated, g_halves_ref[...], 0, 0).astype(LOW)
    down_send_ref[...] = down[:, :half]
    down_keep_ref[...] = down[:, half:]
    up = dot(turned_ref[...], g_hidden).astype(LOW)
    bias_up_grad_ref[...] = column_sums(g_hidden.astype(WIDE))

    @pl.when(step < steps // 2)
    def _():
        up_send_ref[...] = up

    @pl.when(step >= steps // 2)
    def _():
        up_keep_ref[...] = up

    @pl.when(step == steps - 1)
    def _():
        final = residual_ref[...] + (total_ref[...] + bias_down_ref[...][None])
        output_ref[...] = jnp.where(alive, final, 0.0).astype(LOW)


def feed_forward(
    place,
    attended,
    embedded,
    cotangent,
    w_out,
    bias_out,
    gain,
    offset,
    w_up,
    bias_up,
    w_down,
    bias_down,
):
    rows, width = attended.shape
    units = w_up.shape[1]
    tile = 768
    steps = units // tile
    turn = lambda j, place: lax.rem(j + (1 - place[0]) * (steps // 2), steps)
    down_tile = pl.BlockSpec((tile, width // 2), lambda j, place: (turn(j, place), 0))
    return pl.pallas_call(
        ffn_kernel,
        grid_spec=pltpu.PrefetchScalarGridSpec(
            num_scalar_prefetch=1,
            grid=(steps,),
            in_specs=[
                whole((rows, width)),
                whole((rows, width)),
                whole((rows, width)),
                whole((width, width)),
                whole((width,)),
                whole((width,)),
                whole((width,)),
                pl.BlockSpec((width, tile), lambda j, place: (0, turn(j, place))),
                pl.BlockSpec((1, tile), lambda j, place: (0, turn(j, place))),
                pl.BlockSpec((tile, width), lambda j, place: (turn(j, place), 0)),
                whole((width,)),
            ],
            out_specs=[
                whole((rows, width)),
                whole((rows, width)),
                whole((rows, width)),
                pl.BlockSpec((width, tile), lambda j, _: (0, jnp.minimum(j, steps // 2 - 1))),
                pl.BlockSpec((width, tile), lambda j, _: (0, jnp.maximum(j - steps // 2, 0))),
                down_tile,
                down_tile,
                pl.BlockSpec((1, tile), lambda j, place: (0, turn(j, place))),
            ],
            scratch_shapes=[
                pltpu.VMEM((rows, width), LOW),
                pltpu.VMEM((width, rows), LOW),
                pltpu.VMEM((rows, width), WIDE),
                pltpu.VMEM((rows, width), LOW),
                pltpu.VMEM((rows, width), LOW),
            ],
        ),
        out_shape=[
            shaped((rows, width), LOW),
            shaped((rows, width), WIDE),
            shaped((rows, width), WIDE),
            shaped((width, units // 2), LOW),
            shaped((width, units // 2), LOW),
            shaped((units, width // 2), LOW),
            shaped((units, width // 2), LOW),
            shaped((1, units), WIDE),
        ],
        compiler_params=params(),
        cost_estimate=LONG,
        name="feed_forward",
    )(
        place,
        attended,
        embedded,
        cotangent,
        w_out,
        bias_out,
        gain,
        offset,
        w_up,
        bias_up,
        w_down,
        bias_down,
    )


def branch_kernel(
    place_ref,
    residual_ref,
    g_normed_ref,
    cotangent_ref,
    attended_ref,
    w_out_ref,
    gain_ref,
    *rest,
):
    g_residual_ref, g_attended_ref, out_send_ref, out_keep_ref, vectors_ref, total_ref = rest[-6:]
    step, steps = pl.program_id(0), pl.num_programs(0)
    rows, width = residual_ref.shape
    half = width // 2
    mine = place_ref[0]
    alive = step * rows + lax.broadcasted_iota(jnp.int32, (rows, 1), 0) < place_ref[1]

    @pl.when(step == 0)
    def _():
        total_ref[...] = jnp.zeros_like(total_ref)
        vectors_ref[...] = jnp.zeros_like(vectors_ref)

    unit, scale = normalize(residual_ref[...])
    g_final = jnp.where(alive, cotangent_ref[...].astype(WIDE), 0.0)
    g_normed = g_normed_ref[...]
    g_residual = g_final + norm_back(g_normed, unit, scale, gain_ref[...][None])
    g_residual_ref[...] = g_residual
    g_branch = g_residual.astype(LOW)
    g_attended_ref[...] = dot(g_branch, w_out_ref[...], 1, 1).astype(LOW)
    total_ref[...] += dot(attended_ref[...], g_branch, 0, 0)
    vectors_ref[...] += jnp.concatenate(
        [
            column_sums(g_branch.astype(WIDE)),
            column_sums(g_normed * unit),
            column_sums(g_normed),
            column_sums(g_final),
        ],
        0,
    )

    @pl.when(step == steps - 1)
    def _():
        out_send_ref[...] = total_ref[:, half_of(1 - mine, half)].astype(LOW)
        out_keep_ref[...] = total_ref[:, half_of(mine, half)].astype(LOW)


def branch_back(place, residual, g_normed, cotangent, attended, w_out, gain, after):
    rows, width = residual.shape
    steps = 2
    tile = pl.BlockSpec((rows // steps, width), lambda j, _: (j, 0))
    return pl.pallas_call(
        branch_kernel,
        grid_spec=pltpu.PrefetchScalarGridSpec(
            num_scalar_prefetch=1,
            grid=(steps,),
            in_specs=[tile, tile, tile, tile, whole((width, width)), whole((width,))]
            + unread(after),
            out_specs=[
                tile,
                tile,
                whole((width, width // 2)),
                whole((width, width // 2)),
                whole((4, width)),
            ],
            scratch_shapes=[pltpu.VMEM((width, width), WIDE)],
        ),
        out_shape=[
            shaped((rows, width), WIDE),
            shaped((rows, width), LOW),
            shaped((width, width // 2), LOW),
            shaped((width, width // 2), LOW),
            shaped((4, width), WIDE),
        ],
        compiler_params=params(),
        cost_estimate=LONG,
        name="branch_back",
    )(place, residual, g_normed, cotangent, attended, w_out, gain, *after)


def project_back(place_ref, normed_turned, dq_ref, own_ref, got_ref, weights, joined_ref, send_ref, keep_ref, bias_ref):
    group = dq_ref.shape[1]
    half = 3 * group // 2
    mine = place_ref[0]
    joined_ref[:, :group] = dq_ref[...]
    for index in range(2):
        total = own_ref[index].astype(WIDE) + got_ref[index].astype(WIDE)
        joined_ref[:, (1 + index) * group : (2 + index) * group] = total.astype(LOW)
    if send_ref is not None:
        send_ref[...] = dot(normed_turned, joined_ref[:, half_of(1 - mine, half)]).astype(LOW)
        keep_ref[...] = dot(normed_turned, joined_ref[:, half_of(mine, half)]).astype(LOW)
    bias_ref[0:1] = column_sums(joined_ref[:, :group].astype(WIDE))
    bias_ref[1:2] = column_sums(joined_ref[:, 2 * group :].astype(WIDE))
    back = 0.0
    for index, weight_ref in enumerate(weights):
        part = joined_ref[:, index * group : (index + 1) * group]
        back = back + dot(part, weight_ref[...], 1, 1)
    return back


def first_back_kernel(
    place_ref,
    normed_ref,
    dq_ref,
    own_ref,
    got_ref,
    wq_ref,
    wk_ref,
    wv_ref,
    *rest,
):
    send_ref, keep_ref, bias_ref, part_ref, turned_ref, joined_ref = rest[-6:]

    @pl.when(pl.program_id(0) == 0)
    def _():
        turned_ref[...] = normed_ref[...].astype(WIDE).T.astype(LOW)
        part_ref[...] = jnp.zeros_like(part_ref)

    part_ref[...] += project_back(
        place_ref,
        turned_ref[...],
        dq_ref,
        own_ref,
        got_ref,
        (wq_ref, wk_ref, wv_ref),
        joined_ref,
        send_ref,
        keep_ref,
        bias_ref,
    )


def last_back_kernel(
    groups,
    place_ref,
    normed_ref,
    dq_ref,
    own_ref,
    got_ref,
    wq_ref,
    wk_ref,
    wv_ref,
    part_ref,
    embedded_ref,
    g_residual_ref,
    gain_ref,
    prior_ref,
    expression_ref,
    bias_first_ref,
    vectors_ref,
    bias_up_ref,
    *rest,
):
    send_ref, keep_ref, g_low_ref = rest[-8:-5]
    turned_ref, joined_ref, bias_ref, rows_ref, owned_ref = rest[-5:]
    rows, width = normed_ref.shape
    half = width // 2
    mine = place_ref[0]
    turned_ref[...] = normed_ref[...].astype(WIDE).T.astype(LOW)
    back = part_ref[...] + project_back(
        place_ref,
        turned_ref[...],
        dq_ref,
        own_ref,
        got_ref,
        (wq_ref, wk_ref, wv_ref),
        joined_ref,
        None,
        None,
        bias_ref,
    )
    unit, scale = normalize(embedded_ref[...])
    g_embedded = g_residual_ref[...] + norm_back(back, unit, scale, gain_ref[...][None])
    g_low_ref[...] = g_embedded.astype(LOW)
    prior = prior_ref[...].astype(WIDE).T.astype(LOW)
    count = owned_ref.shape[0]
    share = width // count
    for out_ref, side in ((send_ref, 1 - mine), (keep_ref, mine)):
        know = dot(prior, g_low_ref[:, half_of(side, half)]).astype(LOW)
        project = dot(
            turned_ref[...], joined_ref[:, half_of(side, half)]
        ).astype(LOW)
        for owner in range(count):
            entry = slice(owner * share, (owner + 1) * share)
            out_ref[owner, :share, :half] = project[entry]
            out_ref[owner, :share, half:] = know[entry]
    expression = jnp.broadcast_to(expression_ref[...], (8, rows)).T[:, :1]
    total = column_sums(g_embedded)
    hot = lax.broadcasted_iota(jnp.int32, (groups, width), 0) == place_ref[3]
    rows_ref[:groups] = jnp.where(hot, total, 0.0)
    rows_ref[groups : groups + 16] = jnp.concatenate(
        [
            column_sums(expression * g_embedded),
            column_sums(back * unit),
            column_sums(back),
            jnp.concatenate([bias_first_ref[0, 0:1], bias_first_ref[1, 0:1], bias_ref[0:1]], 1),
            jnp.concatenate([bias_first_ref[0, 1:2], bias_first_ref[1, 1:2], bias_ref[1:2]], 1),
            vectors_ref[...],
            jnp.zeros((7, width), WIDE),
        ],
        0,
    )
    owned_ref[...] = jnp.zeros_like(owned_ref)
    for owner in range(count):
        columns = slice(owner * share, (owner + 1) * share)
        for start in range(0, groups + 16, 32):
            size = min(32, groups + 16 - start)
            lanes = slice(start * 4, start * 4 + share)
            owned_ref[owner, :size, lanes] = rows_ref[start : start + size, columns]
        at, lanes = groups % 32 + 9, slice(groups // 32 * 128, groups // 32 * 128 + share)
        for part in range(4):
            first = (owner * 4 + part) * share
            owned_ref[owner, at + part : at + part + 1, lanes] = bias_up_ref[
                :, first : first + share
            ]
    low = up16(share)
    for out_ref, side in ((send_ref, 1 - mine), (keep_ref, mine)):
        rows_in = pl.ds(pl.multiple_of(side * 16, 16), 16)
        out_ref[:, low : low + 16, :half] = owned_ref[:, rows_in, :].astype(LOW)


def back_specs(rows, width, group, first):
    third = width // group
    weight = lambda part: pl.BlockSpec((width, group), lambda j, _: (0, part * third + first + j))
    both = pl.BlockSpec((2, rows, group), lambda j, _: (0, 0, j))
    return [
        whole((rows, width)),
        pl.BlockSpec((rows, group), lambda j, _: (0, j)),
        both,
        both,
        weight(0),
        weight(1),
        weight(2),
    ]


def first_back(place, normed, dq, own, got, w_qkv, group, after):
    rows, width = normed.shape
    count = dq.shape[1] // group
    half = 3 * group // 2
    tile = pl.BlockSpec((width, half), lambda j, _: (0, j))
    return pl.pallas_call(
        first_back_kernel,
        grid_spec=pltpu.PrefetchScalarGridSpec(
            num_scalar_prefetch=1,
            grid=(count,),
            in_specs=back_specs(rows, width, group, 0) + unread(after),
            out_specs=[
                tile,
                tile,
                pl.BlockSpec((None, 2, group), lambda j, _: (j, 0, 0)),
                whole((rows, width)),
            ],
            scratch_shapes=[
                pltpu.VMEM((width, rows), LOW),
                pltpu.VMEM((rows, 3 * group), LOW),
            ],
        ),
        out_shape=[
            shaped((width, count * half), LOW),
            shaped((width, count * half), LOW),
            shaped((count, 2, group), WIDE),
            shaped((rows, width), WIDE),
        ],
        compiler_params=params(),
        cost_estimate=LONG,
        name="first_back",
    )(place, normed, dq, own, got, w_qkv, w_qkv, w_qkv, *after)


def last_back(
    place,
    normed,
    dq,
    own,
    got,
    w_qkv,
    group,
    part,
    embedded,
    g_residual,
    gain,
    prior,
    expression,
    bias_first,
    vectors,
    bias_up,
    groups,
    count,
    after,
):
    rows, width = normed.shape
    half = width // 2
    first = width // group - 1
    entry = up16(width // count) + 16
    return pl.pallas_call(
        functools.partial(last_back_kernel, groups),
        grid_spec=pltpu.PrefetchScalarGridSpec(
            num_scalar_prefetch=1,
            grid=(1,),
            in_specs=back_specs(rows, width, group, first)
            + [
                whole((rows, width)),
                whole((rows, width)),
                whole((rows, width)),
                whole((width,)),
                whole((rows, width)),
                whole((1, rows)),
                whole(bias_first.shape),
                whole((4, width)),
                whole(bias_up.shape),
            ]
            + unread(after),
            out_specs=[
                whole((count, entry, width)),
                whole((count, entry, width)),
                whole((rows, width)),
            ],
            scratch_shapes=[
                pltpu.VMEM((width, rows), LOW),
                pltpu.VMEM((rows, 3 * group), LOW),
                pltpu.VMEM((2, group), WIDE),
                pltpu.VMEM((groups + 16, width), WIDE),
                pltpu.VMEM((count, 32, 384), WIDE),
            ],
        ),
        out_shape=[
            shaped((count, entry, width), LOW),
            shaped((count, entry, width), LOW),
            shaped((rows, width), LOW),
        ],
        compiler_params=params(),
        cost_estimate=LONG,
        name="last_back",
    )(
        place,
        normed,
        dq,
        own,
        got,
        w_qkv,
        w_qkv,
        w_qkv,
        part,
        embedded,
        g_residual,
        gain,
        prior,
        expression,
        bias_first,
        vectors,
        bias_up,
        *after,
    )


def gene_kernel(slots_ref, ids_ref, grad_ref, *rest):
    out_ref = rest[-1]
    slots = slots_ref[...]
    rows = grad_ref.shape[0]
    picker = jnp.where(slots == jnp.broadcast_to(ids_ref[...], (slots.shape[0], rows)), 1.0, 0.0)
    out_ref[...] = dot(picker.astype(LOW), grad_ref[...]).astype(LOW)


def gene_rows(slots, ids, grad, after):
    count = slots.shape[0]
    rows, width = grad.shape
    tile = min(count, 1152)
    return pl.pallas_call(
        gene_kernel,
        grid=(count // tile,),
        in_specs=[
            pl.BlockSpec((tile, 1), lambda j: (j, 0)),
            whole((1, rows)),
            whole((rows, width)),
        ]
        + unread(after),
        out_specs=pl.BlockSpec((tile, width), lambda j: (j, 0)),
        out_shape=shaped((count, width), LOW),
        compiler_params=params(),
        cost_estimate=LONG,
        name="gene_rows",
    )(slots, ids, grad, *after)


def swap_cores(array):
    return lax.ppermute(array, "blk", [(0, 1), (1, 0)])


def bits_apart(array, mask):
    count = lax.axis_size("dp")
    return lax.ppermute(array, "dp", [(i, i ^ mask) for i in range(count)])


def pick(array, position, index):
    return lax.dynamic_index_in_dim(array, index, position, keepdims=False)


class Share:
    QUAD = "quad"

    def __init__(self, segments, route):
        self.bits = lax.axis_size("dp").bit_length() - 1
        self.route = list(route)
        self.rows = []
        self.sources = []
        dims = tuple(range(self.bits - 1, -1, -1))
        for arrays, blocks, *rows in segments:
            first, single = len(self.rows), len(blocks) == 1
            rows = rows[0] if rows else [(0, arrays[0].shape[1])] * len(blocks)
            self.rows += [size for _, size in rows]
            parts = [
                (first + at, rows[at][0], 0 if single else block * LANES)
                for at, block in enumerate(blocks)
            ]
            columns = LANES if single else arrays[0].shape[2]
            where, height = (0, blocks[0] if single else 0), arrays[0].shape[1]
            start, size = rows[0]
            if single and size % 16 == start % size == height % size == 0:
                where, height = (start // size, where[1]), size
                parts = [(first, 0, 0)]
            for array in arrays:
                shape = (2,) * self.bits + array.shape[1:]
                self.sources.append((array.reshape(shape), dims, where, (height, columns), parts))
        self.arriving = []
        self.fixed = ()
        self.settle_places()

    def join(self, other):
        shift = len(self.rows)
        moved = lambda sources: [
            source[:4] + ([(index + shift, row, column) for index, row, column in source[4]],)
            for source in sources
        ]
        self.rows = self.rows + other.rows
        self.sources += moved(other.sources)
        self.arriving += moved(other.arriving)
        self.settle_places()
        return self

    def settle_places(self):
        self.places, place = [], 0
        for rows in self.rows:
            self.places.append(place)
            place += up16(rows)
        self.height = self.places[-1] + self.rows[-1]

    def parts(self):
        return [(index, place, 0) for index, place in enumerate(self.places)]

    def targets(self):
        step = self.route[0]
        if step == self.QUAD:
            low, high = self.bits - 2, self.bits - 1
            return [{low: way & 1, high: way >> 1} for way in (1, 2, 3)]
        return [{step: 1}]

    def left(self, target=()):
        gone = self.fixed + tuple(target)
        return [bit for bit in range(self.bits - 1, -1, -1) if bit not in gone]

    def receive(self, targets, sent):
        self.route.pop(0)
        for target, array in zip(targets, sent):
            mask = sum(flip << bit for bit, flip in target.items())
            dims = tuple(self.left(target))
            self.arriving.append(
                (bits_apart(array, mask), dims, (0, 0), array.shape[-2:], self.parts())
            )
        self.fixed += tuple(targets[0])

    def arrived(self):
        self.sources, self.arriving = self.sources + self.arriving, []


SEND, SETTLE, FINISH = range(3)


def combine(place, shares, after, mode=SEND, last=None):
    operands, specs, plan, out_specs, out_shape = [], [], [], [], []
    steps = []
    for share in shares:
        if mode != SETTLE:
            share.arrived()
        targets = share.targets() if mode == SEND else [{}]
        steps.append(targets)
        left = share.left(targets[0]) if mode != FINISH else []
        quad = len(targets) > 1
        used = []
        for array, dims, block, size, parts in share.sources:
            shape, where, picked = [], [], []
            for bit in dims:
                free = bit in left or (quad and bit in targets[0])
                shape.append(2 if free else None)
                where.append(None if free else (bit, targets[0].get(bit, 0)))
                if quad and bit in targets[0]:
                    picked.append(bit)

            def index(_, place, where=tuple(where), block=block):
                lead = tuple(
                    0 if at is None else (1 - place[4 + at[0]] if at[1] else place[4 + at[0]])
                    for at in where
                )
                return lead + block

            specs.append(pl.BlockSpec(tuple(shape) + tuple(size), index))
            used.append((len(operands), parts))
            operands.append(array)
        for target in targets:
            plan.append((share.rows, share.places, used, target if quad else {}))
            if mode != FINISH:
                shape = (2,) * len(left) + (share.height, LANES)
                out_specs.append(whole(shape))
                out_shape.append(shaped(shape, LOW if mode == SEND else WIDE))
    for shape, _ in last or []:
        out_specs.append(whole(shape))
        out_shape.append(shaped(shape, WIDE))
    count = len(operands)

    def kernel(*refs):
        place_ref, sources, outs = refs[0], refs[1 : 1 + count], refs[1 + count + len(after) :]

        def summed(item, block):
            rows, _, used, target = plan[item]
            total = None
            way = tuple(
                1 - place_ref[4 + bit] if flip else place_ref[4 + bit]
                for bit, flip in sorted(target.items(), reverse=True)
            )
            for operand, parts in used:
                for index, row, column in parts:
                    if index == block:
                        ref = sources[operand]
                        spot = (slice(row, row + rows[block]), slice(column, column + LANES))
                        lead = way + (slice(None),) * (len(ref.shape) - 2 - len(way))
                        part = ref[lead + spot].astype(WIDE)
                        total = part if total is None else total + part
            return total

        if mode == FINISH:
            for (_, pieces), out in zip(last, outs):
                for item, block, row, column in pieces:
                    value = summed(item, block)
                    out[row : row + value.shape[0], column : column + LANES] = value
            return
        for item, out in enumerate(outs):
            for block, start in enumerate(plan[item][1]):
                value = summed(item, block)
                out[..., start : start + value.shape[-2], :] = value.astype(out.dtype)

    outs = pl.pallas_call(
        kernel,
        grid_spec=pltpu.PrefetchScalarGridSpec(
            num_scalar_prefetch=1,
            grid=(1,),
            in_specs=specs + unread(after),
            out_specs=out_specs,
        ),
        out_shape=out_shape,
        compiler_params=params(),
        cost_estimate=LONG,
        name="combine",
    )(place, *operands, *after)
    taken = 0
    for share, targets in zip(shares, steps):
        if mode == SEND:
            share.receive(targets, outs[taken : taken + len(targets)])
        if mode == SETTLE:
            share.sources = [
                (outs[taken], tuple(share.left()), (0, 0), outs[taken].shape[-2:], share.parts())
            ]
        taken += len(targets)
    return outs


def assemble(place, own, other, shapes, pieces, small_row=None):
    def kernel(place_ref, own_ref, other_ref, *outs):
        first = place_ref[0] == 0

        def of_core(core, rows, columns):
            return jnp.where(first == (core == 0), own_ref[rows, columns], other_ref[rows, columns])

        for core, row, rows, column, columns, target, out_column in pieces:
            value = of_core(core, slice(row, row + rows), slice(column, column + columns))
            outs[target][:, out_column : out_column + columns] = value
        if small_row is None:
            return
        group_ref, vector_refs, long_ref = outs[2], outs[3:-1], outs[-1]
        share, groups = group_ref.shape
        rows = slice(small_row, small_row + 16)
        for start in range(0, groups, 16):
            lanes = slice(start // 32 * 128, start // 32 * 128 + share)
            group_ref[:, start : start + 16] = of_core(start // 16 % 2, rows, lanes).T
        rest = of_core(0, rows, slice(groups // 32 * 128, groups // 32 * 128 + 128))
        for index, ref in enumerate(vector_refs):
            ref[...] = rest[index, :share]
        long_ref[...] = jnp.concatenate(
            [rest[9 + part : 10 + part, :share] for part in range(4)], 1
        )[0]

    return pl.pallas_call(
        kernel,
        grid_spec=pltpu.PrefetchScalarGridSpec(
            num_scalar_prefetch=1,
            grid=(1,),
            in_specs=[whole(own.shape), whole(own.shape)],
            out_specs=[whole(shape) for shape in shapes],
        ),
        out_shape=[shaped(shape, WIDE) for shape in shapes],
        compiler_params=params(),
        cost_estimate=LONG,
        name="assemble",
    )(place, own, other)


def body(
    gene_ids,
    values,
    knowledge,
    lengths,
    groups,
    gene_table,
    group_table,
    w_know,
    w_value,
    norm1_gain,
    norm1_bias,
    w_qkv,
    bias_q,
    bias_v,
    w_out,
    bias_out,
    norm2_gain,
    norm2_bias,
    w_up,
    bias_up,
    w_down,
    bias_down,
    cotangent,
):
    width = w_out.shape[0]
    units = w_up.shape[1]
    rows = gene_ids.shape[1]
    count = lax.axis_size("dp")
    mine = lax.axis_index("blk")
    length, group = lengths[0], groups[0]
    prior = knowledge[0]
    row = lambda vector: vector.reshape(1, -1)
    me = lax.axis_index("dp")
    bits = count.bit_length() - 1
    place = jnp.stack(
        [mine, length - mine * rows, length - (1 - mine) * rows, group]
        + [(me >> bit) & 1 for bit in range(bits)]
    ).astype(jnp.int32)
    if gene_table.shape[0] > 8 * rows:
        table = gene_table[gene_ids[0]]
    else:
        table = gene_table
    embedded, normed, kv_own = embed(
        place,
        gene_ids,
        values,
        prior,
        table,
        group_table,
        w_know,
        w_value,
        norm1_gain,
        norm1_bias,
        w_qkv,
        bias_v,
    )
    kv_other = swap_cores(kv_own)
    queries = project_queries(normed, w_qkv, bias_q)
    attended, probs, inverse = attend(place, queries, kv_own, kv_other)
    (
        block_output,
        residual,
        g_normed_two,
        up_send,
        up_keep,
        down_send,
        down_keep,
        bias_up_grad,
    ) = feed_forward(
        place,
        attended,
        embedded,
        cotangent[0],
        w_out,
        bias_out,
        norm2_gain,
        norm2_bias,
        w_up,
        row(bias_up),
        w_down,
        bias_down,
    )
    g_residual, g_attended, out_send, out_keep, vectors = branch_back(
        place,
        residual,
        g_normed_two,
        cotangent[0],
        attended,
        w_out,
        norm2_gain,
        [up_send, down_send],
    )

    owners = lambda array: array.reshape(count, -1, array.shape[-1])
    low_bits = list(range(bits - 2))
    turned = low_bits[1::-1] + low_bits[2:]
    quad = [Share.QUAD]
    up_terms = [owners(up_keep), owners(swap_cores(up_send))]
    blocks = units // 2 // LANES
    out_terms = [owners(out_keep), owners(swap_cores(out_send))]
    down_terms = [owners(down_keep), owners(swap_cores(down_send))]
    high = units // count
    early = [
        Share([(down_terms, [0]), (out_terms, [0])], low_bits + quad),
        Share([(up_terms, list(range(blocks)))], turned + quad),
    ]
    token = combine(place, early, [])
    dq1, own1, other1 = attend_back(
        queries, kv_own, kv_other, attended, g_attended, probs, inverse, 0, 4, token
    )
    got1 = swap_cores(other1)
    dq2, own2, other2 = attend_back(
        queries, kv_own, kv_other, attended, g_attended, probs, inverse, 4, 2, [dq1]
    )
    got2 = swap_cores(other2)
    qkv_send, qkv_keep, bias_first, part = first_back(
        place, normed, dq1, own1, got1, w_qkv, 256, [dq2]
    )
    qkv = [owners(qkv_keep), owners(swap_cores(qkv_send))]
    token = [part, qkv_send]
    for _ in low_bits[1:]:
        token = combine(place, early, token)
    early = [early[0].join(early[1])]
    tail_send, tail_keep, g_low = last_back(
        place,
        normed,
        dq2,
        own2,
        got2,
        w_qkv,
        256,
        part,
        embedded,
        g_residual,
        norm1_gain,
        prior,
        values,
        bias_first,
        vectors,
        bias_up_grad,
        group_table.shape[0],
        count,
        token,
    )
    slot = jnp.arange(count * VOC_DEV, dtype=jnp.int32)[:, None]
    slot = slot + slot // VOC_DEV * VOC_DEV
    gene_send = gene_rows(slot + (1 - mine) * VOC_DEV, gene_ids, g_low, [tail_send, qkv[1]])
    gene_got = swap_cores(gene_send)
    gene_keep = gene_rows(slot + mine * VOC_DEV, gene_ids, g_low, [gene_send])
    share = width // count
    tail = [tail_keep, swap_cores(tail_send)]
    gene = [owners(gene_keep), owners(gene_got)]
    small_at = up16(share)
    late = [
        Share([(qkv, [0, 1]), (gene, [0])], low_bits + quad),
        Share(
            [
                (tail, [0], [(0, share)]),
                (tail, [1], [(0, share)]),
                (tail, [0], [(small_at, 16)]),
                (gene, [1]),
            ],
            turned + quad,
        ),
    ]
    token = combine(place, late, [gene_keep])
    token = combine(place, early, token)
    for _ in low_bits[1:]:
        token = combine(place, late, token)
    token = combine(place, late, token, SETTLE)
    late = [late[0].join(late[1])]
    step = up16(share)
    layout = [(0, 0, 0, 0), (0, 1, high + blocks * step, 0)]
    layout += [(0, 2 + block, high + block * step, 0) for block in range(blocks)]
    (own,) = combine(place, early, token, FINISH, [((high + (blocks + 1) * step, LANES), layout)])
    other = swap_cores(own)
    combine(place, late, [own])
    pieces = []
    for core in range(2):
        pieces.append((core, 0, high, 0, LANES, 0, core * LANES))
        for block in range(blocks):
            place_in = (core * blocks + block) * LANES
            pieces.append((core, high + block * step, share, 0, LANES, 1, place_in))
        pieces.append((core, high + blocks * step, share, 0, LANES, 2, core * LANES))
    w_down_share, w_up_share, w_out_share = assemble(
        place, own, other, [(high, width), (share, units), (share, width)], pieces
    )
    layout = [(0, 0, 0, 0), (0, 1, step, 0)]
    layout += [(0, 3 + index, (2 + index) * step, 0) for index in range(3)]
    own, gene_grad = combine(
        place,
        late,
        [w_out_share],
        FINISH,
        [
            ((4 * step + 16, LANES), layout),
            ((VOC_DEV, width), [(0, 2, 0, 0), (0, 6, 0, LANES)]),
        ],
    )
    other = swap_cores(own)
    pieces = []
    for block in range(3):
        at = block * step
        pieces.append((0, at, share, 0, 256, 0, block * 256))
        pieces.append((0, at, share, 256, 128, 0, width + block * 256))
        pieces.append((1, at, share, 0, 128, 0, width + block * 256 + 128))
        pieces.append((1, at, share, 128, 256, 0, 2 * width + block * 256))
    for core in range(2):
        pieces.append((core, 3 * step, share, 0, LANES, 1, core * LANES))
    w_qkv_share, w_know_share, group_share, *extra, bias_up_share = assemble(
        place,
        own,
        other,
        [(share, 3 * width), (share, width), (share, group_table.shape[0])]
        + [(share,)] * 9
        + [(units // count,)],
        pieces,
        4 * step,
    )
    return (
        block_output[None],
        gene_grad,
        group_share.T,
        w_know_share,
        extra[0],
        extra[1],
        extra[2],
        w_qkv_share,
        extra[3],
        extra[4],
        w_out_share,
        extra[5],
        extra[6],
        extra[7],
        w_up_share,
        bias_up_share,
        w_down_share,
        extra[8],
    )


def solution(mesh):
    in_specs = (
        P("dp", "blk"),
        P("dp", "blk"),
        P("dp", "blk", None),
        P("dp"),
        P("dp"),
        P(),
        P(),
        P(),
        P(),
        P(),
        P(),
        P(),
        P(),
        P(),
        P(),
        P(),
        P(),
        P(),
        P(),
        P(),
        P(),
        P(),
        P("dp", "blk", None),
    )
    out_specs = (
        P("dp", "blk", None),
        P(("dp", "blk"), None),
        P(None, "dp"),
        P("dp", None),
        P("dp"),
        P("dp"),
        P("dp"),
        P("dp", None),
        P("dp"),
        P("dp"),
        P("dp", None),
        P("dp"),
        P("dp"),
        P("dp"),
        P("dp", None),
        P("dp"),
        P("dp", None),
        P("dp"),
    )
    return jax.shard_map(body, mesh=mesh, in_specs=in_specs, out_specs=out_specs, check_vma=False)
```

```python
import functools

import jax
import jax.numpy as jnp
from jax import lax
from jax.experimental import pallas as pl
from jax.experimental.pallas import tpu as pltpu
from jax.sharding import PartitionSpec as P

HEAD_DIM = 64
VOC_DEV = 72
EPSILON = 1e-05
LANES = 384
LOW = jnp.bfloat16
WIDE = jnp.float32
GRANT = 44 << 20


LONG = pl.CostEstimate(flops=10**12, bytes_accessed=1, transcendentals=0)


def dot(left, right, left_dim=1, right_dim=0):
    return lax.dot_general(
        left, right, (((left_dim,), (right_dim,)), ((), ())), preferred_element_type=WIDE
    )


def column_sums(array):
    return jnp.sum(array, 0, keepdims=True)


def row_means(array):
    return jnp.mean(array, -1, keepdims=True)


def normalize(array):
    center = array - row_means(array)
    scale = lax.rsqrt(row_means(center * center) + EPSILON)
    return center * scale, scale


def norm_back(grad, unit, scale, gain):
    inner = grad * gain
    return scale * (inner - row_means(inner) - unit * row_means(inner * unit))


def half_of(index, half):
    return pl.ds(pl.multiple_of(index * half, 128), half)


def whole(shape):
    return pl.BlockSpec(shape, lambda *_: (0,) * len(shape))


def up16(rows):
    return -(-rows // 16) * 16


def unread(arrays):
    return [pl.BlockSpec(memory_space=pl.ANY)] * len(arrays)


def params(grant=GRANT):
    return pltpu.CompilerParams(vmem_limit_bytes=grant)


def shaped(shape, dtype):
    return jax.ShapeDtypeStruct(shape, dtype)


def embed_kernel(
    place_ref,
    ids_ref,
    expression_ref,
    prior_ref,
    table_ref,
    group_ref,
    w_know_ref,
    w_value_ref,
    gain_ref,
    offset_ref,
    w_key_ref,
    w_val_ref,
    bias_val_ref,
    embedded_ref,
    normed_ref,
    kv_ref,
):
    rows, width = prior_ref.shape
    embedded = dot(prior_ref[...], w_know_ref[...])
    if table_ref.shape[0] == rows:
        gathered = table_ref[...].astype(WIDE)
    else:
        ids = jnp.broadcast_to(ids_ref[...], (8, rows)).T[:, :1]
        slots = lax.broadcasted_iota(jnp.int32, (rows, table_ref.shape[0]), 1)
        picker = jnp.where(slots == ids, 1.0, 0.0).astype(LOW)
        gathered = dot(picker, table_ref[...])
    expression = jnp.broadcast_to(expression_ref[...], (8, rows)).T[:, :1]
    groups = lax.broadcasted_iota(jnp.int32, (8, group_ref.shape[0]), 1)
    group_row = dot(jnp.where(groups == place_ref[3], 1.0, 0.0).astype(LOW), group_ref[...])[:1]
    embedded = gathered + group_row + expression * w_value_ref[...][None] + embedded
    embedded_ref[...] = embedded
    unit, _ = normalize(embedded)
    normed = (unit * gain_ref[...][None] + offset_ref[...][None]).astype(LOW)
    normed_ref[...] = normed
    kv_ref[:, :width] = dot(normed, w_key_ref[...]).astype(LOW)
    kv_ref[:, width:] = (dot(normed, w_val_ref[...]) + bias_val_ref[...][None]).astype(LOW)


def embed(
    place, ids, expression, prior, table, group_table, w_know, w_value, gain, offset, w_qkv, bias_v
):
    rows, width = prior.shape
    columns = lambda index: pl.BlockSpec((width, width), lambda *_: (0, index))
    return pl.pallas_call(
        embed_kernel,
        grid_spec=pltpu.PrefetchScalarGridSpec(
            num_scalar_prefetch=1,
            grid=(1,),
            in_specs=[
                whole((1, rows)),
                whole((1, rows)),
                whole((rows, width)),
                whole(table.shape),
                whole(group_table.shape),
                whole((width, width)),
                whole((width,)),
                whole((width,)),
                whole((width,)),
                columns(1),
                columns(2),
                whole((width,)),
            ],
            out_specs=[whole((rows, width)), whole((rows, width)), whole((rows, 2 * width))],
        ),
        out_shape=[
            shaped((rows, width), WIDE),
            shaped((rows, width), LOW),
            shaped((rows, 2 * width), LOW),
        ],
        compiler_params=params(60 << 20),
        name="embed",
    )(
        place,
        ids,
        expression,
        prior,
        table,
        group_table,
        w_know,
        w_value,
        gain,
        offset,
        w_qkv,
        w_qkv,
        bias_v,
    )


def query_kernel(normed_ref, w_query_ref, bias_ref, out_ref):
    out_ref[...] = (dot(normed_ref[...], w_query_ref[...]) + bias_ref[...][None]).astype(LOW)


def project_queries(normed, w_qkv, bias_q):
    rows, width = normed.shape
    return pl.pallas_call(
        query_kernel,
        grid=(1,),
        in_specs=[whole((rows, width)), whole((width, width)), whole((width,))],
        out_specs=whole((rows, width)),
        out_shape=shaped((rows, width), LOW),
        compiler_params=params(),
        cost_estimate=pl.CostEstimate(
            flops=2 * rows * width * width, bytes_accessed=4 * rows * width, transcendentals=0
        ),
        name="queries",
    )(normed, w_qkv, bias_q)


def attend_kernel(place_ref, q_ref, ko_ref, vo_ref, kr_ref, vr_ref, out_ref, p_ref, c_ref):
    rows = q_ref.shape[0]
    lane = lax.broadcasted_iota(jnp.int32, (rows, 128), 1)
    place = lax.broadcasted_iota(jnp.int32, (rows, 128), 0)
    queries = q_ref[...] * LOW(HEAD_DIM**-0.5)
    halves = []
    for index, k_ref in enumerate((ko_ref, kr_ref)):
        dead = jnp.where(place < place_ref[1 + index], 0.0, -1e30).astype(LOW)
        halves.append((k_ref[...], dead))
    values = [vo_ref[...].T, vr_ref[...].T]
    ones = jnp.ones((16, rows), LOW)
    scored, outs = [], []
    for head in range(2):
        inside = (lane < HEAD_DIM) if head == 0 else (lane >= HEAD_DIM)
        spare = HEAD_DIM * (1 - head)
        asked = jnp.where(inside, queries, jnp.where(lane == spare, 1.0, 0.0).astype(LOW))
        scored.append(
            [dot(jnp.where(lane == spare, dead, keys), asked, 1, 1) for keys, dead in halves]
        )
    for head in range(2):
        scores = scored[head]
        top = jnp.maximum(*[jnp.max(part, 0, keepdims=True) for part in scores])
        mixed = 0.0
        for index in range(2):
            low = jnp.exp(scores[index] - top).astype(LOW)
            p_ref[head, index * rows : (index + 1) * rows, :] = low
            own = values[index][head * HEAD_DIM : (head + 1) * HEAD_DIM]
            mixed = mixed + dot(jnp.concatenate([own, ones], 0), low)
        inverse = 1.0 / mixed[HEAD_DIM : HEAD_DIM + 1]
        c_ref[0, head : head + 1, :] = inverse
        outs.append(mixed[:HEAD_DIM] * inverse)
    out_ref[...] = jnp.concatenate(outs, 0).T.astype(LOW)


def attend(place, queries, kv_own, kv_other):
    rows, width = queries.shape
    pairs = width // 128
    block = lambda shift: pl.BlockSpec((rows, 128), lambda j, _: (0, shift + j))
    return pl.pallas_call(
        attend_kernel,
        grid_spec=pltpu.PrefetchScalarGridSpec(
            num_scalar_prefetch=1,
            grid=(pairs,),
            in_specs=[block(0), block(0), block(pairs), block(0), block(pairs)],
            out_specs=[
                block(0),
                pl.BlockSpec((2, 2 * rows, rows), lambda j, _: (j, 0, 0)),
                pl.BlockSpec((1, 2, rows), lambda j, _: (j, 0, 0)),
            ],
        ),
        out_shape=[
            shaped((rows, width), LOW),
            shaped((2 * pairs, 2 * rows, rows), LOW),
            shaped((pairs, 2, rows), WIDE),
        ],
        compiler_params=params(),
        cost_estimate=pl.CostEstimate(
            flops=16 * rows * rows * width,
            bytes_accessed=8 * rows * rows * pairs,
            transcendentals=4 * rows * rows * pairs,
        ),
        name="attend",
    )(place, queries, kv_own, kv_own, kv_other, kv_other)


def attend_back_kernel(
    q_ref,
    ko_ref,
    vo_ref,
    kr_ref,
    vr_ref,
    a_ref,
    g_ref,
    p_ref,
    c_ref,
    *rest,
):
    dq_ref, dkvo_ref, dkvr_ref = rest[-3:]
    rows = q_ref.shape[0]
    lane = lax.broadcasted_iota(jnp.int32, (rows, 128), 1)
    mixed = a_ref[...].astype(WIDE).T
    grad = g_ref[...].astype(WIDE).T
    grad = jnp.concatenate(
        [grad[:HEAD_DIM] * c_ref[0, :1, :], grad[HEAD_DIM:] * c_ref[0, 1:, :]], 0
    )
    inner = grad * mixed
    inner = [column_sums(inner[:HEAD_DIM]), column_sums(inner[HEAD_DIM:])]
    first = lax.broadcasted_iota(jnp.int32, (128, rows), 0) < HEAD_DIM
    low = grad.astype(LOW)
    masked = [
        jnp.where(first, low, jnp.zeros_like(low)),
        jnp.where(first, jnp.zeros_like(low), low),
    ]
    grad_rows = grad.T.astype(LOW)
    queries = q_ref[...]
    parts = [0.0, 0.0]
    for index, (k_ref, v_ref, out_ref) in enumerate(
        ((ko_ref, vo_ref, dkvo_ref), (kr_ref, vr_ref, dkvr_ref))
    ):
        keys = k_ref[...].T
        values = v_ref[...]
        key_grads, val_grads = [], []
        for head in range(2):
            probs = p_ref[head, index * rows : (index + 1) * rows, :]
            wide = dot(values, masked[head]) - inner[head]
            score = (probs.astype(WIDE) * wide).astype(LOW)
            val_grads.append(dot(probs, grad_rows))
            key_grads.append(dot(score, queries))
            parts[head] = parts[head] + dot(keys[head * HEAD_DIM : (head + 1) * HEAD_DIM], score)
        chosen = lane < HEAD_DIM
        out_ref[0] = (jnp.where(chosen, *key_grads) * HEAD_DIM**-0.5).astype(LOW)
        out_ref[1] = jnp.where(chosen, *val_grads).astype(LOW)
    dq_ref[...] = (jnp.concatenate(parts, 0).T * HEAD_DIM**-0.5).astype(LOW)


def attend_back(queries, kv_own, kv_other, attended, grad, probs, inverse, start, count, after):
    rows, width = queries.shape
    pairs = width // 128
    block = lambda shift: pl.BlockSpec((rows, 128), lambda j: (0, shift + j))
    near, far = block(start), block(pairs + start)
    both = pl.BlockSpec((2, rows, 128), lambda j: (0, 0, j))
    return pl.pallas_call(
        attend_back_kernel,
        grid=(count,),
        in_specs=[
            near,
            near,
            far,
            near,
            far,
            near,
            near,
            pl.BlockSpec((2, 2 * rows, rows), lambda j: (start + j, 0, 0)),
            pl.BlockSpec((1, 2, rows), lambda j: (start + j, 0, 0)),
        ]
        + unread(after),
        out_specs=[block(0), both, both],
        out_shape=[
            shaped((rows, 128 * count), LOW),
            shaped((2, rows, 128 * count), LOW),
            shaped((2, rows, 128 * count), LOW),
        ],
        compiler_params=params(),
        cost_estimate=LONG,
        name="attend_back",
    )(queries, kv_own, kv_own, kv_other, kv_other, attended, grad, probs, inverse, *after)


def ffn_kernel(
    place_ref,
    attended_ref,
    embedded_ref,
    cotangent_ref,
    w_out_ref,
    bias_out_ref,
    gain_ref,
    offset_ref,
    w_up_ref,
    bias_up_ref,
    w_down_ref,
    bias_down_ref,
    output_ref,
    residual_ref,
    g_normed_ref,
    up_send_ref,
    up_keep_ref,
    down_send_ref,
    down_keep_ref,
    bias_up_grad_ref,
    normed_ref,
    total_ref,
    g_out_ref,
    g_halves_ref,
):
    step, steps = pl.program_id(0), pl.num_programs(0)
    rows, width = attended_ref.shape
    half = width // 2
    mine = place_ref[0]
    alive = lax.broadcasted_iota(jnp.int32, (rows, 1), 0) < place_ref[1]

    @pl.when(step == 0)
    def _():
        residual = embedded_ref[...] + (
            dot(attended_ref[...], w_out_ref[...]) + bias_out_ref[...][None]
        )
        residual_ref[...] = residual
        unit, _ = normalize(residual)
        normed_ref[...] = (unit * gain_ref[...][None] + offset_ref[...][None]).astype(LOW)
        g_out_ref[...] = jnp.where(alive, cotangent_ref[...].astype(WIDE), 0.0).astype(LOW)
        g_halves_ref[:, :half] = g_out_ref[:, half_of(1 - mine, half)]
        g_halves_ref[:, half:] = g_out_ref[:, half_of(mine, half)]
        total_ref[...] = jnp.zeros_like(total_ref)
        g_normed_ref[...] = jnp.zeros_like(g_normed_ref)

    hidden = dot(normed_ref[...], w_up_ref[...]) + bias_up_ref[...]
    g_act = dot(g_out_ref[...], w_down_ref[...], 1, 1)
    share = 0.5 * (1.0 + lax.erf(hidden * 0.5**0.5))
    density = jnp.exp(-0.5 * hidden * hidden) * 0.3989422804014327
    activated = (hidden * share).astype(LOW)
    g_hidden = (g_act * (share + hidden * density)).astype(LOW)
    total_ref[...] += dot(activated, w_down_ref[...])
    g_normed_ref[...] += dot(g_hidden, w_up_ref[...], 1, 1)
    down = dot(activated, g_halves_ref[...], 0, 0).astype(LOW)
    down_send_ref[...] = down[:, :half]
    down_keep_ref[...] = down[:, half:]
    up = dot(normed_ref[...], g_hidden, 0, 0).astype(LOW)
    bias_up_grad_ref[...] = column_sums(g_hidden.astype(WIDE))

    @pl.when(step < steps // 2)
    def _():
        up_send_ref[...] = up

    @pl.when(step >= steps // 2)
    def _():
        up_keep_ref[...] = up

    @pl.when(step == steps - 1)
    def _():
        final = residual_ref[...] + (total_ref[...] + bias_down_ref[...][None])
        output_ref[...] = jnp.where(alive, final, 0.0).astype(LOW)


def feed_forward(
    place,
    attended,
    embedded,
    cotangent,
    w_out,
    bias_out,
    gain,
    offset,
    w_up,
    bias_up,
    w_down,
    bias_down,
):
    rows, width = attended.shape
    units = w_up.shape[1]
    tile = 768
    steps = units // tile
    turn = lambda j, place: lax.rem(j + (1 - place[0]) * (steps // 2), steps)
    down_tile = pl.BlockSpec((tile, width // 2), lambda j, place: (turn(j, place), 0))
    return pl.pallas_call(
        ffn_kernel,
        grid_spec=pltpu.PrefetchScalarGridSpec(
            num_scalar_prefetch=1,
            grid=(steps,),
            in_specs=[
                whole((rows, width)),
                whole((rows, width)),
                whole((rows, width)),
                whole((width, width)),
                whole((width,)),
                whole((width,)),
                whole((width,)),
                pl.BlockSpec((width, tile), lambda j, place: (0, turn(j, place))),
                pl.BlockSpec((1, tile), lambda j, place: (0, turn(j, place))),
                pl.BlockSpec((tile, width), lambda j, place: (turn(j, place), 0)),
                whole((width,)),
            ],
            out_specs=[
                whole((rows, width)),
                whole((rows, width)),
                whole((rows, width)),
                pl.BlockSpec((width, tile), lambda j, _: (0, jnp.minimum(j, steps // 2 - 1))),
                pl.BlockSpec((width, tile), lambda j, _: (0, jnp.maximum(j - steps // 2, 0))),
                down_tile,
                down_tile,
                pl.BlockSpec((1, tile), lambda j, place: (0, turn(j, place))),
            ],
            scratch_shapes=[
                pltpu.VMEM((rows, width), LOW),
                pltpu.VMEM((rows, width), WIDE),
                pltpu.VMEM((rows, width), LOW),
                pltpu.VMEM((rows, width), LOW),
            ],
        ),
        out_shape=[
            shaped((rows, width), LOW),
            shaped((rows, width), WIDE),
            shaped((rows, width), WIDE),
            shaped((width, units // 2), LOW),
            shaped((width, units // 2), LOW),
            shaped((units, width // 2), LOW),
            shaped((units, width // 2), LOW),
            shaped((1, units), WIDE),
        ],
        compiler_params=params(),
        cost_estimate=LONG,
        name="feed_forward",
    )(
        place,
        attended,
        embedded,
        cotangent,
        w_out,
        bias_out,
        gain,
        offset,
        w_up,
        bias_up,
        w_down,
        bias_down,
    )


def branch_kernel(
    place_ref,
    residual_ref,
    g_normed_ref,
    cotangent_ref,
    attended_ref,
    w_out_ref,
    gain_ref,
    *rest,
):
    g_residual_ref, g_attended_ref, out_send_ref, out_keep_ref, vectors_ref, total_ref = rest[-6:]
    step, steps = pl.program_id(0), pl.num_programs(0)
    rows, width = residual_ref.shape
    half = width // 2
    mine = place_ref[0]
    alive = step * rows + lax.broadcasted_iota(jnp.int32, (rows, 1), 0) < place_ref[1]

    @pl.when(step == 0)
    def _():
        total_ref[...] = jnp.zeros_like(total_ref)
        vectors_ref[...] = jnp.zeros_like(vectors_ref)

    unit, scale = normalize(residual_ref[...])
    g_final = jnp.where(alive, cotangent_ref[...].astype(WIDE), 0.0)
    g_normed = g_normed_ref[...]
    g_residual = g_final + norm_back(g_normed, unit, scale, gain_ref[...][None])
    g_residual_ref[...] = g_residual
    g_branch = g_residual.astype(LOW)
    g_attended_ref[...] = dot(g_branch, w_out_ref[...], 1, 1).astype(LOW)
    total_ref[...] += dot(attended_ref[...], g_branch, 0, 0)
    vectors_ref[...] += jnp.concatenate(
        [
            column_sums(g_branch.astype(WIDE)),
            column_sums(g_normed * unit),
            column_sums(g_normed),
            column_sums(g_final),
        ],
        0,
    )

    @pl.when(step == steps - 1)
    def _():
        out_send_ref[...] = total_ref[:, half_of(1 - mine, half)].astype(LOW)
        out_keep_ref[...] = total_ref[:, half_of(mine, half)].astype(LOW)


def branch_back(place, residual, g_normed, cotangent, attended, w_out, gain, after):
    rows, width = residual.shape
    steps = 2
    tile = pl.BlockSpec((rows // steps, width), lambda j, _: (j, 0))
    return pl.pallas_call(
        branch_kernel,
        grid_spec=pltpu.PrefetchScalarGridSpec(
            num_scalar_prefetch=1,
            grid=(steps,),
            in_specs=[tile, tile, tile, tile, whole((width, width)), whole((width,))]
            + unread(after),
            out_specs=[
                tile,
                tile,
                whole((width, width // 2)),
                whole((width, width // 2)),
                whole((4, width)),
            ],
            scratch_shapes=[pltpu.VMEM((width, width), WIDE)],
        ),
        out_shape=[
            shaped((rows, width), WIDE),
            shaped((rows, width), LOW),
            shaped((width, width // 2), LOW),
            shaped((width, width // 2), LOW),
            shaped((4, width), WIDE),
        ],
        compiler_params=params(),
        cost_estimate=LONG,
        name="branch_back",
    )(place, residual, g_normed, cotangent, attended, w_out, gain, *after)


def project_back(place_ref, normed_turned, dq_ref, own_ref, got_ref, weights, joined_ref, send_ref, keep_ref, bias_ref):
    group = dq_ref.shape[1]
    half = 3 * group // 2
    mine = place_ref[0]
    joined_ref[:, :group] = dq_ref[...]
    for index in range(2):
        total = own_ref[index].astype(WIDE) + got_ref[index].astype(WIDE)
        joined_ref[:, (1 + index) * group : (2 + index) * group] = total.astype(LOW)
    if send_ref is not None:
        send_ref[...] = dot(normed_turned, joined_ref[:, half_of(1 - mine, half)]).astype(LOW)
        keep_ref[...] = dot(normed_turned, joined_ref[:, half_of(mine, half)]).astype(LOW)
    bias_ref[0:1] = column_sums(joined_ref[:, :group].astype(WIDE))
    bias_ref[1:2] = column_sums(joined_ref[:, 2 * group :].astype(WIDE))
    back = 0.0
    for index, weight_ref in enumerate(weights):
        part = joined_ref[:, index * group : (index + 1) * group]
        back = back + dot(part, weight_ref[...], 1, 1)
    return back


def first_back_kernel(
    place_ref,
    normed_ref,
    dq_ref,
    own_ref,
    got_ref,
    wq_ref,
    wk_ref,
    wv_ref,
    *rest,
):
    send_ref, keep_ref, bias_ref, part_ref, turned_ref, joined_ref = rest[-6:]

    @pl.when(pl.program_id(0) == 0)
    def _():
        turned_ref[...] = normed_ref[...].astype(WIDE).T.astype(LOW)
        part_ref[...] = jnp.zeros_like(part_ref)

    part_ref[...] += project_back(
        place_ref,
        turned_ref[...],
        dq_ref,
        own_ref,
        got_ref,
        (wq_ref, wk_ref, wv_ref),
        joined_ref,
        send_ref,
        keep_ref,
        bias_ref,
    )


def last_back_kernel(
    groups,
    place_ref,
    normed_ref,
    dq_ref,
    own_ref,
    got_ref,
    wq_ref,
    wk_ref,
    wv_ref,
    part_ref,
    embedded_ref,
    g_residual_ref,
    gain_ref,
    prior_ref,
    expression_ref,
    bias_first_ref,
    vectors_ref,
    bias_up_ref,
    *rest,
):
    send_ref, keep_ref, g_low_ref = rest[-8:-5]
    turned_ref, joined_ref, bias_ref, rows_ref, owned_ref = rest[-5:]
    rows, width = normed_ref.shape
    half = width // 2
    mine = place_ref[0]
    turned_ref[...] = normed_ref[...].astype(WIDE).T.astype(LOW)
    back = part_ref[...] + project_back(
        place_ref,
        turned_ref[...],
        dq_ref,
        own_ref,
        got_ref,
        (wq_ref, wk_ref, wv_ref),
        joined_ref,
        None,
        None,
        bias_ref,
    )
    unit, scale = normalize(embedded_ref[...])
    g_embedded = g_residual_ref[...] + norm_back(back, unit, scale, gain_ref[...][None])
    g_low_ref[...] = g_embedded.astype(LOW)
    prior = prior_ref[...].astype(WIDE).T.astype(LOW)
    count = owned_ref.shape[0]
    share = width // count
    for out_ref, side in ((send_ref, 1 - mine), (keep_ref, mine)):
        know = dot(prior, g_low_ref[:, half_of(side, half)]).astype(LOW)
        project = dot(
            turned_ref[...], joined_ref[:, half_of(side, half)]
        ).astype(LOW)
        for owner in range(count):
            entry = slice(owner * share, (owner + 1) * share)
            out_ref[owner, :share, :half] = project[entry]
            out_ref[owner, :share, half:] = know[entry]
    expression = jnp.broadcast_to(expression_ref[...], (8, rows)).T[:, :1]
    total = column_sums(g_embedded)
    hot = lax.broadcasted_iota(jnp.int32, (groups, width), 0) == place_ref[3]
    rows_ref[:groups] = jnp.where(hot, total, 0.0)
    rows_ref[groups : groups + 16] = jnp.concatenate(
        [
            column_sums(expression * g_embedded),
            column_sums(back * unit),
            column_sums(back),
            jnp.concatenate([bias_first_ref[0, 0:1], bias_first_ref[1, 0:1], bias_ref[0:1]], 1),
            jnp.concatenate([bias_first_ref[0, 1:2], bias_first_ref[1, 1:2], bias_ref[1:2]], 1),
            vectors_ref[...],
            jnp.zeros((7, width), WIDE),
        ],
        0,
    )
    owned_ref[...] = jnp.zeros_like(owned_ref)
    for owner in range(count):
        columns = slice(owner * share, (owner + 1) * share)
        for start in range(0, groups + 16, 32):
            size = min(32, groups + 16 - start)
            lanes = slice(start * 4, start * 4 + share)
            owned_ref[owner, :size, lanes] = rows_ref[start : start + size, columns]
        at, lanes = groups % 32 + 9, slice(groups // 32 * 128, groups // 32 * 128 + share)
        for part in range(4):
            first = (owner * 4 + part) * share
            owned_ref[owner, at + part : at + part + 1, lanes] = bias_up_ref[
                :, first : first + share
            ]
    low = up16(share)
    for out_ref, side in ((send_ref, 1 - mine), (keep_ref, mine)):
        rows_in = pl.ds(pl.multiple_of(side * 16, 16), 16)
        out_ref[:, low : low + 16, :half] = owned_ref[:, rows_in, :].astype(LOW)


def back_specs(rows, width, group, first):
    third = width // group
    weight = lambda part: pl.BlockSpec((width, group), lambda j, _: (0, part * third + first + j))
    both = pl.BlockSpec((2, rows, group), lambda j, _: (0, 0, j))
    return [
        whole((rows, width)),
        pl.BlockSpec((rows, group), lambda j, _: (0, j)),
        both,
        both,
        weight(0),
        weight(1),
        weight(2),
    ]


def first_back(place, normed, dq, own, got, w_qkv, group, after):
    rows, width = normed.shape
    count = dq.shape[1] // group
    half = 3 * group // 2
    tile = pl.BlockSpec((width, half), lambda j, _: (0, j))
    return pl.pallas_call(
        first_back_kernel,
        grid_spec=pltpu.PrefetchScalarGridSpec(
            num_scalar_prefetch=1,
            grid=(count,),
            in_specs=back_specs(rows, width, group, 0) + unread(after),
            out_specs=[
                tile,
                tile,
                pl.BlockSpec((None, 2, group), lambda j, _: (j, 0, 0)),
                whole((rows, width)),
            ],
            scratch_shapes=[
                pltpu.VMEM((width, rows), LOW),
                pltpu.VMEM((rows, 3 * group), LOW),
            ],
        ),
        out_shape=[
            shaped((width, count * half), LOW),
            shaped((width, count * half), LOW),
            shaped((count, 2, group), WIDE),
            shaped((rows, width), WIDE),
        ],
        compiler_params=params(),
        cost_estimate=LONG,
        name="first_back",
    )(place, normed, dq, own, got, w_qkv, w_qkv, w_qkv, *after)


def last_back(
    place,
    normed,
    dq,
    own,
    got,
    w_qkv,
    group,
    part,
    embedded,
    g_residual,
    gain,
    prior,
    expression,
    bias_first,
    vectors,
    bias_up,
    groups,
    count,
    after,
):
    rows, width = normed.shape
    half = width // 2
    first = width // group - 1
    entry = up16(width // count) + 16
    return pl.pallas_call(
        functools.partial(last_back_kernel, groups),
        grid_spec=pltpu.PrefetchScalarGridSpec(
            num_scalar_prefetch=1,
            grid=(1,),
            in_specs=back_specs(rows, width, group, first)
            + [
                whole((rows, width)),
                whole((rows, width)),
                whole((rows, width)),
                whole((width,)),
                whole((rows, width)),
                whole((1, rows)),
                whole(bias_first.shape),
                whole((4, width)),
                whole(bias_up.shape),
            ]
            + unread(after),
            out_specs=[
                whole((count, entry, width)),
                whole((count, entry, width)),
                whole((rows, width)),
            ],
            scratch_shapes=[
                pltpu.VMEM((width, rows), LOW),
                pltpu.VMEM((rows, 3 * group), LOW),
                pltpu.VMEM((2, group), WIDE),
                pltpu.VMEM((groups + 16, width), WIDE),
                pltpu.VMEM((count, 32, 384), WIDE),
            ],
        ),
        out_shape=[
            shaped((count, entry, width), LOW),
            shaped((count, entry, width), LOW),
            shaped((rows, width), LOW),
        ],
        compiler_params=params(),
        cost_estimate=LONG,
        name="last_back",
    )(
        place,
        normed,
        dq,
        own,
        got,
        w_qkv,
        w_qkv,
        w_qkv,
        part,
        embedded,
        g_residual,
        gain,
        prior,
        expression,
        bias_first,
        vectors,
        bias_up,
        *after,
    )


def gene_kernel(slots_ref, ids_ref, grad_ref, *rest):
    out_ref = rest[-1]
    slots = slots_ref[...]
    rows = grad_ref.shape[0]
    picker = jnp.where(slots == jnp.broadcast_to(ids_ref[...], (slots.shape[0], rows)), 1.0, 0.0)
    out_ref[...] = dot(picker.astype(LOW), grad_ref[...]).astype(LOW)


def gene_rows(slots, ids, grad, after):
    count = slots.shape[0]
    rows, width = grad.shape
    tile = min(count, 1152)
    return pl.pallas_call(
        gene_kernel,
        grid=(count // tile,),
        in_specs=[
            pl.BlockSpec((tile, 1), lambda j: (j, 0)),
            whole((1, rows)),
            whole((rows, width)),
        ]
        + unread(after),
        out_specs=pl.BlockSpec((tile, width), lambda j: (j, 0)),
        out_shape=shaped((count, width), LOW),
        compiler_params=params(),
        cost_estimate=LONG,
        name="gene_rows",
    )(slots, ids, grad, *after)


def swap_cores(array):
    return lax.ppermute(array, "blk", [(0, 1), (1, 0)])


def bits_apart(array, mask):
    count = lax.axis_size("dp")
    return lax.ppermute(array, "dp", [(i, i ^ mask) for i in range(count)])


def pick(array, position, index):
    return lax.dynamic_index_in_dim(array, index, position, keepdims=False)


class Share:
    QUAD = "quad"

    def __init__(self, segments, route):
        self.bits = lax.axis_size("dp").bit_length() - 1
        self.route = list(route)
        self.rows = []
        self.sources = []
        dims = tuple(range(self.bits - 1, -1, -1))
        for arrays, blocks, *rows in segments:
            first, single = len(self.rows), len(blocks) == 1
            rows = rows[0] if rows else [(0, arrays[0].shape[1])] * len(blocks)
            self.rows += [size for _, size in rows]
            parts = [
                (first + at, rows[at][0], 0 if single else block * LANES)
                for at, block in enumerate(blocks)
            ]
            columns = LANES if single else arrays[0].shape[2]
            where, height = (0, blocks[0] if single else 0), arrays[0].shape[1]
            start, size = rows[0]
            if single and size % 16 == start % size == height % size == 0:
                where, height = (start // size, where[1]), size
                parts = [(first, 0, 0)]
            for array in arrays:
                shape = (2,) * self.bits + array.shape[1:]
                self.sources.append((array.reshape(shape), dims, where, (height, columns), parts))
        self.arriving = []
        self.fixed = ()
        self.settle_places()

    def join(self, other):
        shift = len(self.rows)
        moved = lambda sources: [
            source[:4] + ([(index + shift, row, column) for index, row, column in source[4]],)
            for source in sources
        ]
        self.rows = self.rows + other.rows
        self.sources += moved(other.sources)
        self.arriving += moved(other.arriving)
        self.settle_places()
        return self

    def settle_places(self):
        self.places, place = [], 0
        for rows in self.rows:
            self.places.append(place)
            place += up16(rows)
        self.height = self.places[-1] + self.rows[-1]

    def parts(self):
        return [(index, place, 0) for index, place in enumerate(self.places)]

    def targets(self):
        step = self.route[0]
        if step == self.QUAD:
            low, high = self.bits - 2, self.bits - 1
            return [{low: way & 1, high: way >> 1} for way in (1, 2, 3)]
        return [{step: 1}]

    def left(self, target=()):
        gone = self.fixed + tuple(target)
        return [bit for bit in range(self.bits - 1, -1, -1) if bit not in gone]

    def receive(self, targets, sent):
        self.route.pop(0)
        for target, array in zip(targets, sent):
            mask = sum(flip << bit for bit, flip in target.items())
            dims = tuple(self.left(target))
            self.arriving.append(
                (bits_apart(array, mask), dims, (0, 0), array.shape[-2:], self.parts())
            )
        self.fixed += tuple(targets[0])

    def arrived(self):
        self.sources, self.arriving = self.sources + self.arriving, []


SEND, SETTLE, FINISH = range(3)


def combine(place, shares, after, mode=SEND, last=None):
    operands, specs, plan, out_specs, out_shape = [], [], [], [], []
    steps = []
    top = shares[0].bits - 1
    halves = mode == SETTLE or (
        mode == SEND and not any(top in share.fixed or top in share.targets()[0] for share in shares)
    )
    for share in shares:
        if mode != SETTLE:
            share.arrived()
        targets = share.targets() if mode == SEND else [{}]
        steps.append(targets)
        left = share.left(targets[0]) if mode != FINISH else []
        quad = len(targets) > 1
        used = []
        for array, dims, block, size, parts in share.sources:
            shape, where, picked = [], [], []
            for bit in dims:
                free = bit in left or (quad and bit in targets[0])
                stepped = halves and bit == top
                shape.append(2 if free and not stepped else None)
                where.append(bit if stepped else None if free else (bit, targets[0].get(bit, 0)))
                if quad and bit in targets[0]:
                    picked.append(bit)

            def index(step, place, where=tuple(where), block=block):
                lead = []
                for at in where:
                    if at is None:
                        lead.append(0)
                    elif at == top:
                        lead.append(step)
                    else:
                        lead.append(1 - place[4 + at[0]] if at[1] else place[4 + at[0]])
                return tuple(lead) + block

            specs.append(pl.BlockSpec(tuple(shape) + tuple(size), index))
            used.append((len(operands), parts))
            operands.append(array)
        for target in targets:
            plan.append((share.rows, share.places, used, target if quad else {}))
            if mode != FINISH:
                shape = (2,) * len(left) + (share.height, LANES)
                if halves:
                    zeros = (0,) * (len(shape) - 1)
                    out_specs.append(
                        pl.BlockSpec(
                            (None,) + shape[1:], lambda step, _, zeros=zeros: (step,) + zeros
                        )
                    )
                else:
                    out_specs.append(whole(shape))
                out_shape.append(shaped(shape, LOW if mode == SEND else WIDE))
    for shape, _ in last or []:
        out_specs.append(whole(shape))
        out_shape.append(shaped(shape, WIDE))
    count = len(operands)

    def kernel(*refs):
        place_ref, sources, outs = refs[0], refs[1 : 1 + count], refs[1 + count + len(after) :]

        def summed(item, block):
            rows, _, used, target = plan[item]
            total = None
            way = tuple(
                1 - place_ref[4 + bit] if flip else place_ref[4 + bit]
                for bit, flip in sorted(target.items(), reverse=True)
            )
            for operand, parts in used:
                for index, row, column in parts:
                    if index == block:
                        ref = sources[operand]
                        spot = (slice(row, row + rows[block]), slice(column, column + LANES))
                        lead = way + (slice(None),) * (len(ref.shape) - 2 - len(way))
                        part = ref[lead + spot].astype(WIDE)
                        total = part if total is None else total + part
            return total

        if mode == FINISH:
            for (_, pieces), out in zip(last, outs):
                for item, block, row, column in pieces:
                    value = summed(item, block)
                    out[row : row + value.shape[0], column : column + LANES] = value
            return
        for item, out in enumerate(outs):
            for block, start in enumerate(plan[item][1]):
                value = summed(item, block)
                out[..., start : start + value.shape[-2], :] = value.astype(out.dtype)

    outs = pl.pallas_call(
        kernel,
        grid_spec=pltpu.PrefetchScalarGridSpec(
            num_scalar_prefetch=1,
            grid=(2 if halves else 1,),
            in_specs=specs + unread(after),
            out_specs=out_specs,
        ),
        out_shape=out_shape,
        compiler_params=params(),
        cost_estimate=LONG,
        name="combine",
    )(place, *operands, *after)
    taken = 0
    for share, targets in zip(shares, steps):
        if mode == SEND:
            share.receive(targets, outs[taken : taken + len(targets)])
        if mode == SETTLE:
            share.sources = [
                (outs[taken], tuple(share.left()), (0, 0), outs[taken].shape[-2:], share.parts())
            ]
        taken += len(targets)
    return outs


def assemble(place, own, other, shapes, pieces, small_row=None):
    def kernel(place_ref, own_ref, other_ref, *outs):
        first = place_ref[0] == 0

        def of_core(core, rows, columns):
            return jnp.where(first == (core == 0), own_ref[rows, columns], other_ref[rows, columns])

        for core, row, rows, column, columns, target, out_column in pieces:
            value = of_core(core, slice(row, row + rows), slice(column, column + columns))
            outs[target][:, out_column : out_column + columns] = value
        if small_row is None:
            outs[-1][...] = jnp.zeros_like(outs[-1])
            return
        group_ref, vector_refs, long_ref = outs[2], outs[3:-1], outs[-1]
        share, groups = group_ref.shape
        rows = slice(small_row, small_row + 16)
        for start in range(0, groups, 16):
            lanes = slice(start // 32 * 128, start // 32 * 128 + share)
            group_ref[:, start : start + 16] = of_core(start // 16 % 2, rows, lanes).T
        rest = of_core(0, rows, slice(groups // 32 * 128, groups // 32 * 128 + 128))
        for index, ref in enumerate(vector_refs):
            ref[...] = rest[index, :share]
        long_ref[...] = jnp.concatenate(
            [rest[9 + part : 10 + part, :share] for part in range(4)], 1
        )[0]

    return pl.pallas_call(
        kernel,
        grid_spec=pltpu.PrefetchScalarGridSpec(
            num_scalar_prefetch=1,
            grid=(1,),
            in_specs=[whole(own.shape), whole(own.shape)],
            out_specs=[whole(shape) for shape in shapes],
        ),
        out_shape=[shaped(shape, WIDE) for shape in shapes],
        compiler_params=params(),
        cost_estimate=LONG,
        name="assemble",
    )(place, own, other)


def body(
    gene_ids,
    values,
    knowledge,
    lengths,
    groups,
    gene_table,
    group_table,
    w_know,
    w_value,
    norm1_gain,
    norm1_bias,
    w_qkv,
    bias_q,
    bias_v,
    w_out,
    bias_out,
    norm2_gain,
    norm2_bias,
    w_up,
    bias_up,
    w_down,
    bias_down,
    cotangent,
):
    width = w_out.shape[0]
    units = w_up.shape[1]
    rows = gene_ids.shape[1]
    count = lax.axis_size("dp")
    mine = lax.axis_index("blk")
    length, group = lengths[0], groups[0]
    prior = knowledge[0]
    row = lambda vector: vector.reshape(1, -1)
    me = lax.axis_index("dp")
    bits = count.bit_length() - 1
    place = jnp.stack(
        [mine, length - mine * rows, length - (1 - mine) * rows, group]
        + [(me >> bit) & 1 for bit in range(bits)]
    ).astype(jnp.int32)
    if gene_table.shape[0] > 8 * rows:
        table = gene_table[gene_ids[0]]
    else:
        table = gene_table
    embedded, normed, kv_own = embed(
        place,
        gene_ids,
        values,
        prior,
        table,
        group_table,
        w_know,
        w_value,
        norm1_gain,
        norm1_bias,
        w_qkv,
        bias_v,
    )
    kv_other = swap_cores(kv_own)
    queries = project_queries(normed, w_qkv, bias_q)
    attended, probs, inverse = attend(place, queries, kv_own, kv_other)
    (
        block_output,
        residual,
        g_normed_two,
        up_send,
        up_keep,
        down_send,
        down_keep,
        bias_up_grad,
    ) = feed_forward(
        place,
        attended,
        embedded,
        cotangent[0],
        w_out,
        bias_out,
        norm2_gain,
        norm2_bias,
        w_up,
        row(bias_up),
        w_down,
        bias_down,
    )
    g_residual, g_attended, out_send, out_keep, vectors = branch_back(
        place,
        residual,
        g_normed_two,
        cotangent[0],
        attended,
        w_out,
        norm2_gain,
        [up_send, down_send],
    )

    owners = lambda array: array.reshape(count, -1, array.shape[-1])
    low_bits = list(range(bits - 2))
    turned = low_bits[1::-1] + low_bits[2:]
    quad, high_bits = [Share.QUAD], [bits - 2, bits - 1]
    up_terms = [owners(up_keep), owners(swap_cores(up_send))]
    blocks = units // 2 // LANES
    out_terms = [owners(out_keep), owners(swap_cores(out_send))]
    down_terms = [owners(down_keep), owners(swap_cores(down_send))]
    high, share = units // count, width // count
    out_cut = min(share, up16(2 * share // 3))
    out_rest = [(out_terms, [0], [(out_cut, share - out_cut)])] if out_cut < share else []
    early = [
        Share([(down_terms, [0]), (out_terms, [0], [(0, out_cut)])], low_bits + quad),
        Share([(up_terms, list(range(blocks)))] + out_rest, turned + quad),
    ]
    token = combine(place, early, [])
    dq1, own1, other1 = attend_back(
        queries, kv_own, kv_other, attended, g_attended, probs, inverse, 0, 4, token
    )
    got1 = swap_cores(other1)
    dq2, own2, other2 = attend_back(
        queries, kv_own, kv_other, attended, g_attended, probs, inverse, 4, 2, [dq1]
    )
    got2 = swap_cores(other2)
    qkv_send, qkv_keep, bias_first, part = first_back(
        place, normed, dq1, own1, got1, w_qkv, 256, [dq2]
    )
    qkv = [owners(qkv_keep), owners(swap_cores(qkv_send))]
    project = Share([(qkv, [0, 1])], high_bits + low_bits)
    token = [part, qkv_send]
    for bit in low_bits[1:]:
        token = combine(place, early + [project] * (bit == low_bits[-1]), token)
    early = [early[0].join(early[1])]
    tail_send, tail_keep, g_low = last_back(
        place,
        normed,
        dq2,
        own2,
        got2,
        w_qkv,
        256,
        part,
        embedded,
        g_residual,
        norm1_gain,
        prior,
        values,
        bias_first,
        vectors,
        bias_up_grad,
        group_table.shape[0],
        count,
        token,
    )
    slot = jnp.arange(count * VOC_DEV, dtype=jnp.int32)[:, None]
    slot = slot + slot // VOC_DEV * VOC_DEV
    gene_send = gene_rows(slot + (1 - mine) * VOC_DEV, gene_ids, g_low, [tail_send])
    gene_got = swap_cores(gene_send)
    gene_keep = gene_rows(slot + mine * VOC_DEV, gene_ids, g_low, [gene_send])
    tail = [tail_keep, swap_cores(tail_send)]
    gene = [owners(gene_keep), owners(gene_got)]
    small_at = up16(share)
    late = [
        Share([(tail, [0], [(0, share)]), (gene, [0])], low_bits + quad),
        Share(
            [(tail, [1], [(0, share)]), (tail, [0], [(small_at, 16)]), (gene, [1])], turned + quad
        ),
    ]
    token = combine(place, [project], [gene_keep])
    token = combine(place, late, token)
    token = combine(place, early, token)
    for _ in low_bits[1:]:
        token = combine(place, late + [project], token)
    token = combine(place, late, token, SETTLE)
    late = [late[0].join(late[1]), project]
    step = up16(share)
    layout = [(0, 0, 0, 0), (0, 1, high + blocks * step, 0)]
    if out_rest:
        layout.append((0, 2 + blocks, high + blocks * step + out_cut, 0))
    layout += [(0, 2 + block, high + block * step, 0) for block in range(blocks)]
    (own,) = combine(place, early, token, FINISH, [((high + (blocks + 1) * step, LANES), layout)])
    other = swap_cores(own)
    combine(place, late, [own])
    pieces = []
    for core in range(2):
        pieces.append((core, 0, high, 0, LANES, 0, core * LANES))
        for block in range(blocks):
            place_in = (core * blocks + block) * LANES
            pieces.append((core, high + block * step, share, 0, LANES, 1, place_in))
        pieces.append((core, high + blocks * step, share, 0, LANES, 2, core * LANES))
    w_down_share, w_up_share, w_out_share, done = assemble(
        place, own, other, [(high, width), (share, units), (share, width), (8, 128)], pieces
    )
    layout = [(1, 0, 0, 0), (1, 1, step, 0), (0, 0, 2 * step, 0), (0, 2, 3 * step, 0)]
    layout += [(0, 3, 4 * step, 0)]
    own, gene_grad = combine(
        place,
        late,
        [done],
        FINISH,
        [
            ((4 * step + 16, LANES), layout),
            ((VOC_DEV, width), [(0, 1, 0, 0), (0, 4, 0, LANES)]),
        ],
    )
    other = swap_cores(own)
    pieces = []
    for block in range(3):
        at = block * step
        pieces.append((0, at, share, 0, 256, 0, block * 256))
        pieces.append((0, at, share, 256, 128, 0, width + block * 256))
        pieces.append((1, at, share, 0, 128, 0, width + block * 256 + 128))
        pieces.append((1, at, share, 128, 256, 0, 2 * width + block * 256))
    for core in range(2):
        pieces.append((core, 3 * step, share, 0, LANES, 1, core * LANES))
    w_qkv_share, w_know_share, group_share, *extra, bias_up_share = assemble(
        place,
        own,
        other,
        [(share, 3 * width), (share, width), (share, group_table.shape[0])]
        + [(share,)] * 9
        + [(units // count,)],
        pieces,
        4 * step,
    )
    return (
        block_output[None],
        gene_grad,
        group_share.T,
        w_know_share,
        extra[0],
        extra[1],
        extra[2],
        w_qkv_share,
        extra[3],
        extra[4],
        w_out_share,
        extra[5],
        extra[6],
        extra[7],
        w_up_share,
        bias_up_share,
        w_down_share,
        extra[8],
    )


def solution(mesh):
    in_specs = (
        P("dp", "blk"),
        P("dp", "blk"),
        P("dp", "blk", None),
        P("dp"),
        P("dp"),
        P(),
        P(),
        P(),
        P(),
        P(),
        P(),
        P(),
        P(),
        P(),
        P(),
        P(),
        P(),
        P(),
        P(),
        P(),
        P(),
        P(),
        P("dp", "blk", None),
    )
    out_specs = (
        P("dp", "blk", None),
        P(("dp", "blk"), None),
        P(None, "dp"),
        P("dp", None),
        P("dp"),
        P("dp"),
        P("dp"),
        P("dp", None),
        P("dp"),
        P("dp"),
        P("dp", None),
        P("dp"),
        P("dp"),
        P("dp"),
        P("dp", None),
        P("dp"),
        P("dp", None),
        P("dp"),
    )
    return jax.shard_map(body, mesh=mesh, in_specs=in_specs, out_specs=out_specs, check_vma=False)
```

```python
import functools

import jax
import jax.numpy as jnp
from jax import lax
from jax.experimental import pallas as pl
from jax.experimental.pallas import tpu as pltpu
from jax.sharding import PartitionSpec as P

HEAD_DIM = 64
VOC_DEV = 72
EPSILON = 1e-05
LANES = 384
LOW = jnp.bfloat16
WIDE = jnp.float32
GRANT = 44 << 20


LONG = pl.CostEstimate(flops=10**12, bytes_accessed=1, transcendentals=0)


def dot(left, right, left_dim=1, right_dim=0):
    return lax.dot_general(
        left, right, (((left_dim,), (right_dim,)), ((), ())), preferred_element_type=WIDE
    )


def column_sums(array):
    return jnp.sum(array, 0, keepdims=True)


def row_means(array):
    return jnp.mean(array, -1, keepdims=True)


def normalize(array):
    center = array - row_means(array)
    scale = lax.rsqrt(row_means(center * center) + EPSILON)
    return center * scale, scale


def norm_back(grad, unit, scale, gain):
    inner = grad * gain
    return scale * (inner - row_means(inner) - unit * row_means(inner * unit))


def half_of(index, half):
    return pl.ds(pl.multiple_of(index * half, 128), half)


def whole(shape):
    return pl.BlockSpec(shape, lambda *_: (0,) * len(shape))


def up16(rows):
    return -(-rows // 16) * 16


def unread(arrays):
    return [pl.BlockSpec(memory_space=pl.ANY)] * len(arrays)


def params(grant=GRANT):
    return pltpu.CompilerParams(vmem_limit_bytes=grant)


def shaped(shape, dtype):
    return jax.ShapeDtypeStruct(shape, dtype)


def embed_kernel(
    place_ref,
    ids_ref,
    expression_ref,
    prior_ref,
    table_ref,
    group_ref,
    w_know_ref,
    w_value_ref,
    gain_ref,
    offset_ref,
    w_key_ref,
    w_val_ref,
    bias_val_ref,
    embedded_ref,
    normed_ref,
    kv_ref,
):
    rows, width = prior_ref.shape
    embedded = dot(prior_ref[...], w_know_ref[...])
    if table_ref.shape[0] == rows:
        gathered = table_ref[...].astype(WIDE)
    else:
        ids = jnp.broadcast_to(ids_ref[...], (8, rows)).T[:, :1]
        slots = lax.broadcasted_iota(jnp.int32, (rows, table_ref.shape[0]), 1)
        picker = jnp.where(slots == ids, 1.0, 0.0).astype(LOW)
        gathered = dot(picker, table_ref[...])
    expression = jnp.broadcast_to(expression_ref[...], (8, rows)).T[:, :1]
    groups = lax.broadcasted_iota(jnp.int32, (8, group_ref.shape[0]), 1)
    group_row = dot(jnp.where(groups == place_ref[3], 1.0, 0.0).astype(LOW), group_ref[...])[:1]
    embedded = gathered + group_row + expression * w_value_ref[...][None] + embedded
    embedded_ref[...] = embedded
    unit, _ = normalize(embedded)
    normed = (unit * gain_ref[...][None] + offset_ref[...][None]).astype(LOW)
    normed_ref[...] = normed
    kv_ref[:, :width] = dot(normed, w_key_ref[...]).astype(LOW)
    kv_ref[:, width:] = (dot(normed, w_val_ref[...]) + bias_val_ref[...][None]).astype(LOW)


def embed(
    place, ids, expression, prior, table, group_table, w_know, w_value, gain, offset, w_qkv, bias_v
):
    rows, width = prior.shape
    columns = lambda index: pl.BlockSpec((width, width), lambda *_: (0, index))
    return pl.pallas_call(
        embed_kernel,
        grid_spec=pltpu.PrefetchScalarGridSpec(
            num_scalar_prefetch=1,
            grid=(1,),
            in_specs=[
                whole((1, rows)),
                whole((1, rows)),
                whole((rows, width)),
                whole(table.shape),
                whole(group_table.shape),
                whole((width, width)),
                whole((width,)),
                whole((width,)),
                whole((width,)),
                columns(1),
                columns(2),
                whole((width,)),
            ],
            out_specs=[whole((rows, width)), whole((rows, width)), whole((rows, 2 * width))],
        ),
        out_shape=[
            shaped((rows, width), WIDE),
            shaped((rows, width), LOW),
            shaped((rows, 2 * width), LOW),
        ],
        compiler_params=params(60 << 20),
        name="embed",
    )(
        place,
        ids,
        expression,
        prior,
        table,
        group_table,
        w_know,
        w_value,
        gain,
        offset,
        w_qkv,
        w_qkv,
        bias_v,
    )


def query_kernel(normed_ref, w_query_ref, bias_ref, out_ref):
    out_ref[...] = (dot(normed_ref[...], w_query_ref[...]) + bias_ref[...][None]).astype(LOW)


def project_queries(normed, w_qkv, bias_q):
    rows, width = normed.shape
    return pl.pallas_call(
        query_kernel,
        grid=(1,),
        in_specs=[whole((rows, width)), whole((width, width)), whole((width,))],
        out_specs=whole((rows, width)),
        out_shape=shaped((rows, width), LOW),
        compiler_params=params(),
        cost_estimate=pl.CostEstimate(
            flops=2 * rows * width * width, bytes_accessed=4 * rows * width, transcendentals=0
        ),
        name="queries",
    )(normed, w_qkv, bias_q)


def attend_kernel(place_ref, q_ref, ko_ref, vo_ref, kr_ref, vr_ref, out_ref, p_ref, c_ref):
    rows = q_ref.shape[0]
    lane = lax.broadcasted_iota(jnp.int32, (rows, 128), 1)
    place = lax.broadcasted_iota(jnp.int32, (rows, 128), 0)
    queries = q_ref[...] * LOW(HEAD_DIM**-0.5)
    halves = []
    for index, k_ref in enumerate((ko_ref, kr_ref)):
        dead = jnp.where(place < place_ref[1 + index], 0.0, -1e30).astype(LOW)
        halves.append((k_ref[...], dead))
    values = [vo_ref[...].T, vr_ref[...].T]
    ones = jnp.ones((16, rows), LOW)
    scored, outs = [], []
    for head in range(2):
        inside = (lane < HEAD_DIM) if head == 0 else (lane >= HEAD_DIM)
        spare = HEAD_DIM * (1 - head)
        asked = jnp.where(inside, queries, jnp.where(lane == spare, 1.0, 0.0).astype(LOW))
        scored.append(
            [dot(jnp.where(lane == spare, dead, keys), asked, 1, 1) for keys, dead in halves]
        )
    for head in range(2):
        scores = scored[head]
        top = jnp.maximum(*[jnp.max(part, 0, keepdims=True) for part in scores])
        mixed = 0.0
        for index in range(2):
            low = jnp.exp(scores[index] - top).astype(LOW)
            p_ref[head, index * rows : (index + 1) * rows, :] = low
            own = values[index][head * HEAD_DIM : (head + 1) * HEAD_DIM]
            mixed = mixed + dot(jnp.concatenate([own, ones], 0), low)
        inverse = 1.0 / mixed[HEAD_DIM : HEAD_DIM + 1]
        c_ref[0, head : head + 1, :] = inverse
        outs.append(mixed[:HEAD_DIM] * inverse)
    out_ref[...] = jnp.concatenate(outs, 0).T.astype(LOW)


def attend(place, queries, kv_own, kv_other):
    rows, width = queries.shape
    pairs = width // 128
    block = lambda shift: pl.BlockSpec((rows, 128), lambda j, _: (0, shift + j))
    return pl.pallas_call(
        attend_kernel,
        grid_spec=pltpu.PrefetchScalarGridSpec(
            num_scalar_prefetch=1,
            grid=(pairs,),
            in_specs=[block(0), block(0), block(pairs), block(0), block(pairs)],
            out_specs=[
                block(0),
                pl.BlockSpec((2, 2 * rows, rows), lambda j, _: (j, 0, 0)),
                pl.BlockSpec((1, 2, rows), lambda j, _: (j, 0, 0)),
            ],
        ),
        out_shape=[
            shaped((rows, width), LOW),
            shaped((2 * pairs, 2 * rows, rows), LOW),
            shaped((pairs, 2, rows), WIDE),
        ],
        compiler_params=params(),
        cost_estimate=pl.CostEstimate(
            flops=16 * rows * rows * width,
            bytes_accessed=8 * rows * rows * pairs,
            transcendentals=4 * rows * rows * pairs,
        ),
        name="attend",
    )(place, queries, kv_own, kv_own, kv_other, kv_other)


def attend_back_kernel(
    q_ref,
    ko_ref,
    vo_ref,
    kr_ref,
    vr_ref,
    a_ref,
    g_ref,
    p_ref,
    c_ref,
    *rest,
):
    dq_ref, dkvo_ref, dkvr_ref = rest[-3:]
    rows = q_ref.shape[0]
    lane = lax.broadcasted_iota(jnp.int32, (rows, 128), 1)
    mixed = a_ref[...].astype(WIDE).T
    grad = g_ref[...].astype(WIDE).T
    grad = jnp.concatenate(
        [grad[:HEAD_DIM] * c_ref[0, :1, :], grad[HEAD_DIM:] * c_ref[0, 1:, :]], 0
    )
    inner = grad * mixed
    inner = [column_sums(inner[:HEAD_DIM]), column_sums(inner[HEAD_DIM:])]
    first = lax.broadcasted_iota(jnp.int32, (128, rows), 0) < HEAD_DIM
    low = grad.astype(LOW)
    masked = [
        jnp.where(first, low, jnp.zeros_like(low)),
        jnp.where(first, jnp.zeros_like(low), low),
    ]
    grad_rows = grad.T.astype(LOW)
    queries = q_ref[...]
    parts = [0.0, 0.0]
    for index, (k_ref, v_ref, out_ref) in enumerate(
        ((ko_ref, vo_ref, dkvo_ref), (kr_ref, vr_ref, dkvr_ref))
    ):
        keys = k_ref[...].T
        values = v_ref[...]
        key_grads, val_grads = [], []
        for head in range(2):
            probs = p_ref[head, index * rows : (index + 1) * rows, :]
            wide = dot(values, masked[head]) - inner[head]
            score = (probs.astype(WIDE) * wide).astype(LOW)
            val_grads.append(dot(probs, grad_rows))
            key_grads.append(dot(score, queries))
            parts[head] = parts[head] + dot(keys[head * HEAD_DIM : (head + 1) * HEAD_DIM], score)
        chosen = lane < HEAD_DIM
        out_ref[0] = (jnp.where(chosen, *key_grads) * HEAD_DIM**-0.5).astype(LOW)
        out_ref[1] = jnp.where(chosen, *val_grads).astype(LOW)
    dq_ref[...] = (jnp.concatenate(parts, 0).T * HEAD_DIM**-0.5).astype(LOW)


def attend_back(queries, kv_own, kv_other, attended, grad, probs, inverse, start, count, after):
    rows, width = queries.shape
    pairs = width // 128
    block = lambda shift: pl.BlockSpec((rows, 128), lambda j: (0, shift + j))
    near, far = block(start), block(pairs + start)
    both = pl.BlockSpec((2, rows, 128), lambda j: (0, 0, j))
    return pl.pallas_call(
        attend_back_kernel,
        grid=(count,),
        in_specs=[
            near,
            near,
            far,
            near,
            far,
            near,
            near,
            pl.BlockSpec((2, 2 * rows, rows), lambda j: (start + j, 0, 0)),
            pl.BlockSpec((1, 2, rows), lambda j: (start + j, 0, 0)),
        ]
        + unread(after),
        out_specs=[block(0), both, both],
        out_shape=[
            shaped((rows, 128 * count), LOW),
            shaped((2, rows, 128 * count), LOW),
            shaped((2, rows, 128 * count), LOW),
        ],
        compiler_params=params(),
        cost_estimate=LONG,
        name="attend_back",
    )(queries, kv_own, kv_own, kv_other, kv_other, attended, grad, probs, inverse, *after)


def ffn_kernel(
    place_ref,
    attended_ref,
    embedded_ref,
    cotangent_ref,
    w_out_ref,
    bias_out_ref,
    gain_ref,
    offset_ref,
    w_up_ref,
    bias_up_ref,
    w_down_ref,
    bias_down_ref,
    output_ref,
    residual_ref,
    g_normed_ref,
    up_send_ref,
    up_keep_ref,
    down_send_ref,
    down_keep_ref,
    bias_up_grad_ref,
    normed_ref,
    total_ref,
    g_out_ref,
    g_halves_ref,
):
    step, steps = pl.program_id(0), pl.num_programs(0)
    rows, width = attended_ref.shape
    half = width // 2
    mine = place_ref[0]
    alive = lax.broadcasted_iota(jnp.int32, (rows, 1), 0) < place_ref[1]

    @pl.when(step == 0)
    def _():
        residual = embedded_ref[...] + (
            dot(attended_ref[...], w_out_ref[...]) + bias_out_ref[...][None]
        )
        residual_ref[...] = residual
        unit, _ = normalize(residual)
        normed_ref[...] = (unit * gain_ref[...][None] + offset_ref[...][None]).astype(LOW)
        g_out_ref[...] = jnp.where(alive, cotangent_ref[...].astype(WIDE), 0.0).astype(LOW)
        g_halves_ref[:, :half] = g_out_ref[:, half_of(1 - mine, half)]
        g_halves_ref[:, half:] = g_out_ref[:, half_of(mine, half)]
        total_ref[...] = jnp.zeros_like(total_ref)
        g_normed_ref[...] = jnp.zeros_like(g_normed_ref)

    hidden = dot(normed_ref[...], w_up_ref[...]) + bias_up_ref[...]
    g_act = dot(g_out_ref[...], w_down_ref[...], 1, 1)
    share = 0.5 * (1.0 + lax.erf(hidden * 0.5**0.5))
    density = jnp.exp(-0.5 * hidden * hidden) * 0.3989422804014327
    activated = (hidden * share).astype(LOW)
    g_hidden = (g_act * (share + hidden * density)).astype(LOW)
    total_ref[...] += dot(activated, w_down_ref[...])
    g_normed_ref[...] += dot(g_hidden, w_up_ref[...], 1, 1)
    down = dot(activated, g_halves_ref[...], 0, 0).astype(LOW)
    down_send_ref[...] = down[:, :half]
    down_keep_ref[...] = down[:, half:]
    up = dot(normed_ref[...], g_hidden, 0, 0).astype(LOW)
    bias_up_grad_ref[...] = column_sums(g_hidden.astype(WIDE))

    @pl.when(step < steps // 2)
    def _():
        up_send_ref[...] = up

    @pl.when(step >= steps // 2)
    def _():
        up_keep_ref[...] = up

    @pl.when(step == steps - 1)
    def _():
        final = residual_ref[...] + (total_ref[...] + bias_down_ref[...][None])
        output_ref[...] = jnp.where(alive, final, 0.0).astype(LOW)


def feed_forward(
    place,
    attended,
    embedded,
    cotangent,
    w_out,
    bias_out,
    gain,
    offset,
    w_up,
    bias_up,
    w_down,
    bias_down,
):
    rows, width = attended.shape
    units = w_up.shape[1]
    tile = 768
    steps = units // tile
    turn = lambda j, place: lax.rem(j + (1 - place[0]) * (steps // 2), steps)
    down_tile = pl.BlockSpec((tile, width // 2), lambda j, place: (turn(j, place), 0))
    return pl.pallas_call(
        ffn_kernel,
        grid_spec=pltpu.PrefetchScalarGridSpec(
            num_scalar_prefetch=1,
            grid=(steps,),
            in_specs=[
                whole((rows, width)),
                whole((rows, width)),
                whole((rows, width)),
                whole((width, width)),
                whole((width,)),
                whole((width,)),
                whole((width,)),
                pl.BlockSpec((width, tile), lambda j, place: (0, turn(j, place))),
                pl.BlockSpec((1, tile), lambda j, place: (0, turn(j, place))),
                pl.BlockSpec((tile, width), lambda j, place: (turn(j, place), 0)),
                whole((width,)),
            ],
            out_specs=[
                whole((rows, width)),
                whole((rows, width)),
                whole((rows, width)),
                pl.BlockSpec((width, tile), lambda j, _: (0, jnp.minimum(j, steps // 2 - 1))),
                pl.BlockSpec((width, tile), lambda j, _: (0, jnp.maximum(j - steps // 2, 0))),
                down_tile,
                down_tile,
                pl.BlockSpec((1, tile), lambda j, place: (0, turn(j, place))),
            ],
            scratch_shapes=[
                pltpu.VMEM((rows, width), LOW),
                pltpu.VMEM((rows, width), WIDE),
                pltpu.VMEM((rows, width), LOW),
                pltpu.VMEM((rows, width), LOW),
            ],
        ),
        out_shape=[
            shaped((rows, width), LOW),
            shaped((rows, width), WIDE),
            shaped((rows, width), WIDE),
            shaped((width, units // 2), LOW),
            shaped((width, units // 2), LOW),
            shaped((units, width // 2), LOW),
            shaped((units, width // 2), LOW),
            shaped((1, units), WIDE),
        ],
        compiler_params=params(),
        cost_estimate=LONG,
        name="feed_forward",
    )(
        place,
        attended,
        embedded,
        cotangent,
        w_out,
        bias_out,
        gain,
        offset,
        w_up,
        bias_up,
        w_down,
        bias_down,
    )


def branch_kernel(
    place_ref,
    residual_ref,
    g_normed_ref,
    cotangent_ref,
    attended_ref,
    w_out_ref,
    gain_ref,
    *rest,
):
    g_residual_ref, g_attended_ref, out_send_ref, out_keep_ref, vectors_ref, total_ref = rest[-6:]
    step, steps = pl.program_id(0), pl.num_programs(0)
    rows, width = residual_ref.shape
    half = width // 2
    mine = place_ref[0]
    alive = step * rows + lax.broadcasted_iota(jnp.int32, (rows, 1), 0) < place_ref[1]

    @pl.when(step == 0)
    def _():
        total_ref[...] = jnp.zeros_like(total_ref)
        vectors_ref[...] = jnp.zeros_like(vectors_ref)

    unit, scale = normalize(residual_ref[...])
    g_final = jnp.where(alive, cotangent_ref[...].astype(WIDE), 0.0)
    g_normed = g_normed_ref[...]
    g_residual = g_final + norm_back(g_normed, unit, scale, gain_ref[...][None])
    g_residual_ref[...] = g_residual
    g_branch = g_residual.astype(LOW)
    g_attended_ref[...] = dot(g_branch, w_out_ref[...], 1, 1).astype(LOW)
    total_ref[...] += dot(attended_ref[...], g_branch, 0, 0)
    vectors_ref[...] += jnp.concatenate(
        [
            column_sums(g_branch.astype(WIDE)),
            column_sums(g_normed * unit),
            column_sums(g_normed),
            column_sums(g_final),
        ],
        0,
    )

    @pl.when(step == steps - 1)
    def _():
        out_send_ref[...] = total_ref[:, half_of(1 - mine, half)].astype(LOW)
        out_keep_ref[...] = total_ref[:, half_of(mine, half)].astype(LOW)


def branch_back(place, residual, g_normed, cotangent, attended, w_out, gain, after):
    rows, width = residual.shape
    steps = 2
    tile = pl.BlockSpec((rows // steps, width), lambda j, _: (j, 0))
    return pl.pallas_call(
        branch_kernel,
        grid_spec=pltpu.PrefetchScalarGridSpec(
            num_scalar_prefetch=1,
            grid=(steps,),
            in_specs=[tile, tile, tile, tile, whole((width, width)), whole((width,))]
            + unread(after),
            out_specs=[
                tile,
                tile,
                whole((width, width // 2)),
                whole((width, width // 2)),
                whole((4, width)),
            ],
            scratch_shapes=[pltpu.VMEM((width, width), WIDE)],
        ),
        out_shape=[
            shaped((rows, width), WIDE),
            shaped((rows, width), LOW),
            shaped((width, width // 2), LOW),
            shaped((width, width // 2), LOW),
            shaped((4, width), WIDE),
        ],
        compiler_params=params(),
        cost_estimate=LONG,
        name="branch_back",
    )(place, residual, g_normed, cotangent, attended, w_out, gain, *after)


def project_back(place_ref, normed_turned, dq_ref, own_ref, got_ref, weights, joined_ref, send_ref, keep_ref, bias_ref):
    group = dq_ref.shape[1]
    half = 3 * group // 2
    mine = place_ref[0]
    joined_ref[:, :group] = dq_ref[...]
    for index in range(2):
        total = own_ref[index].astype(WIDE) + got_ref[index].astype(WIDE)
        joined_ref[:, (1 + index) * group : (2 + index) * group] = total.astype(LOW)
    if send_ref is not None:
        send_ref[...] = dot(normed_turned, joined_ref[:, half_of(1 - mine, half)]).astype(LOW)
        keep_ref[...] = dot(normed_turned, joined_ref[:, half_of(mine, half)]).astype(LOW)
    bias_ref[0:1] = column_sums(joined_ref[:, :group].astype(WIDE))
    bias_ref[1:2] = column_sums(joined_ref[:, 2 * group :].astype(WIDE))
    back = 0.0
    for index, weight_ref in enumerate(weights):
        part = joined_ref[:, index * group : (index + 1) * group]
        back = back + dot(part, weight_ref[...], 1, 1)
    return back


def first_back_kernel(
    place_ref,
    normed_ref,
    dq_ref,
    own_ref,
    got_ref,
    wq_ref,
    wk_ref,
    wv_ref,
    *rest,
):
    send_ref, keep_ref, bias_ref, part_ref, turned_ref, joined_ref = rest[-6:]

    @pl.when(pl.program_id(0) == 0)
    def _():
        turned_ref[...] = normed_ref[...].astype(WIDE).T.astype(LOW)
        part_ref[...] = jnp.zeros_like(part_ref)

    part_ref[...] += project_back(
        place_ref,
        turned_ref[...],
        dq_ref,
        own_ref,
        got_ref,
        (wq_ref, wk_ref, wv_ref),
        joined_ref,
        send_ref,
        keep_ref,
        bias_ref,
    )


def last_back_kernel(
    groups,
    place_ref,
    normed_ref,
    dq_ref,
    own_ref,
    got_ref,
    wq_ref,
    wk_ref,
    wv_ref,
    part_ref,
    embedded_ref,
    g_residual_ref,
    gain_ref,
    prior_ref,
    expression_ref,
    bias_first_ref,
    vectors_ref,
    bias_up_ref,
    *rest,
):
    send_ref, keep_ref, g_low_ref = rest[-8:-5]
    turned_ref, joined_ref, bias_ref, rows_ref, owned_ref = rest[-5:]
    rows, width = normed_ref.shape
    half = width // 2
    mine = place_ref[0]
    turned_ref[...] = normed_ref[...].astype(WIDE).T.astype(LOW)
    back = part_ref[...] + project_back(
        place_ref,
        turned_ref[...],
        dq_ref,
        own_ref,
        got_ref,
        (wq_ref, wk_ref, wv_ref),
        joined_ref,
        None,
        None,
        bias_ref,
    )
    unit, scale = normalize(embedded_ref[...])
    g_embedded = g_residual_ref[...] + norm_back(back, unit, scale, gain_ref[...][None])
    g_low_ref[...] = g_embedded.astype(LOW)
    prior = prior_ref[...].astype(WIDE).T.astype(LOW)
    count = owned_ref.shape[0]
    share = width // count
    for out_ref, side in ((send_ref, 1 - mine), (keep_ref, mine)):
        know = dot(prior, g_low_ref[:, half_of(side, half)]).astype(LOW)
        project = dot(
            turned_ref[...], joined_ref[:, half_of(side, half)]
        ).astype(LOW)
        for owner in range(count):
            entry = slice(owner * share, (owner + 1) * share)
            out_ref[owner, :share, :half] = project[entry]
            out_ref[owner, :share, half:] = know[entry]
    expression = jnp.broadcast_to(expression_ref[...], (8, rows)).T[:, :1]
    total = column_sums(g_embedded)
    hot = lax.broadcasted_iota(jnp.int32, (groups, width), 0) == place_ref[3]
    rows_ref[:groups] = jnp.where(hot, total, 0.0)
    rows_ref[groups : groups + 16] = jnp.concatenate(
        [
            column_sums(expression * g_embedded),
            column_sums(back * unit),
            column_sums(back),
            jnp.concatenate([bias_first_ref[0, 0:1], bias_first_ref[1, 0:1], bias_ref[0:1]], 1),
            jnp.concatenate([bias_first_ref[0, 1:2], bias_first_ref[1, 1:2], bias_ref[1:2]], 1),
            vectors_ref[...],
            jnp.zeros((7, width), WIDE),
        ],
        0,
    )
    owned_ref[...] = jnp.zeros_like(owned_ref)
    for owner in range(count):
        columns = slice(owner * share, (owner + 1) * share)
        for start in range(0, groups + 16, 32):
            size = min(32, groups + 16 - start)
            lanes = slice(start * 4, start * 4 + share)
            owned_ref[owner, :size, lanes] = rows_ref[start : start + size, columns]
        at, lanes = groups % 32 + 9, slice(groups // 32 * 128, groups // 32 * 128 + share)
        for part in range(4):
            first = (owner * 4 + part) * share
            owned_ref[owner, at + part : at + part + 1, lanes] = bias_up_ref[
                :, first : first + share
            ]
    low = up16(share)
    for out_ref, side in ((send_ref, 1 - mine), (keep_ref, mine)):
        rows_in = pl.ds(pl.multiple_of(side * 16, 16), 16)
        out_ref[:, low : low + 16, :half] = owned_ref[:, rows_in, :].astype(LOW)


def back_specs(rows, width, group, first):
    third = width // group
    weight = lambda part: pl.BlockSpec((width, group), lambda j, _: (0, part * third + first + j))
    both = pl.BlockSpec((2, rows, group), lambda j, _: (0, 0, j))
    return [
        whole((rows, width)),
        pl.BlockSpec((rows, group), lambda j, _: (0, j)),
        both,
        both,
        weight(0),
        weight(1),
        weight(2),
    ]


def first_back(place, normed, dq, own, got, w_qkv, group, after):
    rows, width = normed.shape
    count = dq.shape[1] // group
    half = 3 * group // 2
    tile = pl.BlockSpec((width, half), lambda j, _: (0, j))
    return pl.pallas_call(
        first_back_kernel,
        grid_spec=pltpu.PrefetchScalarGridSpec(
            num_scalar_prefetch=1,
            grid=(count,),
            in_specs=back_specs(rows, width, group, 0) + unread(after),
            out_specs=[
                tile,
                tile,
                pl.BlockSpec((None, 2, group), lambda j, _: (j, 0, 0)),
                whole((rows, width)),
            ],
            scratch_shapes=[
                pltpu.VMEM((width, rows), LOW),
                pltpu.VMEM((rows, 3 * group), LOW),
            ],
        ),
        out_shape=[
            shaped((width, count * half), LOW),
            shaped((width, count * half), LOW),
            shaped((count, 2, group), WIDE),
            shaped((rows, width), WIDE),
        ],
        compiler_params=params(),
        cost_estimate=LONG,
        name="first_back",
    )(place, normed, dq, own, got, w_qkv, w_qkv, w_qkv, *after)


def last_back(
    place,
    normed,
    dq,
    own,
    got,
    w_qkv,
    group,
    part,
    embedded,
    g_residual,
    gain,
    prior,
    expression,
    bias_first,
    vectors,
    bias_up,
    groups,
    count,
    after,
):
    rows, width = normed.shape
    half = width // 2
    first = width // group - 1
    entry = up16(width // count) + 16
    return pl.pallas_call(
        functools.partial(last_back_kernel, groups),
        grid_spec=pltpu.PrefetchScalarGridSpec(
            num_scalar_prefetch=1,
            grid=(1,),
            in_specs=back_specs(rows, width, group, first)
            + [
                whole((rows, width)),
                whole((rows, width)),
                whole((rows, width)),
                whole((width,)),
                whole((rows, width)),
                whole((1, rows)),
                whole(bias_first.shape),
                whole((4, width)),
                whole(bias_up.shape),
            ]
            + unread(after),
            out_specs=[
                whole((count, entry, width)),
                whole((count, entry, width)),
                whole((rows, width)),
            ],
            scratch_shapes=[
                pltpu.VMEM((width, rows), LOW),
                pltpu.VMEM((rows, 3 * group), LOW),
                pltpu.VMEM((2, group), WIDE),
                pltpu.VMEM((groups + 16, width), WIDE),
                pltpu.VMEM((count, 32, 384), WIDE),
            ],
        ),
        out_shape=[
            shaped((count, entry, width), LOW),
            shaped((count, entry, width), LOW),
            shaped((rows, width), LOW),
        ],
        compiler_params=params(),
        cost_estimate=LONG,
        name="last_back",
    )(
        place,
        normed,
        dq,
        own,
        got,
        w_qkv,
        w_qkv,
        w_qkv,
        part,
        embedded,
        g_residual,
        gain,
        prior,
        expression,
        bias_first,
        vectors,
        bias_up,
        *after,
    )


def gene_kernel(slots_ref, ids_ref, grad_ref, *rest):
    out_ref = rest[-1]
    slots = slots_ref[...]
    rows = grad_ref.shape[0]
    picker = jnp.where(slots == jnp.broadcast_to(ids_ref[...], (slots.shape[0], rows)), 1.0, 0.0)
    out_ref[...] = dot(picker.astype(LOW), grad_ref[...]).astype(LOW)


def gene_rows(slots, ids, grad, after):
    count = slots.shape[0]
    rows, width = grad.shape
    tile = min(count, 1152)
    return pl.pallas_call(
        gene_kernel,
        grid=(count // tile,),
        in_specs=[
            pl.BlockSpec((tile, 1), lambda j: (j, 0)),
            whole((1, rows)),
            whole((rows, width)),
        ]
        + unread(after),
        out_specs=pl.BlockSpec((tile, width), lambda j: (j, 0)),
        out_shape=shaped((count, width), LOW),
        compiler_params=params(),
        cost_estimate=LONG,
        name="gene_rows",
    )(slots, ids, grad, *after)


def swap_cores(array):
    return lax.ppermute(array, "blk", [(0, 1), (1, 0)])


def bits_apart(array, mask):
    count = lax.axis_size("dp")
    return lax.ppermute(array, "dp", [(i, i ^ mask) for i in range(count)])


def pick(array, position, index):
    return lax.dynamic_index_in_dim(array, index, position, keepdims=False)


class Share:
    QUAD = "quad"

    def __init__(self, segments, route):
        self.bits = lax.axis_size("dp").bit_length() - 1
        self.route = list(route)
        self.rows = []
        self.sources = []
        dims = tuple(range(self.bits - 1, -1, -1))
        for arrays, blocks, *rows in segments:
            first, single = len(self.rows), len(blocks) == 1
            rows = rows[0] if rows else [(0, arrays[0].shape[1])] * len(blocks)
            self.rows += [size for _, size in rows]
            parts = [
                (first + at, rows[at][0], 0 if single else block * LANES)
                for at, block in enumerate(blocks)
            ]
            columns = LANES if single else arrays[0].shape[2]
            where, height = (0, blocks[0] if single else 0), arrays[0].shape[1]
            start, size = rows[0]
            if single and size % 16 == start % size == height % size == 0:
                where, height = (start // size, where[1]), size
                parts = [(first, 0, 0)]
            for array in arrays:
                shape = (2,) * self.bits + array.shape[1:]
                self.sources.append((array.reshape(shape), dims, where, (height, columns), parts))
        self.arriving = []
        self.fixed = ()
        self.settle_places()

    def join(self, other):
        shift = len(self.rows)
        moved = lambda sources: [
            source[:4] + ([(index + shift, row, column) for index, row, column in source[4]],)
            for source in sources
        ]
        self.rows = self.rows + other.rows
        self.sources += moved(other.sources)
        self.arriving += moved(other.arriving)
        self.settle_places()
        return self

    def settle_places(self):
        self.places, place = [], 0
        for rows in self.rows:
            self.places.append(place)
            place += up16(rows)
        self.height = self.places[-1] + self.rows[-1]

    def parts(self):
        return [(index, place, 0) for index, place in enumerate(self.places)]

    def targets(self):
        step = self.route[0]
        if step == self.QUAD:
            low, high = self.bits - 2, self.bits - 1
            return [{low: way & 1, high: way >> 1} for way in (1, 2, 3)]
        return [{step: 1}]

    def left(self, target=()):
        gone = self.fixed + tuple(target)
        return [bit for bit in range(self.bits - 1, -1, -1) if bit not in gone]

    def receive(self, targets, sent):
        self.route.pop(0)
        for target, array in zip(targets, sent):
            mask = sum(flip << bit for bit, flip in target.items())
            dims = tuple(self.left(target))
            self.arriving.append(
                (bits_apart(array, mask), dims, (0, 0), array.shape[-2:], self.parts())
            )
        self.fixed += tuple(targets[0])

    def arrived(self):
        self.sources, self.arriving = self.sources + self.arriving, []


SEND, SETTLE, FINISH = range(3)


def combine(place, shares, after, mode=SEND, last=None):
    operands, specs, plan, out_specs, out_shape = [], [], [], [], []
    steps = []
    top = shares[0].bits - 1
    halves = mode == SETTLE or (
        mode == SEND and not any(top in share.fixed or top in share.targets()[0] for share in shares)
    )
    for share in shares:
        if mode != SETTLE:
            share.arrived()
        targets = share.targets() if mode == SEND else [{}]
        steps.append(targets)
        left = share.left(targets[0]) if mode != FINISH else []
        quad = len(targets) > 1
        used = []
        for array, dims, block, size, parts in share.sources:
            shape, where, picked = [], [], []
            for bit in dims:
                free = bit in left or (quad and bit in targets[0])
                stepped = halves and bit == top
                shape.append(2 if free and not stepped else None)
                where.append(bit if stepped else None if free else (bit, targets[0].get(bit, 0)))
                if quad and bit in targets[0]:
                    picked.append(bit)

            def index(step, place, where=tuple(where), block=block):
                lead = []
                for at in where:
                    if at is None:
                        lead.append(0)
                    elif at == top:
                        lead.append(step)
                    else:
                        lead.append(1 - place[4 + at[0]] if at[1] else place[4 + at[0]])
                return tuple(lead) + block

            specs.append(pl.BlockSpec(tuple(shape) + tuple(size), index))
            used.append((len(operands), parts))
            operands.append(array)
        for target in targets:
            plan.append((share.rows, share.places, used, target if quad else {}))
            if mode != FINISH:
                shape = (2,) * len(left) + (share.height, LANES)
                if halves:
                    zeros = (0,) * (len(shape) - 1)
                    out_specs.append(
                        pl.BlockSpec(
                            (None,) + shape[1:], lambda step, _, zeros=zeros: (step,) + zeros
                        )
                    )
                else:
                    out_specs.append(whole(shape))
                out_shape.append(shaped(shape, LOW if mode == SEND else WIDE))
    for shape, _ in last or []:
        out_specs.append(whole(shape))
        out_shape.append(shaped(shape, WIDE))
    count = len(operands)

    def kernel(*refs):
        place_ref, sources, outs = refs[0], refs[1 : 1 + count], refs[1 + count + len(after) :]

        def summed(item, block):
            rows, _, used, target = plan[item]
            total = None
            way = tuple(
                1 - place_ref[4 + bit] if flip else place_ref[4 + bit]
                for bit, flip in sorted(target.items(), reverse=True)
            )
            for operand, parts in used:
                for index, row, column in parts:
                    if index == block:
                        ref = sources[operand]
                        spot = (slice(row, row + rows[block]), slice(column, column + LANES))
                        lead = way + (slice(None),) * (len(ref.shape) - 2 - len(way))
                        part = ref[lead + spot].astype(WIDE)
                        total = part if total is None else total + part
            return total

        if mode == FINISH:
            for (_, pieces), out in zip(last, outs):
                for item, block, row, column in pieces:
                    value = summed(item, block)
                    out[row : row + value.shape[0], column : column + LANES] = value
            return
        for item, out in enumerate(outs):
            for block, start in enumerate(plan[item][1]):
                value = summed(item, block)
                out[..., start : start + value.shape[-2], :] = value.astype(out.dtype)

    outs = pl.pallas_call(
        kernel,
        grid_spec=pltpu.PrefetchScalarGridSpec(
            num_scalar_prefetch=1,
            grid=(2 if halves else 1,),
            in_specs=specs + unread(after),
            out_specs=out_specs,
        ),
        out_shape=out_shape,
        compiler_params=params(),
        cost_estimate=LONG,
        name="combine",
    )(place, *[pltpu.with_memory_space_constraint(x, pltpu.HBM) for x in operands], *after)
    taken = 0
    for share, targets in zip(shares, steps):
        if mode == SEND:
            share.receive(targets, outs[taken : taken + len(targets)])
        if mode == SETTLE:
            share.sources = [
                (outs[taken], tuple(share.left()), (0, 0), outs[taken].shape[-2:], share.parts())
            ]
        taken += len(targets)
    return outs


def assemble(place, own, other, shapes, pieces, small_row=None):
    def kernel(place_ref, own_ref, other_ref, *outs):
        first = place_ref[0] == 0

        def of_core(core, rows, columns):
            return jnp.where(first == (core == 0), own_ref[rows, columns], other_ref[rows, columns])

        for core, row, rows, column, columns, target, out_column in pieces:
            value = of_core(core, slice(row, row + rows), slice(column, column + columns))
            outs[target][:, out_column : out_column + columns] = value
        if small_row is None:
            outs[-1][...] = jnp.zeros_like(outs[-1])
            return
        group_ref, vector_refs, long_ref = outs[2], outs[3:-1], outs[-1]
        share, groups = group_ref.shape
        rows = slice(small_row, small_row + 16)
        for start in range(0, groups, 16):
            lanes = slice(start // 32 * 128, start // 32 * 128 + share)
            group_ref[:, start : start + 16] = of_core(start // 16 % 2, rows, lanes).T
        rest = of_core(0, rows, slice(groups // 32 * 128, groups // 32 * 128 + 128))
        for index, ref in enumerate(vector_refs):
            ref[...] = rest[index, :share]
        long_ref[...] = jnp.concatenate(
            [rest[9 + part : 10 + part, :share] for part in range(4)], 1
        )[0]

    return pl.pallas_call(
        kernel,
        grid_spec=pltpu.PrefetchScalarGridSpec(
            num_scalar_prefetch=1,
            grid=(1,),
            in_specs=[whole(own.shape), whole(own.shape)],
            out_specs=[whole(shape) for shape in shapes],
        ),
        out_shape=[shaped(shape, WIDE) for shape in shapes],
        compiler_params=params(),
        cost_estimate=LONG,
        name="assemble",
    )(place, own, other)


def body(
    gene_ids,
    values,
    knowledge,
    lengths,
    groups,
    gene_table,
    group_table,
    w_know,
    w_value,
    norm1_gain,
    norm1_bias,
    w_qkv,
    bias_q,
    bias_v,
    w_out,
    bias_out,
    norm2_gain,
    norm2_bias,
    w_up,
    bias_up,
    w_down,
    bias_down,
    cotangent,
):
    width = w_out.shape[0]
    units = w_up.shape[1]
    rows = gene_ids.shape[1]
    count = lax.axis_size("dp")
    mine = lax.axis_index("blk")
    length, group = lengths[0], groups[0]
    prior = knowledge[0]
    row = lambda vector: vector.reshape(1, -1)
    me = lax.axis_index("dp")
    bits = count.bit_length() - 1
    place = jnp.stack(
        [mine, length - mine * rows, length - (1 - mine) * rows, group]
        + [(me >> bit) & 1 for bit in range(bits)]
    ).astype(jnp.int32)
    if gene_table.shape[0] > 8 * rows:
        table = gene_table[gene_ids[0]]
    else:
        table = gene_table
    embedded, normed, kv_own = embed(
        place,
        gene_ids,
        values,
        prior,
        table,
        group_table,
        w_know,
        w_value,
        norm1_gain,
        norm1_bias,
        w_qkv,
        bias_v,
    )
    kv_other = swap_cores(kv_own)
    queries = project_queries(normed, w_qkv, bias_q)
    attended, probs, inverse = attend(place, queries, kv_own, kv_other)
    (
        block_output,
        residual,
        g_normed_two,
        up_send,
        up_keep,
        down_send,
        down_keep,
        bias_up_grad,
    ) = feed_forward(
        place,
        attended,
        embedded,
        cotangent[0],
        w_out,
        bias_out,
        norm2_gain,
        norm2_bias,
        w_up,
        row(bias_up),
        w_down,
        bias_down,
    )
    g_residual, g_attended, out_send, out_keep, vectors = branch_back(
        place,
        residual,
        g_normed_two,
        cotangent[0],
        attended,
        w_out,
        norm2_gain,
        [up_send, down_send],
    )

    owners = lambda array: array.reshape(count, -1, array.shape[-1])
    low_bits = list(range(bits - 2))
    turned = low_bits[1::-1] + low_bits[2:]
    quad, high_bits = [Share.QUAD], [bits - 2, bits - 1]
    up_terms = [owners(up_keep), owners(swap_cores(up_send))]
    blocks = units // 2 // LANES
    out_terms = [owners(out_keep), owners(swap_cores(out_send))]
    down_terms = [owners(down_keep), owners(swap_cores(down_send))]
    high, share = units // count, width // count
    out_cut = min(share, up16(2 * share // 3))
    out_rest = [(out_terms, [0], [(out_cut, share - out_cut)])] if out_cut < share else []
    early = [
        Share([(down_terms, [0]), (out_terms, [0], [(0, out_cut)])], low_bits + quad),
        Share([(up_terms, list(range(blocks)))] + out_rest, turned + quad),
    ]
    token = combine(place, early, [])
    dq1, own1, other1 = attend_back(
        queries, kv_own, kv_other, attended, g_attended, probs, inverse, 0, 4, token
    )
    got1 = swap_cores(other1)
    dq2, own2, other2 = attend_back(
        queries, kv_own, kv_other, attended, g_attended, probs, inverse, 4, 2, [dq1]
    )
    got2 = swap_cores(other2)
    qkv_send, qkv_keep, bias_first, part = first_back(
        place, normed, dq1, own1, got1, w_qkv, 256, [dq2]
    )
    qkv = [owners(qkv_keep), owners(swap_cores(qkv_send))]
    project = Share([(qkv, [0, 1])], high_bits + low_bits)
    token = [part, qkv_send]
    for bit in low_bits[1:]:
        token = combine(place, early + [project] * (bit == low_bits[-1]), token)
    early = [early[0].join(early[1])]
    tail_send, tail_keep, g_low = last_back(
        place,
        normed,
        dq2,
        own2,
        got2,
        w_qkv,
        256,
        part,
        embedded,
        g_residual,
        norm1_gain,
        prior,
        values,
        bias_first,
        vectors,
        bias_up_grad,
        group_table.shape[0],
        count,
        token,
    )
    slot = jnp.arange(count * VOC_DEV, dtype=jnp.int32)[:, None]
    slot = slot + slot // VOC_DEV * VOC_DEV
    gene_send = gene_rows(slot + (1 - mine) * VOC_DEV, gene_ids, g_low, [tail_send])
    gene_got = swap_cores(gene_send)
    gene_keep = gene_rows(slot + mine * VOC_DEV, gene_ids, g_low, [gene_send])
    tail = [tail_keep, swap_cores(tail_send)]
    gene = [owners(gene_keep), owners(gene_got)]
    small_at = up16(share)
    late = [
        Share([(tail, [0], [(0, share)]), (gene, [0])], low_bits + quad),
        Share(
            [(tail, [1], [(0, share)]), (tail, [0], [(small_at, 16)]), (gene, [1])], turned + quad
        ),
    ]
    token = combine(place, [project], [gene_keep])
    token = combine(place, late, token)
    token = combine(place, early, token)
    for _ in low_bits[1:]:
        token = combine(place, late + [project], token)
    token = combine(place, late, token, SETTLE)
    late = [late[0].join(late[1]), project]
    step = up16(share)
    layout = [(0, 0, 0, 0), (0, 1, high + blocks * step, 0)]
    if out_rest:
        layout.append((0, 2 + blocks, high + blocks * step + out_cut, 0))
    layout += [(0, 2 + block, high + block * step, 0) for block in range(blocks)]
    (own,) = combine(place, early, token, FINISH, [((high + (blocks + 1) * step, LANES), layout)])
    other = swap_cores(own)
    combine(place, late, [own])
    pieces = []
    for core in range(2):
        pieces.append((core, 0, high, 0, LANES, 0, core * LANES))
        for block in range(blocks):
            place_in = (core * blocks + block) * LANES
            pieces.append((core, high + block * step, share, 0, LANES, 1, place_in))
        pieces.append((core, high + blocks * step, share, 0, LANES, 2, core * LANES))
    w_down_share, w_up_share, w_out_share, done = assemble(
        place, own, other, [(high, width), (share, units), (share, width), (8, 128)], pieces
    )
    layout = [(1, 0, 0, 0), (1, 1, step, 0), (0, 0, 2 * step, 0), (0, 2, 3 * step, 0)]
    layout += [(0, 3, 4 * step, 0)]
    own, gene_grad = combine(
        place,
        late,
        [done],
        FINISH,
        [
            ((4 * step + 16, LANES), layout),
            ((VOC_DEV, width), [(0, 1, 0, 0), (0, 4, 0, LANES)]),
        ],
    )
    other = swap_cores(own)
    pieces = []
    for block in range(3):
        at = block * step
        pieces.append((0, at, share, 0, 256, 0, block * 256))
        pieces.append((0, at, share, 256, 128, 0, width + block * 256))
        pieces.append((1, at, share, 0, 128, 0, width + block * 256 + 128))
        pieces.append((1, at, share, 128, 256, 0, 2 * width + block * 256))
    for core in range(2):
        pieces.append((core, 3 * step, share, 0, LANES, 1, core * LANES))
    w_qkv_share, w_know_share, group_share, *extra, bias_up_share = assemble(
        place,
        own,
        other,
        [(share, 3 * width), (share, width), (share, group_table.shape[0])]
        + [(share,)] * 9
        + [(units // count,)],
        pieces,
        4 * step,
    )
    return (
        block_output[None],
        gene_grad,
        group_share.T,
        w_know_share,
        extra[0],
        extra[1],
        extra[2],
        w_qkv_share,
        extra[3],
        extra[4],
        w_out_share,
        extra[5],
        extra[6],
        extra[7],
        w_up_share,
        bias_up_share,
        w_down_share,
        extra[8],
    )


def solution(mesh):
    in_specs = (
        P("dp", "blk"),
        P("dp", "blk"),
        P("dp", "blk", None),
        P("dp"),
        P("dp"),
        P(),
        P(),
        P(),
        P(),
        P(),
        P(),
        P(),
        P(),
        P(),
        P(),
        P(),
        P(),
        P(),
        P(),
        P(),
        P(),
        P(),
        P("dp", "blk", None),
    )
    out_specs = (
        P("dp", "blk", None),
        P(("dp", "blk"), None),
        P(None, "dp"),
        P("dp", None),
        P("dp"),
        P("dp"),
        P("dp"),
        P("dp", None),
        P("dp"),
        P("dp"),
        P("dp", None),
        P("dp"),
        P("dp"),
        P("dp"),
        P("dp", None),
        P("dp"),
        P("dp", None),
        P("dp"),
    )
    return jax.shard_map(body, mesh=mesh, in_specs=in_specs, out_specs=out_specs, check_vma=False)
```

```python
import functools

import jax
import jax.numpy as jnp
from jax import lax
from jax.experimental import pallas as pl
from jax.experimental.pallas import tpu as pltpu
from jax.sharding import PartitionSpec as P

HEAD_DIM = 64
VOC_DEV = 72
EPSILON = 1e-05
LANES = 384
LOW = jnp.bfloat16
WIDE = jnp.float32
GRANT = 44 << 20


LONG = pl.CostEstimate(flops=10**12, bytes_accessed=1, transcendentals=0)


def dot(left, right, left_dim=1, right_dim=0):
    return lax.dot_general(
        left, right, (((left_dim,), (right_dim,)), ((), ())), preferred_element_type=WIDE
    )


def column_sums(array):
    return jnp.sum(array, 0, keepdims=True)


def row_means(array):
    return jnp.mean(array, -1, keepdims=True)


def normalize(array):
    center = array - row_means(array)
    scale = lax.rsqrt(row_means(center * center) + EPSILON)
    return center * scale, scale


def norm_back(grad, unit, scale, gain):
    inner = grad * gain
    return scale * (inner - row_means(inner) - unit * row_means(inner * unit))


def half_of(index, half):
    return pl.ds(pl.multiple_of(index * half, 128), half)


def whole(shape):
    return pl.BlockSpec(shape, lambda *_: (0,) * len(shape))


def up16(rows):
    return -(-rows // 16) * 16


def unread(arrays):
    return [pl.BlockSpec(memory_space=pl.ANY)] * len(arrays)


def params(grant=GRANT):
    return pltpu.CompilerParams(vmem_limit_bytes=grant)


def shaped(shape, dtype):
    return jax.ShapeDtypeStruct(shape, dtype)


def embed_kernel(
    place_ref,
    ids_ref,
    expression_ref,
    prior_ref,
    table_ref,
    group_ref,
    w_know_ref,
    w_value_ref,
    gain_ref,
    offset_ref,
    w_key_ref,
    w_val_ref,
    bias_val_ref,
    embedded_ref,
    normed_ref,
    kv_ref,
):
    rows, width = prior_ref.shape
    embedded = dot(prior_ref[...], w_know_ref[...])
    if table_ref.shape[0] == rows:
        gathered = table_ref[...].astype(WIDE)
    else:
        ids = jnp.broadcast_to(ids_ref[...], (8, rows)).T[:, :1]
        slots = lax.broadcasted_iota(jnp.int32, (rows, table_ref.shape[0]), 1)
        picker = jnp.where(slots == ids, 1.0, 0.0).astype(LOW)
        gathered = dot(picker, table_ref[...])
    expression = jnp.broadcast_to(expression_ref[...], (8, rows)).T[:, :1]
    groups = lax.broadcasted_iota(jnp.int32, (8, group_ref.shape[0]), 1)
    group_row = dot(jnp.where(groups == place_ref[3], 1.0, 0.0).astype(LOW), group_ref[...])[:1]
    embedded = gathered + group_row + expression * w_value_ref[...][None] + embedded
    embedded_ref[...] = embedded
    unit, _ = normalize(embedded)
    normed = (unit * gain_ref[...][None] + offset_ref[...][None]).astype(LOW)
    normed_ref[...] = normed
    kv_ref[:, :width] = dot(normed, w_key_ref[...]).astype(LOW)
    kv_ref[:, width:] = (dot(normed, w_val_ref[...]) + bias_val_ref[...][None]).astype(LOW)


def embed(
    place, ids, expression, prior, table, group_table, w_know, w_value, gain, offset, w_qkv, bias_v
):
    rows, width = prior.shape
    columns = lambda index: pl.BlockSpec((width, width), lambda *_: (0, index))
    return pl.pallas_call(
        embed_kernel,
        grid_spec=pltpu.PrefetchScalarGridSpec(
            num_scalar_prefetch=1,
            grid=(1,),
            in_specs=[
                whole((1, rows)),
                whole((1, rows)),
                whole((rows, width)),
                whole(table.shape),
                whole(group_table.shape),
                whole((width, width)),
                whole((width,)),
                whole((width,)),
                whole((width,)),
                columns(1),
                columns(2),
                whole((width,)),
            ],
            out_specs=[whole((rows, width)), whole((rows, width)), whole((rows, 2 * width))],
        ),
        out_shape=[
            shaped((rows, width), WIDE),
            shaped((rows, width), LOW),
            shaped((rows, 2 * width), LOW),
        ],
        compiler_params=params(60 << 20),
        name="embed",
    )(
        place,
        ids,
        expression,
        prior,
        table,
        group_table,
        w_know,
        w_value,
        gain,
        offset,
        w_qkv,
        w_qkv,
        bias_v,
    )


def query_kernel(normed_ref, w_query_ref, bias_ref, out_ref):
    out_ref[...] = (dot(normed_ref[...], w_query_ref[...]) + bias_ref[...][None]).astype(LOW)


def project_queries(normed, w_qkv, bias_q):
    rows, width = normed.shape
    return pl.pallas_call(
        query_kernel,
        grid=(1,),
        in_specs=[whole((rows, width)), whole((width, width)), whole((width,))],
        out_specs=whole((rows, width)),
        out_shape=shaped((rows, width), LOW),
        compiler_params=params(),
        cost_estimate=pl.CostEstimate(
            flops=2 * rows * width * width, bytes_accessed=4 * rows * width, transcendentals=0
        ),
        name="queries",
    )(normed, w_qkv, bias_q)


def attend_kernel(place_ref, q_ref, ko_ref, vo_ref, kr_ref, vr_ref, out_ref, p_ref, c_ref):
    rows = q_ref.shape[0]
    lane = lax.broadcasted_iota(jnp.int32, (rows, 128), 1)
    place = lax.broadcasted_iota(jnp.int32, (rows, 128), 0)
    queries = q_ref[...] * LOW(HEAD_DIM**-0.5)
    halves = []
    for index, k_ref in enumerate((ko_ref, kr_ref)):
        dead = jnp.where(place < place_ref[1 + index], 0.0, -1e30).astype(LOW)
        halves.append((k_ref[...], dead))
    values = [vo_ref[...].T, vr_ref[...].T]
    ones = jnp.ones((16, rows), LOW)
    scored, outs = [], []
    for head in range(2):
        inside = (lane < HEAD_DIM) if head == 0 else (lane >= HEAD_DIM)
        spare = HEAD_DIM * (1 - head)
        asked = jnp.where(inside, queries, jnp.where(lane == spare, 1.0, 0.0).astype(LOW))
        scored.append(
            [dot(jnp.where(lane == spare, dead, keys), asked, 1, 1) for keys, dead in halves]
        )
    for head in range(2):
        scores = scored[head]
        top = jnp.maximum(*[jnp.max(part, 0, keepdims=True) for part in scores])
        mixed = 0.0
        for index in range(2):
            low = jnp.exp(scores[index] - top).astype(LOW)
            p_ref[head, index * rows : (index + 1) * rows, :] = low
            own = values[index][head * HEAD_DIM : (head + 1) * HEAD_DIM]
            mixed = mixed + dot(jnp.concatenate([own, ones], 0), low)
        inverse = 1.0 / mixed[HEAD_DIM : HEAD_DIM + 1]
        c_ref[0, head : head + 1, :] = inverse
        outs.append(mixed[:HEAD_DIM] * inverse)
    out_ref[...] = jnp.concatenate(outs, 0).T.astype(LOW)


def attend(place, queries, kv_own, kv_other):
    rows, width = queries.shape
    pairs = width // 128
    block = lambda shift: pl.BlockSpec((rows, 128), lambda j, _: (0, shift + j))
    return pl.pallas_call(
        attend_kernel,
        grid_spec=pltpu.PrefetchScalarGridSpec(
            num_scalar_prefetch=1,
            grid=(pairs,),
            in_specs=[block(0), block(0), block(pairs), block(0), block(pairs)],
            out_specs=[
                block(0),
                pl.BlockSpec((2, 2 * rows, rows), lambda j, _: (j, 0, 0)),
                pl.BlockSpec((1, 2, rows), lambda j, _: (j, 0, 0)),
            ],
        ),
        out_shape=[
            shaped((rows, width), LOW),
            shaped((2 * pairs, 2 * rows, rows), LOW),
            shaped((pairs, 2, rows), WIDE),
        ],
        compiler_params=params(),
        cost_estimate=pl.CostEstimate(
            flops=16 * rows * rows * width,
            bytes_accessed=8 * rows * rows * pairs,
            transcendentals=4 * rows * rows * pairs,
        ),
        name="attend",
    )(place, queries, kv_own, kv_own, kv_other, kv_other)


def attend_back_kernel(
    q_ref,
    ko_ref,
    vo_ref,
    kr_ref,
    vr_ref,
    a_ref,
    g_ref,
    p_ref,
    c_ref,
    *rest,
):
    dq_ref, dkvo_ref, dkvr_ref = rest[-3:]
    rows = q_ref.shape[0]
    lane = lax.broadcasted_iota(jnp.int32, (rows, 128), 1)
    mixed = a_ref[...].astype(WIDE).T
    grad = g_ref[...].astype(WIDE).T
    grad = jnp.concatenate(
        [grad[:HEAD_DIM] * c_ref[0, :1, :], grad[HEAD_DIM:] * c_ref[0, 1:, :]], 0
    )
    inner = grad * mixed
    inner = [column_sums(inner[:HEAD_DIM]), column_sums(inner[HEAD_DIM:])]
    first = lax.broadcasted_iota(jnp.int32, (128, rows), 0) < HEAD_DIM
    low = grad.astype(LOW)
    masked = [
        jnp.where(first, low, jnp.zeros_like(low)),
        jnp.where(first, jnp.zeros_like(low), low),
    ]
    grad_rows = grad.T.astype(LOW)
    queries = q_ref[...]
    parts = [0.0, 0.0]
    for index, (k_ref, v_ref, out_ref) in enumerate(
        ((ko_ref, vo_ref, dkvo_ref), (kr_ref, vr_ref, dkvr_ref))
    ):
        keys = k_ref[...].T
        values = v_ref[...]
        key_grads, val_grads = [], []
        for head in range(2):
            probs = p_ref[head, index * rows : (index + 1) * rows, :]
            wide = dot(values, masked[head]) - inner[head]
            score = (probs.astype(WIDE) * wide).astype(LOW)
            val_grads.append(dot(probs, grad_rows))
            key_grads.append(dot(score, queries))
            parts[head] = parts[head] + dot(keys[head * HEAD_DIM : (head + 1) * HEAD_DIM], score)
        chosen = lane < HEAD_DIM
        out_ref[0] = (jnp.where(chosen, *key_grads) * HEAD_DIM**-0.5).astype(LOW)
        out_ref[1] = jnp.where(chosen, *val_grads).astype(LOW)
    dq_ref[...] = (jnp.concatenate(parts, 0).T * HEAD_DIM**-0.5).astype(LOW)


def attend_back(queries, kv_own, kv_other, attended, grad, probs, inverse, start, count, after):
    rows, width = queries.shape
    pairs = width // 128
    block = lambda shift: pl.BlockSpec((rows, 128), lambda j: (0, shift + j))
    near, far = block(start), block(pairs + start)
    both = pl.BlockSpec((2, rows, 128), lambda j: (0, 0, j))
    return pl.pallas_call(
        attend_back_kernel,
        grid=(count,),
        in_specs=[
            near,
            near,
            far,
            near,
            far,
            near,
            near,
            pl.BlockSpec((2, 2 * rows, rows), lambda j: (start + j, 0, 0)),
            pl.BlockSpec((1, 2, rows), lambda j: (start + j, 0, 0)),
        ]
        + unread(after),
        out_specs=[block(0), both, both],
        out_shape=[
            shaped((rows, 128 * count), LOW),
            shaped((2, rows, 128 * count), LOW),
            shaped((2, rows, 128 * count), LOW),
        ],
        compiler_params=params(),
        cost_estimate=LONG,
        name="attend_back",
    )(queries, kv_own, kv_own, kv_other, kv_other, attended, grad, probs, inverse, *after)


def ffn_kernel(
    place_ref,
    attended_ref,
    embedded_ref,
    cotangent_ref,
    w_out_ref,
    bias_out_ref,
    gain_ref,
    offset_ref,
    w_up_ref,
    bias_up_ref,
    w_down_ref,
    bias_down_ref,
    output_ref,
    residual_ref,
    g_normed_ref,
    up_send_ref,
    up_keep_ref,
    down_send_ref,
    down_keep_ref,
    bias_up_grad_ref,
    normed_ref,
    total_ref,
    g_out_ref,
    g_halves_ref,
):
    step, steps = pl.program_id(0), pl.num_programs(0)
    rows, width = attended_ref.shape
    half = width // 2
    mine = place_ref[0]
    alive = lax.broadcasted_iota(jnp.int32, (rows, 1), 0) < place_ref[1]

    @pl.when(step == 0)
    def _():
        residual = embedded_ref[...] + (
            dot(attended_ref[...], w_out_ref[...]) + bias_out_ref[...][None]
        )
        residual_ref[...] = residual
        unit, _ = normalize(residual)
        normed_ref[...] = (unit * gain_ref[...][None] + offset_ref[...][None]).astype(LOW)
        g_out_ref[...] = jnp.where(alive, cotangent_ref[...].astype(WIDE), 0.0).astype(LOW)
        g_halves_ref[:, :half] = g_out_ref[:, half_of(1 - mine, half)]
        g_halves_ref[:, half:] = g_out_ref[:, half_of(mine, half)]
        total_ref[...] = jnp.zeros_like(total_ref)
        g_normed_ref[...] = jnp.zeros_like(g_normed_ref)

    hidden = dot(normed_ref[...], w_up_ref[...]) + bias_up_ref[...]
    g_act = dot(g_out_ref[...], w_down_ref[...], 1, 1)
    share = 0.5 * (1.0 + lax.erf(hidden * 0.5**0.5))
    density = jnp.exp(-0.5 * hidden * hidden) * 0.3989422804014327
    activated = (hidden * share).astype(LOW)
    g_hidden = (g_act * (share + hidden * density)).astype(LOW)
    total_ref[...] += dot(activated, w_down_ref[...])
    g_normed_ref[...] += dot(g_hidden, w_up_ref[...], 1, 1)
    down = dot(activated, g_halves_ref[...], 0, 0).astype(LOW)
    down_send_ref[...] = down[:, :half]
    down_keep_ref[...] = down[:, half:]
    up = dot(normed_ref[...], g_hidden, 0, 0).astype(LOW)
    bias_up_grad_ref[...] = column_sums(g_hidden.astype(WIDE))

    @pl.when(step < steps // 2)
    def _():
        up_send_ref[...] = up

    @pl.when(step >= steps // 2)
    def _():
        up_keep_ref[...] = up

    @pl.when(step == steps - 1)
    def _():
        final = residual_ref[...] + (total_ref[...] + bias_down_ref[...][None])
        output_ref[...] = jnp.where(alive, final, 0.0).astype(LOW)


def feed_forward(
    place,
    attended,
    embedded,
    cotangent,
    w_out,
    bias_out,
    gain,
    offset,
    w_up,
    bias_up,
    w_down,
    bias_down,
):
    rows, width = attended.shape
    units = w_up.shape[1]
    tile = 512
    steps = units // tile
    turn = lambda j, place: lax.rem(j + (1 - place[0]) * (steps // 2), steps)
    down_tile = pl.BlockSpec((tile, width // 2), lambda j, place: (turn(j, place), 0))
    return pl.pallas_call(
        ffn_kernel,
        grid_spec=pltpu.PrefetchScalarGridSpec(
            num_scalar_prefetch=1,
            grid=(steps,),
            in_specs=[
                whole((rows, width)),
                whole((rows, width)),
                whole((rows, width)),
                whole((width, width)),
                whole((width,)),
                whole((width,)),
                whole((width,)),
                pl.BlockSpec((width, tile), lambda j, place: (0, turn(j, place))),
                pl.BlockSpec((1, tile), lambda j, place: (0, turn(j, place))),
                pl.BlockSpec((tile, width), lambda j, place: (turn(j, place), 0)),
                whole((width,)),
            ],
            out_specs=[
                whole((rows, width)),
                whole((rows, width)),
                whole((rows, width)),
                pl.BlockSpec((width, tile), lambda j, _: (0, jnp.minimum(j, steps // 2 - 1))),
                pl.BlockSpec((width, tile), lambda j, _: (0, jnp.maximum(j - steps // 2, 0))),
                down_tile,
                down_tile,
                pl.BlockSpec((1, tile), lambda j, place: (0, turn(j, place))),
            ],
            scratch_shapes=[
                pltpu.VMEM((rows, width), LOW),
                pltpu.VMEM((rows, width), WIDE),
                pltpu.VMEM((rows, width), LOW),
                pltpu.VMEM((rows, width), LOW),
            ],
        ),
        out_shape=[
            shaped((rows, width), LOW),
            shaped((rows, width), WIDE),
            shaped((rows, width), WIDE),
            shaped((width, units // 2), LOW),
            shaped((width, units // 2), LOW),
            shaped((units, width // 2), LOW),
            shaped((units, width // 2), LOW),
            shaped((1, units), WIDE),
        ],
        compiler_params=params(),
        cost_estimate=LONG,
        name="feed_forward",
    )(
        place,
        attended,
        embedded,
        cotangent,
        w_out,
        bias_out,
        gain,
        offset,
        w_up,
        bias_up,
        w_down,
        bias_down,
    )


def branch_kernel(
    place_ref,
    residual_ref,
    g_normed_ref,
    cotangent_ref,
    attended_ref,
    w_out_ref,
    gain_ref,
    *rest,
):
    g_residual_ref, g_attended_ref, out_send_ref, out_keep_ref, vectors_ref, total_ref = rest[-6:]
    step, steps = pl.program_id(0), pl.num_programs(0)
    rows, width = residual_ref.shape
    half = width // 2
    mine = place_ref[0]
    alive = step * rows + lax.broadcasted_iota(jnp.int32, (rows, 1), 0) < place_ref[1]

    @pl.when(step == 0)
    def _():
        total_ref[...] = jnp.zeros_like(total_ref)
        vectors_ref[...] = jnp.zeros_like(vectors_ref)

    unit, scale = normalize(residual_ref[...])
    g_final = jnp.where(alive, cotangent_ref[...].astype(WIDE), 0.0)
    g_normed = g_normed_ref[...]
    g_residual = g_final + norm_back(g_normed, unit, scale, gain_ref[...][None])
    g_residual_ref[...] = g_residual
    g_branch = g_residual.astype(LOW)
    g_attended_ref[...] = dot(g_branch, w_out_ref[...], 1, 1).astype(LOW)
    total_ref[...] += dot(attended_ref[...], g_branch, 0, 0)
    vectors_ref[...] += jnp.concatenate(
        [
            column_sums(g_branch.astype(WIDE)),
            column_sums(g_normed * unit),
            column_sums(g_normed),
            column_sums(g_final),
        ],
        0,
    )

    @pl.when(step == steps - 1)
    def _():
        out_send_ref[...] = total_ref[:, half_of(1 - mine, half)].astype(LOW)
        out_keep_ref[...] = total_ref[:, half_of(mine, half)].astype(LOW)


def branch_back(place, residual, g_normed, cotangent, attended, w_out, gain, after):
    rows, width = residual.shape
    steps = 2
    tile = pl.BlockSpec((rows // steps, width), lambda j, _: (j, 0))
    return pl.pallas_call(
        branch_kernel,
        grid_spec=pltpu.PrefetchScalarGridSpec(
            num_scalar_prefetch=1,
            grid=(steps,),
            in_specs=[tile, tile, tile, tile, whole((width, width)), whole((width,))]
            + unread(after),
            out_specs=[
                tile,
                tile,
                whole((width, width // 2)),
                whole((width, width // 2)),
                whole((4, width)),
            ],
            scratch_shapes=[pltpu.VMEM((width, width), WIDE)],
        ),
        out_shape=[
            shaped((rows, width), WIDE),
            shaped((rows, width), LOW),
            shaped((width, width // 2), LOW),
            shaped((width, width // 2), LOW),
            shaped((4, width), WIDE),
        ],
        compiler_params=params(),
        cost_estimate=LONG,
        name="branch_back",
    )(place, residual, g_normed, cotangent, attended, w_out, gain, *after)


def project_back(place_ref, normed_turned, dq_ref, own_ref, got_ref, weights, joined_ref, send_ref, keep_ref, bias_ref):
    group = dq_ref.shape[1]
    half = 3 * group // 2
    mine = place_ref[0]
    joined_ref[:, :group] = dq_ref[...]
    for index in range(2):
        total = own_ref[index].astype(WIDE) + got_ref[index].astype(WIDE)
        joined_ref[:, (1 + index) * group : (2 + index) * group] = total.astype(LOW)
    if send_ref is not None:
        send_ref[...] = dot(normed_turned, joined_ref[:, half_of(1 - mine, half)]).astype(LOW)
        keep_ref[...] = dot(normed_turned, joined_ref[:, half_of(mine, half)]).astype(LOW)
    bias_ref[0:1] = column_sums(joined_ref[:, :group].astype(WIDE))
    bias_ref[1:2] = column_sums(joined_ref[:, 2 * group :].astype(WIDE))
    back = 0.0
    for index, weight_ref in enumerate(weights):
        part = joined_ref[:, index * group : (index + 1) * group]
        back = back + dot(part, weight_ref[...], 1, 1)
    return back


def first_back_kernel(
    place_ref,
    normed_ref,
    dq_ref,
    own_ref,
    got_ref,
    wq_ref,
    wk_ref,
    wv_ref,
    *rest,
):
    send_ref, keep_ref, bias_ref, part_ref, turned_ref, joined_ref = rest[-6:]

    @pl.when(pl.program_id(0) == 0)
    def _():
        turned_ref[...] = normed_ref[...].astype(WIDE).T.astype(LOW)
        part_ref[...] = jnp.zeros_like(part_ref)

    part_ref[...] += project_back(
        place_ref,
        turned_ref[...],
        dq_ref,
        own_ref,
        got_ref,
        (wq_ref, wk_ref, wv_ref),
        joined_ref,
        send_ref,
        keep_ref,
        bias_ref,
    )


def last_back_kernel(
    groups,
    place_ref,
    normed_ref,
    dq_ref,
    own_ref,
    got_ref,
    wq_ref,
    wk_ref,
    wv_ref,
    part_ref,
    embedded_ref,
    g_residual_ref,
    gain_ref,
    prior_ref,
    expression_ref,
    bias_first_ref,
    vectors_ref,
    bias_up_ref,
    *rest,
):
    send_ref, keep_ref, g_low_ref = rest[-8:-5]
    turned_ref, joined_ref, bias_ref, rows_ref, owned_ref = rest[-5:]
    rows, width = normed_ref.shape
    half = width // 2
    mine = place_ref[0]
    turned_ref[...] = normed_ref[...].astype(WIDE).T.astype(LOW)
    back = part_ref[...] + project_back(
        place_ref,
        turned_ref[...],
        dq_ref,
        own_ref,
        got_ref,
        (wq_ref, wk_ref, wv_ref),
        joined_ref,
        None,
        None,
        bias_ref,
    )
    unit, scale = normalize(embedded_ref[...])
    g_embedded = g_residual_ref[...] + norm_back(back, unit, scale, gain_ref[...][None])
    g_low_ref[...] = g_embedded.astype(LOW)
    prior = prior_ref[...].astype(WIDE).T.astype(LOW)
    count = owned_ref.shape[0]
    share = width // count
    for out_ref, side in ((send_ref, 1 - mine), (keep_ref, mine)):
        know = dot(prior, g_low_ref[:, half_of(side, half)]).astype(LOW)
        project = dot(
            turned_ref[...], joined_ref[:, half_of(side, half)]
        ).astype(LOW)
        for owner in range(count):
            entry = slice(owner * share, (owner + 1) * share)
            out_ref[owner, :share, :half] = project[entry]
            out_ref[owner, :share, half:] = know[entry]
    expression = jnp.broadcast_to(expression_ref[...], (8, rows)).T[:, :1]
    total = column_sums(g_embedded)
    hot = lax.broadcasted_iota(jnp.int32, (groups, width), 0) == place_ref[3]
    rows_ref[:groups] = jnp.where(hot, total, 0.0)
    rows_ref[groups : groups + 16] = jnp.concatenate(
        [
            column_sums(expression * g_embedded),
            column_sums(back * unit),
            column_sums(back),
            jnp.concatenate([bias_first_ref[0, 0:1], bias_first_ref[1, 0:1], bias_ref[0:1]], 1),
            jnp.concatenate([bias_first_ref[0, 1:2], bias_first_ref[1, 1:2], bias_ref[1:2]], 1),
            vectors_ref[...],
            jnp.zeros((7, width), WIDE),
        ],
        0,
    )
    owned_ref[...] = jnp.zeros_like(owned_ref)
    for owner in range(count):
        columns = slice(owner * share, (owner + 1) * share)
        for start in range(0, groups + 16, 32):
            size = min(32, groups + 16 - start)
            lanes = slice(start * 4, start * 4 + share)
            owned_ref[owner, :size, lanes] = rows_ref[start : start + size, columns]
        at, lanes = groups % 32 + 9, slice(groups // 32 * 128, groups // 32 * 128 + share)
        for part in range(4):
            first = (owner * 4 + part) * share
            owned_ref[owner, at + part : at + part + 1, lanes] = bias_up_ref[
                :, first : first + share
            ]
    low = up16(share)
    for out_ref, side in ((send_ref, 1 - mine), (keep_ref, mine)):
        rows_in = pl.ds(pl.multiple_of(side * 16, 16), 16)
        out_ref[:, low : low + 16, :half] = owned_ref[:, rows_in, :].astype(LOW)


def back_specs(rows, width, group, first):
    third = width // group
    weight = lambda part: pl.BlockSpec((width, group), lambda j, _: (0, part * third + first + j))
    both = pl.BlockSpec((2, rows, group), lambda j, _: (0, 0, j))
    return [
        whole((rows, width)),
        pl.BlockSpec((rows, group), lambda j, _: (0, j)),
        both,
        both,
        weight(0),
        weight(1),
        weight(2),
    ]


def first_back(place, normed, dq, own, got, w_qkv, group, after):
    rows, width = normed.shape
    count = dq.shape[1] // group
    half = 3 * group // 2
    tile = pl.BlockSpec((width, half), lambda j, _: (0, j))
    return pl.pallas_call(
        first_back_kernel,
        grid_spec=pltpu.PrefetchScalarGridSpec(
            num_scalar_prefetch=1,
            grid=(count,),
            in_specs=back_specs(rows, width, group, 0) + unread(after),
            out_specs=[
                tile,
                tile,
                pl.BlockSpec((None, 2, group), lambda j, _: (j, 0, 0)),
                whole((rows, width)),
            ],
            scratch_shapes=[
                pltpu.VMEM((width, rows), LOW),
                pltpu.VMEM((rows, 3 * group), LOW),
            ],
        ),
        out_shape=[
            shaped((width, count * half), LOW),
            shaped((width, count * half), LOW),
            shaped((count, 2, group), WIDE),
            shaped((rows, width), WIDE),
        ],
        compiler_params=params(),
        cost_estimate=LONG,
        name="first_back",
    )(place, normed, dq, own, got, w_qkv, w_qkv, w_qkv, *after)


def last_back(
    place,
    normed,
    dq,
    own,
    got,
    w_qkv,
    group,
    part,
    embedded,
    g_residual,
    gain,
    prior,
    expression,
    bias_first,
    vectors,
    bias_up,
    groups,
    count,
    after,
):
    rows, width = normed.shape
    half = width // 2
    first = width // group - 1
    entry = up16(width // count) + 16
    return pl.pallas_call(
        functools.partial(last_back_kernel, groups),
        grid_spec=pltpu.PrefetchScalarGridSpec(
            num_scalar_prefetch=1,
            grid=(1,),
            in_specs=back_specs(rows, width, group, first)
            + [
                whole((rows, width)),
                whole((rows, width)),
                whole((rows, width)),
                whole((width,)),
                whole((rows, width)),
                whole((1, rows)),
                whole(bias_first.shape),
                whole((4, width)),
                whole(bias_up.shape),
            ]
            + unread(after),
            out_specs=[
                whole((count, entry, width)),
                whole((count, entry, width)),
                whole((rows, width)),
            ],
            scratch_shapes=[
                pltpu.VMEM((width, rows), LOW),
                pltpu.VMEM((rows, 3 * group), LOW),
                pltpu.VMEM((2, group), WIDE),
                pltpu.VMEM((groups + 16, width), WIDE),
                pltpu.VMEM((count, 32, 384), WIDE),
            ],
        ),
        out_shape=[
            shaped((count, entry, width), LOW),
            shaped((count, entry, width), LOW),
            shaped((rows, width), LOW),
        ],
        compiler_params=params(),
        cost_estimate=LONG,
        name="last_back",
    )(
        place,
        normed,
        dq,
        own,
        got,
        w_qkv,
        w_qkv,
        w_qkv,
        part,
        embedded,
        g_residual,
        gain,
        prior,
        expression,
        bias_first,
        vectors,
        bias_up,
        *after,
    )


def gene_kernel(slots_ref, ids_ref, grad_ref, *rest):
    out_ref = rest[-1]
    slots = slots_ref[...]
    rows = grad_ref.shape[0]
    picker = jnp.where(slots == jnp.broadcast_to(ids_ref[...], (slots.shape[0], rows)), 1.0, 0.0)
    out_ref[...] = dot(picker.astype(LOW), grad_ref[...]).astype(LOW)


def gene_rows(slots, ids, grad, after):
    count = slots.shape[0]
    rows, width = grad.shape
    tile = min(count, 1152)
    return pl.pallas_call(
        gene_kernel,
        grid=(count // tile,),
        in_specs=[
            pl.BlockSpec((tile, 1), lambda j: (j, 0)),
            whole((1, rows)),
            whole((rows, width)),
        ]
        + unread(after),
        out_specs=pl.BlockSpec((tile, width), lambda j: (j, 0)),
        out_shape=shaped((count, width), LOW),
        compiler_params=params(),
        cost_estimate=LONG,
        name="gene_rows",
    )(slots, ids, grad, *after)


def swap_cores(array):
    return lax.ppermute(array, "blk", [(0, 1), (1, 0)])


def bits_apart(array, mask):
    count = lax.axis_size("dp")
    return lax.ppermute(array, "dp", [(i, i ^ mask) for i in range(count)])


def pick(array, position, index):
    return lax.dynamic_index_in_dim(array, index, position, keepdims=False)


class Share:
    QUAD = "quad"

    def __init__(self, segments, route):
        self.bits = lax.axis_size("dp").bit_length() - 1
        self.route = list(route)
        self.rows = []
        self.sources = []
        dims = tuple(range(self.bits - 1, -1, -1))
        for arrays, blocks, *rows in segments:
            first, single = len(self.rows), len(blocks) == 1
            rows = rows[0] if rows else [(0, arrays[0].shape[1])] * len(blocks)
            self.rows += [size for _, size in rows]
            parts = [
                (first + at, rows[at][0], 0 if single else block * LANES)
                for at, block in enumerate(blocks)
            ]
            columns = LANES if single else arrays[0].shape[2]
            where, height = (0, blocks[0] if single else 0), arrays[0].shape[1]
            start, size = rows[0]
            if single and size % 16 == start % size == height % size == 0:
                where, height = (start // size, where[1]), size
                parts = [(first, 0, 0)]
            for array in arrays:
                shape = (2,) * self.bits + array.shape[1:]
                self.sources.append((array.reshape(shape), dims, where, (height, columns), parts))
        self.arriving = []
        self.fixed = ()
        self.settle_places()

    def join(self, other):
        shift = len(self.rows)
        moved = lambda sources: [
            source[:4] + ([(index + shift, row, column) for index, row, column in source[4]],)
            for source in sources
        ]
        self.rows = self.rows + other.rows
        self.sources += moved(other.sources)
        self.arriving += moved(other.arriving)
        self.settle_places()
        return self

    def settle_places(self):
        self.places, place = [], 0
        for rows in self.rows:
            self.places.append(place)
            place += up16(rows)
        self.height = self.places[-1] + self.rows[-1]

    def parts(self):
        return [(index, place, 0) for index, place in enumerate(self.places)]

    def targets(self):
        step = self.route[0]
        if step == self.QUAD:
            low, high = self.bits - 2, self.bits - 1
            return [{low: way & 1, high: way >> 1} for way in (1, 2, 3)]
        return [{step: 1}]

    def left(self, target=()):
        gone = self.fixed + tuple(target)
        return [bit for bit in range(self.bits - 1, -1, -1) if bit not in gone]

    def receive(self, targets, sent):
        self.route.pop(0)
        for target, array in zip(targets, sent):
            mask = sum(flip << bit for bit, flip in target.items())
            dims = tuple(self.left(target))
            self.arriving.append(
                (bits_apart(array, mask), dims, (0, 0), array.shape[-2:], self.parts())
            )
        self.fixed += tuple(targets[0])

    def arrived(self):
        self.sources, self.arriving = self.sources + self.arriving, []


SEND, SETTLE, FINISH = range(3)


def combine(place, shares, after, mode=SEND, last=None):
    operands, specs, plan, out_specs, out_shape = [], [], [], [], []
    steps = []
    top = shares[0].bits - 1
    halves = mode == SETTLE or (
        mode == SEND and not any(top in share.fixed or top in share.targets()[0] for share in shares)
    )
    for share in shares:
        if mode != SETTLE:
            share.arrived()
        targets = share.targets() if mode == SEND else [{}]
        steps.append(targets)
        left = share.left(targets[0]) if mode != FINISH else []
        quad = len(targets) > 1
        used = []
        for array, dims, block, size, parts in share.sources:
            shape, where, picked = [], [], []
            for bit in dims:
                free = bit in left or (quad and bit in targets[0])
                stepped = halves and bit == top
                shape.append(2 if free and not stepped else None)
                where.append(bit if stepped else None if free else (bit, targets[0].get(bit, 0)))
                if quad and bit in targets[0]:
                    picked.append(bit)

            def index(step, place, where=tuple(where), block=block):
                lead = []
                for at in where:
                    if at is None:
                        lead.append(0)
                    elif at == top:
                        lead.append(step)
                    else:
                        lead.append(1 - place[4 + at[0]] if at[1] else place[4 + at[0]])
                return tuple(lead) + block

            specs.append(pl.BlockSpec(tuple(shape) + tuple(size), index))
            used.append((len(operands), parts))
            operands.append(array)
        for target in targets:
            plan.append((share.rows, share.places, used, target if quad else {}))
            if mode != FINISH:
                shape = (2,) * len(left) + (share.height, LANES)
                if halves:
                    zeros = (0,) * (len(shape) - 1)
                    out_specs.append(
                        pl.BlockSpec(
                            (None,) + shape[1:], lambda step, _, zeros=zeros: (step,) + zeros
                        )
                    )
                else:
                    out_specs.append(whole(shape))
                out_shape.append(shaped(shape, LOW if mode == SEND else WIDE))
    for shape, _ in last or []:
        out_specs.append(whole(shape))
        out_shape.append(shaped(shape, WIDE))
    count = len(operands)

    def kernel(*refs):
        place_ref, sources, outs = refs[0], refs[1 : 1 + count], refs[1 + count + len(after) :]

        def summed(item, block):
            rows, _, used, target = plan[item]
            total = None
            way = tuple(
                1 - place_ref[4 + bit] if flip else place_ref[4 + bit]
                for bit, flip in sorted(target.items(), reverse=True)
            )
            for operand, parts in used:
                for index, row, column in parts:
                    if index == block:
                        ref = sources[operand]
                        spot = (slice(row, row + rows[block]), slice(column, column + LANES))
                        lead = way + (slice(None),) * (len(ref.shape) - 2 - len(way))
                        part = ref[lead + spot].astype(WIDE)
                        total = part if total is None else total + part
            return total

        if mode == FINISH:
            for (_, pieces), out in zip(last, outs):
                for item, block, row, column in pieces:
                    value = summed(item, block)
                    out[row : row + value.shape[0], column : column + LANES] = value
            return
        for item, out in enumerate(outs):
            for block, start in enumerate(plan[item][1]):
                value = summed(item, block)
                out[..., start : start + value.shape[-2], :] = value.astype(out.dtype)

    outs = pl.pallas_call(
        kernel,
        grid_spec=pltpu.PrefetchScalarGridSpec(
            num_scalar_prefetch=1,
            grid=(2 if halves else 1,),
            in_specs=specs + unread(after),
            out_specs=out_specs,
        ),
        out_shape=out_shape,
        compiler_params=params(),
        cost_estimate=LONG,
        name="combine",
    )(place, *[pltpu.with_memory_space_constraint(x, pltpu.HBM) for x in operands], *after)
    taken = 0
    for share, targets in zip(shares, steps):
        if mode == SEND:
            share.receive(targets, outs[taken : taken + len(targets)])
        if mode == SETTLE:
            share.sources = [
                (outs[taken], tuple(share.left()), (0, 0), outs[taken].shape[-2:], share.parts())
            ]
        taken += len(targets)
    return outs


def assemble(place, own, other, shapes, pieces, small_row=None):
    def kernel(place_ref, own_ref, other_ref, *outs):
        first = place_ref[0] == 0

        def of_core(core, rows, columns):
            return jnp.where(first == (core == 0), own_ref[rows, columns], other_ref[rows, columns])

        for core, row, rows, column, columns, target, out_column in pieces:
            value = of_core(core, slice(row, row + rows), slice(column, column + columns))
            outs[target][:, out_column : out_column + columns] = value
        if small_row is None:
            outs[-1][...] = jnp.zeros_like(outs[-1])
            return
        group_ref, vector_refs, long_ref = outs[2], outs[3:-1], outs[-1]
        share, groups = group_ref.shape
        rows = slice(small_row, small_row + 16)
        for start in range(0, groups, 16):
            lanes = slice(start // 32 * 128, start // 32 * 128 + share)
            group_ref[:, start : start + 16] = of_core(start // 16 % 2, rows, lanes).T
        rest = of_core(0, rows, slice(groups // 32 * 128, groups // 32 * 128 + 128))
        for index, ref in enumerate(vector_refs):
            ref[...] = rest[index, :share]
        long_ref[...] = jnp.concatenate(
            [rest[9 + part : 10 + part, :share] for part in range(4)], 1
        )[0]

    return pl.pallas_call(
        kernel,
        grid_spec=pltpu.PrefetchScalarGridSpec(
            num_scalar_prefetch=1,
            grid=(1,),
            in_specs=[whole(own.shape), whole(own.shape)],
            out_specs=[whole(shape) for shape in shapes],
        ),
        out_shape=[shaped(shape, WIDE) for shape in shapes],
        compiler_params=params(),
        cost_estimate=LONG,
        name="assemble",
    )(place, own, other)


def body(
    gene_ids,
    values,
    knowledge,
    lengths,
    groups,
    gene_table,
    group_table,
    w_know,
    w_value,
    norm1_gain,
    norm1_bias,
    w_qkv,
    bias_q,
    bias_v,
    w_out,
    bias_out,
    norm2_gain,
    norm2_bias,
    w_up,
    bias_up,
    w_down,
    bias_down,
    cotangent,
):
    width = w_out.shape[0]
    units = w_up.shape[1]
    rows = gene_ids.shape[1]
    count = lax.axis_size("dp")
    mine = lax.axis_index("blk")
    length, group = lengths[0], groups[0]
    prior = knowledge[0]
    row = lambda vector: vector.reshape(1, -1)
    me = lax.axis_index("dp")
    bits = count.bit_length() - 1
    place = jnp.stack(
        [mine, length - mine * rows, length - (1 - mine) * rows, group]
        + [(me >> bit) & 1 for bit in range(bits)]
    ).astype(jnp.int32)
    if gene_table.shape[0] > 8 * rows:
        table = gene_table[gene_ids[0]]
    else:
        table = gene_table
    embedded, normed, kv_own = embed(
        place,
        gene_ids,
        values,
        prior,
        table,
        group_table,
        w_know,
        w_value,
        norm1_gain,
        norm1_bias,
        w_qkv,
        bias_v,
    )
    kv_other = swap_cores(kv_own)
    queries = project_queries(normed, w_qkv, bias_q)
    attended, probs, inverse = attend(place, queries, kv_own, kv_other)
    (
        block_output,
        residual,
        g_normed_two,
        up_send,
        up_keep,
        down_send,
        down_keep,
        bias_up_grad,
    ) = feed_forward(
        place,
        attended,
        embedded,
        cotangent[0],
        w_out,
        bias_out,
        norm2_gain,
        norm2_bias,
        w_up,
        row(bias_up),
        w_down,
        bias_down,
    )
    g_residual, g_attended, out_send, out_keep, vectors = branch_back(
        place,
        residual,
        g_normed_two,
        cotangent[0],
        attended,
        w_out,
        norm2_gain,
        [up_send, down_send],
    )

    owners = lambda array: array.reshape(count, -1, array.shape[-1])
    low_bits = list(range(bits - 2))
    turned = low_bits[1::-1] + low_bits[2:]
    quad, high_bits = [Share.QUAD], [bits - 2, bits - 1]
    up_terms = [owners(up_keep), owners(swap_cores(up_send))]
    blocks = units // 2 // LANES
    out_terms = [owners(out_keep), owners(swap_cores(out_send))]
    down_terms = [owners(down_keep), owners(swap_cores(down_send))]
    high, share = units // count, width // count
    out_cut = min(share, up16(2 * share // 3))
    out_rest = [(out_terms, [0], [(out_cut, share - out_cut)])] if out_cut < share else []
    early = [
        Share([(down_terms, [0]), (out_terms, [0], [(0, out_cut)])], low_bits + quad),
        Share([(up_terms, list(range(blocks)))] + out_rest, turned + quad),
    ]
    token = combine(place, early, [])
    dq1, own1, other1 = attend_back(
        queries, kv_own, kv_other, attended, g_attended, probs, inverse, 0, 4, token
    )
    got1 = swap_cores(other1)
    dq2, own2, other2 = attend_back(
        queries, kv_own, kv_other, attended, g_attended, probs, inverse, 4, 2, [dq1]
    )
    got2 = swap_cores(other2)
    qkv_send, qkv_keep, bias_first, part = first_back(
        place, normed, dq1, own1, got1, w_qkv, 256, [dq2]
    )
    qkv = [owners(qkv_keep), owners(swap_cores(qkv_send))]
    project = Share([(qkv, [0, 1])], high_bits + low_bits)
    token = [part, qkv_send]
    for bit in low_bits[1:]:
        token = combine(place, early + [project] * (bit == low_bits[-1]), token)
    early = [early[0].join(early[1])]
    tail_send, tail_keep, g_low = last_back(
        place,
        normed,
        dq2,
        own2,
        got2,
        w_qkv,
        256,
        part,
        embedded,
        g_residual,
        norm1_gain,
        prior,
        values,
        bias_first,
        vectors,
        bias_up_grad,
        group_table.shape[0],
        count,
        token,
    )
    slot = jnp.arange(count * VOC_DEV, dtype=jnp.int32)[:, None]
    slot = slot + slot // VOC_DEV * VOC_DEV
    gene_send = gene_rows(slot + (1 - mine) * VOC_DEV, gene_ids, g_low, [tail_send])
    gene_got = swap_cores(gene_send)
    gene_keep = gene_rows(slot + mine * VOC_DEV, gene_ids, g_low, [gene_send])
    tail = [tail_keep, swap_cores(tail_send)]
    gene = [owners(gene_keep), owners(gene_got)]
    small_at = up16(share)
    late = [
        Share([(tail, [0], [(0, share)]), (gene, [0])], low_bits + quad),
        Share(
            [(tail, [1], [(0, share)]), (tail, [0], [(small_at, 16)]), (gene, [1])], turned + quad
        ),
    ]
    token = combine(place, [project], [gene_keep])
    token = combine(place, late, token)
    token = combine(place, early, token)
    for _ in low_bits[1:]:
        token = combine(place, late + [project], token)
    token = combine(place, late, token, SETTLE)
    late = [late[0].join(late[1]), project]
    step = up16(share)
    layout = [(0, 0, 0, 0), (0, 1, high + blocks * step, 0)]
    if out_rest:
        layout.append((0, 2 + blocks, high + blocks * step + out_cut, 0))
    layout += [(0, 2 + block, high + block * step, 0) for block in range(blocks)]
    (own,) = combine(place, early, token, FINISH, [((high + (blocks + 1) * step, LANES), layout)])
    other = swap_cores(own)
    combine(place, late, [own])
    pieces = []
    for core in range(2):
        pieces.append((core, 0, high, 0, LANES, 0, core * LANES))
        for block in range(blocks):
            place_in = (core * blocks + block) * LANES
            pieces.append((core, high + block * step, share, 0, LANES, 1, place_in))
        pieces.append((core, high + blocks * step, share, 0, LANES, 2, core * LANES))
    w_down_share, w_up_share, w_out_share, done = assemble(
        place, own, other, [(high, width), (share, units), (share, width), (8, 128)], pieces
    )
    layout = [(1, 0, 0, 0), (1, 1, step, 0), (0, 0, 2 * step, 0), (0, 2, 3 * step, 0)]
    layout += [(0, 3, 4 * step, 0)]
    own, gene_grad = combine(
        place,
        late,
        [done],
        FINISH,
        [
            ((4 * step + 16, LANES), layout),
            ((VOC_DEV, width), [(0, 1, 0, 0), (0, 4, 0, LANES)]),
        ],
    )
    other = swap_cores(own)
    pieces = []
    for block in range(3):
        at = block * step
        pieces.append((0, at, share, 0, 256, 0, block * 256))
        pieces.append((0, at, share, 256, 128, 0, width + block * 256))
        pieces.append((1, at, share, 0, 128, 0, width + block * 256 + 128))
        pieces.append((1, at, share, 128, 256, 0, 2 * width + block * 256))
    for core in range(2):
        pieces.append((core, 3 * step, share, 0, LANES, 1, core * LANES))
    w_qkv_share, w_know_share, group_share, *extra, bias_up_share = assemble(
        place,
        own,
        other,
        [(share, 3 * width), (share, width), (share, group_table.shape[0])]
        + [(share,)] * 9
        + [(units // count,)],
        pieces,
        4 * step,
    )
    return (
        block_output[None],
        gene_grad,
        group_share.T,
        w_know_share,
        extra[0],
        extra[1],
        extra[2],
        w_qkv_share,
        extra[3],
        extra[4],
        w_out_share,
        extra[5],
        extra[6],
        extra[7],
        w_up_share,
        bias_up_share,
        w_down_share,
        extra[8],
    )


def solution(mesh):
    in_specs = (
        P("dp", "blk"),
        P("dp", "blk"),
        P("dp", "blk", None),
        P("dp"),
        P("dp"),
        P(),
        P(),
        P(),
        P(),
        P(),
        P(),
        P(),
        P(),
        P(),
        P(),
        P(),
        P(),
        P(),
        P(),
        P(),
        P(),
        P(),
        P("dp", "blk", None),
    )
    out_specs = (
        P("dp", "blk", None),
        P(("dp", "blk"), None),
        P(None, "dp"),
        P("dp", None),
        P("dp"),
        P("dp"),
        P("dp"),
        P("dp", None),
        P("dp"),
        P("dp"),
        P("dp", None),
        P("dp"),
        P("dp"),
        P("dp"),
        P("dp", None),
        P("dp"),
        P("dp", None),
        P("dp"),
    )
    return jax.shard_map(body, mesh=mesh, in_specs=in_specs, out_specs=out_specs, check_vma=False)
```
